128 devices in a mesh: grp: 4 (over y), dom: 32 (over x, z, core).
Axes of the slice: x: 4, y: 4, z: 4, core: 2. Of those that a mesh axis runs over, the one named last changes fastest.
Arguments:
- velocity: float32 [3, 64, 1024, 256], P(None, 'grp', 'dom'), may hold values from -6 to 6
- damping: float32 [64, 1024, 256], P('grp', 'dom'), may hold values from 0.02 to 0.5
- displacement: float32 [3, 524288], P(None, ('grp', 'dom')), may hold values from -6 to 6
- stiffness: float32 [12, 12, 524288], P(None, None, ('grp', 'dom'))
- connectivity: int32 [4, 524288], P(None, ('grp', 'dom')), may hold values from 0 to 4159, as said below
- inv_mass: float32 [524288], P(('grp', 'dom')), may hold values from 0.05 to 0.3
- iface_cell: int32 [16384], P(('grp', 'dom')), may hold values from 0 to 131071
- iface_owner: int32 [16384, 1], P(('grp', 'dom')), may hold values from 0 to 127; in each aligned block of 128 rows (0 to 127, 128 to 255, ...) at most 2 rows name the same one
- iface_node: int32 [16384], P(('grp', 'dom')), may hold values from 0 to 4092
- rbf_weight: float32 [4, 16384], P(None, ('grp', 'dom')), may hold values from 0.1 to 1
- normals: float32 [3, 16384], P(None, ('grp', 'dom')), may hold values from -6 to 6
Outputs:
- new_velocity: float32 [3, 64, 1024, 256], P(None, 'grp', 'dom')
- pressure: float32 [64, 1024, 256], P('grp', 'dom')
- new_displacement: float32 [3, 524288], P(None, ('grp', 'dom'))
- iface_velocity: float32 [3, 16384], P(None, ('grp', 'dom'))
The draws below stay inside these ranges and needn't reach their ends.
Inputs may be any that keep to these rules, and one draw needn't show every extreme that they name: `connectivity`: the four corners of element e (e its local number on the device) are four different local nodes from e to e + 64, in no fixed order; numbers from 4096 on name the first 64 nodes of the next device along grp+dom. `iface_owner`: among the 128 points of one device, at most 2 have the same owner.
All inputs are finite; a program needn't handle non-finite values.
Results may differ from the reference program's by a relative error of at most 0.0001.
Values sent between devices are 32-bit elements; how exact they have to be, the bound alone decides.
A program may use at most 192 MiB of HBM per device.

```python
import math
import jax
import jax.numpy as jnp
import numpy as np
from jax import lax

CX = 16
CY = 32
CZ = 256
ITERS = 4
S_DEV = 4096
RIM = 64
RBFW = 4
IF_DEV = 128
NX = 64
NY = 1024
NZ = 256
NODES = 524288
ELEMS = 524288
IFACE = 16384
CAP = 2
N_DOM = 32
DEVICES = 128


def draw_stiffness(key, part):
    key = jax.random.fold_in(key, 11)
    raw_values = jax.random.normal(key, (12, 12, ELEMS), jnp.float32) * 0.5
    symmetric = 0.5 * (raw_values + jnp.swapaxes(raw_values, 0, 1))
    identity = jnp.eye(12, dtype=jnp.float32)[:, :, None]
    return symmetric + 3.0 * identity


def draw_connectivity(key, part):
    key = jax.random.fold_in(key, 23)
    score_key = jax.random.fold_in(key, 1)
    rotate_key = jax.random.fold_in(key, 2)
    local_index = lax.iota(jnp.int32, ELEMS) % S_DEV
    column = lax.iota(jnp.int32, RIM + 1)
    raw_scores = jax.random.randint(score_key, (ELEMS, RIM + 1), 0, 1 << 20, dtype=jnp.int32)
    scores = raw_scores * (RIM + 1) + column[None, :]
    first_elem = (local_index == 0)[:, None] & (column == 0)[None, :]
    last_elem = (local_index == S_DEV - 1)[:, None] & (column == RIM)[None, :]
    scores = scores + jnp.where(first_elem | last_elem, 1 << 28, 0).astype(jnp.int32)
    top_values, chosen = lax.top_k(scores, 4)
    rotation = jax.random.randint(rotate_key, (ELEMS, 1), 0, 4, dtype=jnp.int32)
    corner_slot = (lax.iota(jnp.int32, 4)[None, :] + rotation) % 4
    rotated = jnp.take_along_axis(chosen.astype(jnp.int32), corner_slot, axis=1)
    return jnp.transpose(local_index[:, None] + rotated).astype(jnp.int32)


def touch_ends(array, rng, least, top_value):
    spot = [jax.random.randint(jax.random.fold_in(rng, axis), (), 0, length) for axis, length in enumerate(array.shape)]
    main_axis = array.shape.index(max(array.shape))
    beside = spot[:main_axis] + [(spot[main_axis] + 1) % array.shape[main_axis]] + spot[main_axis + 1:]
    return array.at[tuple(spot)].set(least).at[tuple(beside)].set(top_value)


def levels(rng, dims, cuts, low, largest):
    gain, own = 1.0, jax.random.fold_in(rng, 6)
    for axis_at, parts in cuts:
        heights = jnp.exp(jax.random.uniform(jax.random.fold_in(own, axis_at), (parts,), jnp.float32, low / len(cuts), largest / len(cuts)))
        gain = gain * jnp.repeat(heights, dims[axis_at] // parts).reshape([-1 if axis == axis_at else 1 for axis in range(len(dims))])
    return gain


def routed_block(stream_key, own, number, rows, count, top, reach, slope):
    order = jax.random.permutation(stream_key, count)
    packed, common = shares(count, rows * top, reach, slope, True), shares(count, rows * top, reach, slope, False)
    places = jnp.arange(count)

    def named(tallies, offset_by):
        used = int((tallies > 0).sum())
        fixed = max(1, used // 4)
        moved = fixed + (places - fixed + offset_by * (used - fixed)) % max(1, count - fixed)
        return jnp.zeros((count,), jnp.int32).at[order[jnp.where(places < fixed, places, moved)]].set(jnp.asarray(tallies, jnp.int32))

    tallies = jnp.where(number % 4 == 0, named(packed, number // 4), named(common, number - number // 4 - 1))
    mixed = jax.random.permutation(jax.random.fold_in(own, 3), count)
    source_of, taker = mixed[0:count // 2 * 2:2], mixed[1:count // 2 * 2:2]
    margin = jnp.minimum(tallies[source_of] - 1, reach - tallies[taker]) // 2
    margin = jnp.where((source_of == order[0]) | (taker == order[0]) | (tallies[taker] == 0), 0, jnp.maximum(margin, 0))
    moved = jax.random.randint(jax.random.fold_in(own, 4), (count // 2,), 0, 1 << 20) % (margin + 1)
    tallies = tallies.at[source_of].add(-moved).at[taker].add(moved)
    labels = jnp.searchsorted(jnp.cumsum(tallies), jnp.arange(rows * top), side="right").astype(jnp.int32)
    listing = labels.reshape(top, rows).T
    listing = listing[jax.random.permutation(jax.random.fold_in(own, 1), rows)]
    offset_by = jax.random.randint(jax.random.fold_in(own, 2), (rows, 1), 0, top)
    return jnp.take_along_axis(listing, (jnp.arange(top)[None, :] + offset_by) % top, axis=1)


def shares(amount, total, bound, slope, full):
    portions = [(1 << 20) // math.isqrt(rank ** slope) + 1 for rank in range(1, amount + 1)]
    largest = bound if full else min(bound, max(-(-total // amount), total * portions[0] // sum(portions)))
    least = 1 if total - largest >= amount - 1 else 0
    counts, surplus = [largest] + [least] * (amount - 1), total - largest - least * (amount - 1)
    while surplus > 0:
        candidates = [i for i in range(1, amount) if counts[i] < largest] or [i for i in range(1, amount) if counts[i] < bound]
        pool, remaining = sum([portions[i] for i in candidates]), surplus
        for i in candidates:
            extra = min(bound - counts[i], max(1, remaining * portions[i] // pool), surplus)
            counts[i] = counts[i] + extra
            surplus = surplus - extra
    return np.array(counts)


def normal_values(own_key, dims, deviation, limit, cuts=(), kind=jnp.bfloat16):
    drawn = jax.random.normal(own_key, dims, jnp.float32) * deviation
    if len(cuts) > 0:
        drawn = levels(own_key, dims, cuts, -0.22, 0.18) * drawn
    return jnp.clip(drawn, min=-limit, max=limit).astype(kind)


def setup_inputs(seed: int = 0) -> dict:
    splits = jax.random.split(jax.random.key(seed), 12)
    velocity = normal_values(splits[0], (3, NX, NY, NZ), 1.0, 6.0, ((1, 4), (2, 32)), jnp.float32)
    damping = jnp.clip(jnp.exp(math.log(0.5) - 3.218876 * jax.random.uniform(splits[1], (NX, NY, NZ), jnp.float32) ** levels(splits[1], (NX, NY, NZ), ((0, 4), (1, 32)), -0.2, 0.2)), 0.02, 0.5)
    displacement = normal_values(splits[2], (3, NODES), 1.0, 6.0, ((1, 128),), jnp.float32)
    stiffness = draw_stiffness(jax.random.fold_in(splits[11], 71), 0)
    connectivity = draw_connectivity(jax.random.fold_in(splits[11], 71), 0)
    inv_mass = jnp.clip(jnp.exp(math.log(0.3) - 1.7917595 * jax.random.uniform(splits[5], (NODES,), jnp.float32) ** levels(splits[5], (NODES,), ((0, 128),), -0.2, 0.2)), 0.05, 0.3)
    iface_cell = touch_ends(jax.random.randint(splits[6], (IFACE,), 0, CX * CY * CZ), jax.random.fold_in(splits[6], 1), 0, (CX * CY * CZ) - 1).astype(jnp.int32)
    iface_owner_keys = jax.random.split(jax.random.fold_in(splits[7], 1), IFACE // IF_DEV)
    iface_owner_turns = jax.random.permutation(jax.random.fold_in(splits[7], 3), IFACE // IF_DEV)
    iface_owner = jax.vmap(lambda own, number: routed_block(jax.random.fold_in(splits[7], 2), own, number, IF_DEV, DEVICES, 1, CAP, 2))(iface_owner_keys, iface_owner_turns).reshape((IFACE, 1))
    iface_node = touch_ends(jax.random.randint(splits[8], (IFACE,), 0, S_DEV - RBFW + 1), jax.random.fold_in(splits[8], 1), 0, S_DEV - RBFW).astype(jnp.int32)
    rbf_weight = jnp.clip(jnp.exp(math.log(1.0) - 2.3025851 * jax.random.uniform(splits[9], (RBFW, IFACE), jnp.float32) ** levels(splits[9], (RBFW, IFACE), ((1, 128),), -0.2, 0.2)), 0.1, 1.0)
    normals = normal_values(splits[10], (3, IFACE), 1.0, 6.0, ((1, 128),), jnp.float32)
    return {"velocity": velocity, "damping": damping, "displacement": displacement, "stiffness": stiffness, "connectivity": connectivity, "inv_mass": inv_mass, "iface_cell": iface_cell, "iface_owner": iface_owner, "iface_node": iface_node, "rbf_weight": rbf_weight, "normals": normals}


TIME_STEP = 0.1
VISCOSITY = 1.0
WALL_FRICTION = 0.5
SHELL_STEP = 0.5
UNIT_STEPS = ((1, 0, 0), (0, 1, 0), (0, 0, 1))


def window_at(padded, offsets):
    size_x = padded.shape[-3] - 2
    size_y = padded.shape[-2] - 2
    size_z = padded.shape[-1] - 2
    return padded[..., 1 + offsets[0]:1 + offsets[0] + size_x, 1 + offsets[1]:1 + offsets[1] + size_y, 1 + offsets[2]:1 + offsets[2] + size_z]


def backward(unit_step):
    return tuple(-value for value in unit_step)


def pad_cells(source):
    spec = [(0, 0)] * (source.ndim - 3) + [(1, 1)] * 3
    return jnp.pad(source, spec)


def predictor(padded):
    centre = window_at(padded, (0, 0, 0))
    laplace = -6.0 * centre
    advect = jnp.zeros_like(centre)
    for axis_num, unit_step in enumerate(UNIT_STEPS):
        forward = window_at(padded, unit_step)
        behind_cells = window_at(padded, backward(unit_step))
        laplace = laplace + forward + behind_cells
        advect = advect + centre[axis_num:axis_num + 1] * (0.5 * (forward - behind_cells))
    return centre + TIME_STEP * (VISCOSITY * laplace - advect)


def divergence(padded):
    summed = jnp.zeros(window_at(padded[0], (0, 0, 0)).shape, jnp.float32)
    for axis_num, unit_step in enumerate(UNIT_STEPS):
        component = padded[axis_num]
        summed = summed + 0.5 * (window_at(component, unit_step) - window_at(component, backward(unit_step)))
    return -summed


def apply_padded(padded, damping):
    centre = window_at(padded, (0, 0, 0))
    beside = jnp.zeros_like(centre)
    for unit_step in UNIT_STEPS:
        beside = beside + window_at(padded, unit_step) + window_at(padded, backward(unit_step))
    return (6.0 + damping) * centre - beside


def gradient(padded):
    return jnp.stack([0.5 * (window_at(padded, unit_step) - window_at(padded, backward(unit_step))) for unit_step in UNIT_STEPS])


def reference(velocity, damping, displacement, stiffness, connectivity, inv_mass, iface_cell, iface_owner, iface_node, rbf_weight, normals):
    predicted = predictor(pad_cells(velocity))
    right_side = divergence(pad_cells(predicted))
    pressure = jnp.zeros_like(right_side)
    residual = right_side
    direction = right_side
    norm_now = jnp.sum(residual * residual)
    for sweep in range(ITERS):
        mapped = apply_padded(pad_cells(direction), damping)
        step_size = norm_now / jnp.sum(direction * mapped)
        pressure = pressure + step_size * direction
        residual = residual - step_size * mapped
        norm_next = jnp.sum(residual * residual)
        direction = residual + (norm_next / norm_now) * direction
        norm_now = norm_next
    new_velocity = predicted - gradient(pad_cells(pressure))

    point_count = iface_cell.shape[0]
    source_dev = jnp.arange(point_count, dtype=jnp.int32) // IF_DEV
    grp_index = source_dev // N_DOM
    dom_index = source_dev % N_DOM
    local_x = iface_cell // (CY * CZ)
    local_y = (iface_cell // CZ) % CY
    local_z = iface_cell % CZ
    global_x = grp_index * CX + local_x
    global_y = dom_index * CY + local_y
    pressure_at = pressure[global_x, global_y, local_z]
    velocity_at = new_velocity[:, global_x, global_y, local_z]
    traction = -pressure_at[None] * normals + WALL_FRICTION * velocity_at

    node_count = displacement.shape[1]
    element_count = connectivity.shape[1]
    element_dev = jnp.arange(element_count, dtype=jnp.int32) // S_DEV
    global_nodes = connectivity + element_dev[None] * S_DEV
    extended = jnp.pad(displacement, ((0, 0), (0, RIM)))
    corner_values = extended[:, global_nodes]
    element_dofs = jnp.transpose(corner_values, (1, 0, 2)).reshape(12, element_count)
    element_force = jnp.sum(stiffness * element_dofs[None], axis=1).reshape(4, 3, element_count)
    stiff_force = jnp.zeros((3, node_count + RIM), jnp.float32)
    for corner in range(4):
        stiff_force = stiff_force.at[:, global_nodes[corner]].add(element_force[corner])
    stiff_force = stiff_force[:, :node_count]

    owner_dev = iface_owner[:, 0]
    base_node = owner_dev * S_DEV + iface_node
    applied = jnp.zeros((3, node_count), jnp.float32)
    for offset in range(RBFW):
        applied = applied.at[:, base_node + offset].add(rbf_weight[offset][None] * traction)
    node_velocity = inv_mass[None] * (applied - stiff_force)
    new_displacement = displacement + SHELL_STEP * node_velocity
    iface_velocity = jnp.zeros((3, point_count), jnp.float32)
    for offset in range(RBFW):
        iface_velocity = iface_velocity + rbf_weight[offset][None] * node_velocity[:, base_node + offset]
    return new_velocity, pressure, new_displacement, iface_velocity
```

```python
import functools

import jax
import jax.numpy as jnp
from jax import lax
from jax.experimental import pallas as pl
from jax.experimental.pallas import tpu as pltpu
from jax.sharding import PartitionSpec as P

MESH = pl.DeviceIdType.MESH
NGRP, NDOM = 4, 32
NDEV = NGRP * NDOM
CX, CY, HZ = 16, 32, 128
PX, PY, OX, OY = CX + 4, CY + 16, 2, 8
SLOT = {0: 0, 2: 1, 1: 2}
SHIFT, HALF = 6.26, 6.24
DELAY = 0.1
PAIRS = [(i, j) for i in range(4) for j in range(i, 5)]


def rows_of(ref):
    return ref.reshape(PX * 2 * PY, HZ)


class Plane:
    def __init__(self, x, y, n):
        self.x, self.y, self.n = x, y, n

    def get(self, f, dx=0, dy=0):
        return [f[self.x + dx, h, self.y + dy:self.y + dy + self.n, :] for h in (0, 1)]

    def put(self, f, halves):
        for h in (0, 1):
            f[self.x, h, self.y:self.y + self.n, :] = halves[h]


class Strip:
    def __init__(self, y):
        self.y = y

    def at(self, dx, dy, h):
        return pl.ds(((OX + dx) * 2 + h) * PY + self.y + dy, CX, stride=2 * PY)

    def get(self, f, dx=0, dy=0):
        flat = rows_of(f)
        return [flat[self.at(dx, dy, h), :] for h in (0, 1)]

    def put(self, f, halves):
        flat = rows_of(f)
        for h in (0, 1):
            flat[self.at(0, 0, h), :] = halves[h]


def lanes(a):
    return lax.broadcasted_iota(jnp.int32, a.shape, 1)


def up(a):
    r0, r1 = (pltpu.roll(v, HZ - 1, 1) for v in a)
    edge = lanes(a[0]) == HZ - 1
    return [jnp.where(edge, r1, r0), jnp.where(edge, 0.0, r1)]


def down(a):
    r0, r1 = (pltpu.roll(v, 1, 1) for v in a)
    edge = lanes(a[0]) == 0
    return [jnp.where(edge, 0.0, r0), jnp.where(edge, r0, r1)]


def each(fn, *lists):
    return [fn(*vals) for vals in zip(*lists)]


def pairs_of(region, f):
    centre = region.get(f)
    return centre, (
        (region.get(f, 1, 0), region.get(f, -1, 0)),
        (region.get(f, 0, 1), region.get(f, 0, -1)),
        (up(centre), down(centre)),
    )


def predict(region, vel, c, out):
    others = [region.get(vel.at[SLOT[d]]) for d in range(3)]
    centre, sides = pairs_of(region, vel.at[SLOT[c]])
    res = []
    for h in (0, 1):
        lap = -6.0 * centre[h]
        adv = None
        for d in range(3):
            a, b = sides[d][0][h], sides[d][1][h]
            lap = lap + a + b
            term = others[d][h] * (0.5 * (a - b))
            adv = term if adv is None else adv + term
        res.append(centre[h] + DELAY * (lap - adv))
    region.put(out.at[SLOT[c]], res)


def apply(region, damp, f):
    centre, sides = pairs_of(region, f)
    dv = region.get(damp)
    res = []
    for h in (0, 1):
        s = None
        for a, b in sides:
            s = a[h] + b[h] if s is None else s + a[h] + b[h]
        res.append(((dv[h] + (6.0 - SHIFT)) * centre[h] - s) * (1.0 / HALF))
    return res


def cheb(region, damp, f, before, out):
    res = apply(region, damp, f)
    if before is not None:
        res = each(lambda a, b: 2.0 * a - b, res, region.get(before))
    if out is not None:
        region.put(out, res)
    return res


def all_planes(fn, lo=OX, hi=OX + CX, parts=2):
    def body(x, carry):
        for k in range(parts):
            fn(Plane(x, OY + k * (CY // parts), CY // parts))
        return carry

    lax.fori_loop(lo, hi, body, 0)


def position():
    return lax.axis_index("grp"), lax.axis_index("dom")


def clear_outside(f):
    g, d = position()

    @pl.when(g == 0)
    def _():
        f[0:OX] = jnp.zeros((OX, 2, PY, HZ), jnp.float32)

    @pl.when(g == NGRP - 1)
    def _():
        f[OX + CX:PX] = jnp.zeros((PX - OX - CX, 2, PY, HZ), jnp.float32)

    @pl.when(d == 0)
    def _():
        f[:, :, 0:OY, :] = jnp.zeros((PX, 2, OY, HZ), jnp.float32)

    @pl.when(d == NDOM - 1)
    def _():
        f[:, :, OY + CY:PY, :] = jnp.zeros((PX, 2, PY - OY - CY, HZ), jnp.float32)


def neighbour(dg, dd):
    g, d = position()
    return lax.rem(g + dg + NGRP, NGRP), lax.rem(d + dd + NDOM, NDOM)


def sides_of(ref, lead, width):
    lo, hi = OX, OX + CX
    a, b = OY, OY + CY
    ys = slice(a, b)
    xs = slice(lo, hi)
    w = width
    return [
        ((1, 0), lead + (slice(hi - w, hi), slice(None), ys), lead + (slice(lo - w, lo), slice(None), ys)),
        ((-1, 0), lead + (slice(lo, lo + w), slice(None), ys), lead + (slice(hi, hi + w), slice(None), ys)),
        ((0, 1), lead + (xs, slice(None), slice(b - w, b)), lead + (xs, slice(None), slice(a - w, a))),
        ((0, -1), lead + (xs, slice(None), slice(a, a + w)), lead + (xs, slice(None), slice(b, b + w))),
    ]


def corners_of(ref, lead):
    out = []
    for dg in (1, -1):
        for dd in (1, -1):
            sx = OX + CX - 1 if dg == 1 else OX
            tx = OX - 1 if dg == 1 else OX + CX
            sy = OY + CY - 1 if dd == 1 else OY
            ty = OY - 1 if dd == 1 else OY + CY
            out.append((
                (dg, dd),
                lead + (slice(sx, sx + 1), slice(None), slice(sy, sy + 1)),
                lead + (slice(tx, tx + 1), slice(None), slice(ty, ty + 1)),
            ))
    return out


def start_all(ref, items, send, recv, base):
    copies = []
    for k, (way, src, dst) in enumerate(items):
        cp = pltpu.make_async_remote_copy(
            src_ref=ref.at[src], dst_ref=ref.at[dst],
            send_sem=send.at[base + k], recv_sem=recv.at[base + k],
            device_id=neighbour(*way), device_id_type=MESH,
        )
        cp.start()
        copies.append(cp)
    return copies


def greet_all():
    g, d = position()
    me = g * NDOM + d
    barrier = pltpu.get_barrier_semaphore()

    def body(i, carry):
        t = lax.rem(me + i, NDEV)
        pl.semaphore_signal(barrier, inc=1, device_id=(t // NDOM, lax.rem(t, NDOM)), device_id_type=MESH)
        return carry

    lax.fori_loop(1, NDEV, body, 0, unroll=8)
    return barrier


def exchange_start(out_ref, in_ref, own, send, recv):
    g, d = position()
    me = g * NDOM + d
    mine = pltpu.make_async_copy(out_ref.at[pl.ds(me, 1)], in_ref.at[pl.ds(me, 1)], own)
    mine.start()

    def body(i, carry):
        t = lax.rem(me + i, NDEV)
        pltpu.make_async_remote_copy(
            src_ref=out_ref.at[pl.ds(t, 1)], dst_ref=in_ref.at[pl.ds(me, 1)],
            send_sem=send, recv_sem=recv,
            device_id=(t // NDOM, lax.rem(t, NDOM)), device_id_type=MESH,
        ).start()
        return carry

    lax.fori_loop(1, NDEV, body, 0, unroll=8)
    return mine


def exchange_wait(mine, out_ref, in_ref, send, recv):
    rest = pl.ds(0, NDEV - 1)
    mine.wait()
    pltpu.make_async_copy(out_ref.at[rest], in_ref.at[rest], recv).wait()
    pltpu.make_async_copy(out_ref.at[rest], in_ref.at[rest], send).wait()


def iterate(gram):
    def times(v):
        out = [None] * 5

        def put(i, val):
            out[i] = val if out[i] is None else out[i] + val

        for j, val in enumerate(v):
            if val is None:
                continue
            put(j, SHIFT * val)
            if j == 0:
                put(1, HALF * val)
            else:
                put(j + 1, (0.5 * HALF) * val)
                put(j - 1, (0.5 * HALF) * val)
        return out

    worst = None

    def form(a, b):
        nonlocal worst
        total = size = None
        for i in range(5):
            for j in range(5):
                if a[i] is None or b[j] is None:
                    continue
                term = a[i] * b[j] * gram(min(i, j), max(i, j))
                total = term if total is None else total + term
                mag = jnp.abs(term)
                size = mag if size is None else size + mag
        ratio = total / size
        worst = ratio if worst is None else jnp.minimum(worst, ratio)
        return total

    def axpy(a, s, b):
        return [x if y is None else (s * y if x is None else x + s * y) for x, y in zip(a, b)]

    one = jnp.ones_like(gram(0, 0))
    r = [one, None, None, None, None]
    d = list(r)
    p = [None] * 5
    rr = gram(0, 0)
    for k in range(4):
        m = times(d)
        step = rr / form(d, m)
        p = axpy(p, step, d)
        if k == 3:
            break
        r = axpy(r, -step, m)
        new = form(r, r)
        d = axpy(r, new / rr, d)
        rr = new
    return p[:4], worst


def fluid_kernel(vel_hbm, damp_hbm, nv_hbm, p_hbm, flag_ref, vel, damp, pred, basis, press, nvel,
                 rows_out, rows_in, lsem, ssem, rsem, asem):
    barrier = greet_all()
    loads = []
    for h in (0, 1):
        z = slice(h * HZ, (h + 1) * HZ)
        for c in range(3):
            loads.append(pltpu.make_async_copy(
                vel_hbm.at[c, :, :, z], vel.at[SLOT[c], OX:OX + CX, h, OY:OY + CY, :], lsem.at[len(loads)]))
        loads.append(pltpu.make_async_copy(
            damp_hbm.at[:, :, z], damp.at[OX:OX + CX, h, OY:OY + CY, :], lsem.at[len(loads)]))
    for cp in loads:
        cp.start()
    for cp in loads:
        cp.wait()
    pl.semaphore_wait(barrier, NDEV - 1)

    one = slice(None)
    f_x, f_y, f_z = SLOT[0], SLOT[1], SLOT[2]
    faces = corners_of(vel, (one,))
    wide_x, wide_y = sides_of(vel, (f_x,), 2)[:2], sides_of(vel, (f_y,), 2)[2:]
    thin_x, thin_y = sides_of(vel, (slice(1, 3),), 1)[:2], sides_of(vel, (slice(0, 2),), 1)[2:]
    copies = start_all(vel, faces + wide_x + wide_y + thin_x + thin_y, ssem, rsem, 0)
    copies += start_all(damp, sides_of(damp, (), 1), ssem, rsem, 12)
    for cp in copies:
        cp.wait()
    for c in range(3):
        clear_outside(vel.at[c])

    def pred_main(region):
        for c in range(3):
            predict(region, vel, c, pred)

    all_planes(pred_main)
    for x in (OX - 1, OX + CX):
        for k in range(2):
            predict(Plane(x, OY + 16 * k, 16), vel, 0, pred)
    for y in (OY - 1, OY + CY):
        predict(Strip(y), vel, 1, pred)
    clear_outside(pred.at[f_x])
    clear_outside(pred.at[f_y])

    t0, t1, t2, t3 = (basis.at[j] for j in range(4))

    def diverge(region):
        fx, fy, fz = pred.at[f_x], pred.at[f_y], region.get(pred.at[f_z])
        s = each(lambda a, b: 0.5 * (a - b), region.get(fx, 1, 0), region.get(fx, -1, 0))
        s = each(lambda s, a, b: s + 0.5 * (a - b), s, region.get(fy, 0, 1), region.get(fy, 0, -1))
        s = each(lambda s, a, b: -(s + 0.5 * (a - b)), s, up(fz), down(fz))
        region.put(t0, s)

    all_planes(diverge)

    def swap(f, base):
        cps = start_all(f, corners_of(f, ()) + sides_of(f, (), 2), ssem, rsem, base)
        for cp in cps:
            cp.wait()
        clear_outside(f)

    def grow(f, before, out):
        all_planes(lambda region: cheb(region, damp, f, before, out), OX - 1, OX + CX + 1)
        for y in (OY - 1, OY + CY):
            cheb(Strip(y), damp, f, before, out)
        clear_outside(out)

    swap(t0, 16)
    grow(t0, None, t1)
    all_planes(lambda region: cheb(region, damp, t1, t0, t2))
    swap(t2, 24)
    grow(t2, t1, t3)

    def dots(x, acc):
        acc = list(acc)
        for k in range(2):
            region = Plane(x, OY + 16 * k, 16)
            ts = [region.get(t) for t in (t0, t1, t2, t3)]
            ts.append(cheb(region, damp, t3, t2, None))
            for n, (i, j) in enumerate(PAIRS):
                for h in (0, 1):
                    prod = ts[i][h] * ts[j][h]
                    acc[n] = acc[n] + (prod[0:8] + prod[8:16])
        return tuple(acc)

    acc = lax.fori_loop(OX, OX + CX, dots, tuple(jnp.zeros((8, HZ), jnp.float32) for _ in PAIRS))
    lane = lax.broadcasted_iota(jnp.int32, (1, HZ), 1)
    row = jnp.zeros((1, HZ), jnp.float32)
    for n in range(len(PAIRS)):
        row = row + jnp.where(lane == n, jnp.sum(jnp.sum(acc[n], axis=0, keepdims=True), axis=1, keepdims=True), 0.0)
    rows_out[...] = jnp.broadcast_to(row, (NDEV, HZ))
    mine = exchange_start(rows_out, rows_in, lsem.at[8], asem.at[0], asem.at[1])
    exchange_wait(mine, rows_out, rows_in, asem.at[0], asem.at[1])
    total = jnp.sum(rows_in[...], axis=0, keepdims=True)
    gram = {}
    for n, key in enumerate(PAIRS):
        gram[key] = jnp.broadcast_to(jnp.sum(jnp.where(lane == n, total, 0.0), axis=1, keepdims=True), (1, HZ))
    coef, worst = iterate(lambda i, j: gram[(i, j)])
    flag_ref[...] = jnp.broadcast_to(worst, (8, HZ))

    def combine(region):
        res = None
        for c, t in zip(coef, (t0, t1, t2, t3)):
            vals = [c * v for v in region.get(t)]
            res = vals if res is None else each(lambda a, b: a + b, res, vals)
        region.put(press, res)

    all_planes(combine, OX - 1, OX + CX + 1)
    for y in (OY - 1, OY + CY):
        combine(Strip(y))

    def correct(region):
        _, sides = pairs_of(region, press)
        for c in range(3):
            own = region.get(pred.at[SLOT[c]])
            new = each(lambda v, a, b: v - 0.5 * (a - b), own, sides[c][0], sides[c][1])
            for h in (0, 1):
                nvel[c, region.x - OX, h, region.y - OY:region.y - OY + region.n, :] = new[h]

    all_planes(correct)
    stores = []
    for h in (0, 1):
        z = slice(h * HZ, (h + 1) * HZ)
        stores.append(pltpu.make_async_copy(nvel.at[:, :, h], nv_hbm.at[:, :, :, z], lsem.at[2 * h]))
        stores.append(pltpu.make_async_copy(
            press.at[OX:OX + CX, h, OY:OY + CY, :], p_hbm.at[:, :, z], lsem.at[2 * h + 1]))
    for cp in stores:
        cp.start()
    for cp in stores:
        cp.wait()


def fluid(velocity, damping):
    field = (PX, 2, PY, HZ)
    f32 = jnp.float32
    anywhere = pl.BlockSpec(memory_space=pl.ANY)
    return pl.pallas_call(
        fluid_kernel,
        out_shape=(
            jax.ShapeDtypeStruct(velocity.shape, f32),
            jax.ShapeDtypeStruct(damping.shape, f32),
            jax.ShapeDtypeStruct((8, HZ), f32),
        ),
        in_specs=[anywhere] * 2,
        out_specs=(anywhere, anywhere, pl.BlockSpec(memory_space=pltpu.VMEM)),
        scratch_shapes=[
            pltpu.VMEM((3,) + field, f32),
            pltpu.VMEM(field, f32),
            pltpu.VMEM((3,) + field, f32),
            pltpu.VMEM((4,) + field, f32),
            pltpu.VMEM(field, f32),
            pltpu.VMEM((3, CX, 2, CY, HZ), f32),
            pltpu.VMEM((NDEV, HZ), f32),
            pltpu.VMEM((NDEV, HZ), f32),
            pltpu.SemaphoreType.DMA((9,)),
            pltpu.SemaphoreType.DMA((32,)),
            pltpu.SemaphoreType.DMA((32,)),
            pltpu.SemaphoreType.DMA((2,)),
        ],
        compiler_params=pltpu.CompilerParams(
            collective_id=0, has_side_effects=True, vmem_limit_bytes=48 << 20),
        name="fluid",
    )(velocity, damping)


RIM = 64
RBFW = 4
WALL_FRICTION = 0.5
SHELL_STEP = 0.5


def from_behind(value, axis, steps):
    count = lax.axis_size(axis)
    leading, last = (max(0, -steps), min(count, count - steps))
    return lax.ppermute(value, axis, [(source, source + steps) for source in range(leading, last)])


def local(
    velocity,
    damping,
    displacement,
    stiffness,
    connectivity,
    inv_mass,
    iface_cell,
    iface_owner,
    iface_node,
    rbf_weight,
    normals,
):
    shell_nodes = displacement.shape[1]
    rim_values = from_behind(displacement[:, :RIM], ("grp", "dom"), -1)
    extended_disp = jnp.concatenate([displacement, rim_values], axis=1)
    element_count = connectivity.shape[1]
    corner_values = extended_disp[:, connectivity]
    element_dofs = jnp.transpose(corner_values, (1, 0, 2)).reshape(12, element_count)
    element_force = jnp.sum(stiffness * element_dofs[None], axis=1).reshape(4, 3, element_count)
    node_force = jnp.zeros((3, shell_nodes + RIM), jnp.float32)
    for corner in range(4):
        node_force = node_force.at[:, connectivity[corner]].add(element_force[corner])
    rim_force = from_behind(node_force[:, shell_nodes:], ("grp", "dom"), 1)
    stiff_force = node_force[:, :shell_nodes] + jnp.pad(rim_force, ((0, 0), (0, shell_nodes - RIM)))
    new_velocity, pressure, _ = fluid(velocity, damping)
    pressure_at = pressure.reshape(-1)[iface_cell]
    velocity_at = new_velocity.reshape(3, -1)[:, iface_cell]
    traction = -pressure_at[None] * normals + WALL_FRICTION * velocity_at
    owner_dev = iface_owner[:, 0]
    point_count = owner_dev.shape[0]
    devices = lax.axis_size("grp") * lax.axis_size("dom")
    owner_cap = max(2, 2 * point_count // devices)
    order_index = lax.iota(jnp.int32, point_count)
    earlier = (owner_dev[None, :] == owner_dev[:, None]) & (
        order_index[None, :] < order_index[:, None]
    )
    slot_rank = jnp.sum(earlier.astype(jnp.int32), axis=1)
    slot_index = owner_dev * owner_cap + slot_rank
    slot_count = devices * owner_cap
    payload = jnp.concatenate([traction, rbf_weight, iface_node.astype(jnp.float32)[None]], axis=0)
    outgoing = jnp.zeros((payload.shape[0], slot_count), jnp.float32).at[:, slot_index].set(payload)
    received = lax.all_to_all(outgoing, ("grp", "dom"), split_axis=1, concat_axis=1, tiled=True)
    slot_traction = received[:3]
    slot_weight = received[3 : 3 + RBFW]
    slot_node = received[3 + RBFW].astype(jnp.int32)
    applied = jnp.zeros((3, shell_nodes), jnp.float32)
    for offset in range(RBFW):
        applied = applied.at[:, slot_node + offset].add(slot_weight[offset][None] * slot_traction)
    node_velocity = inv_mass[None] * (applied - stiff_force)
    new_displacement = displacement + SHELL_STEP * node_velocity
    slot_velocity = jnp.zeros((3, slot_count), jnp.float32)
    for offset in range(RBFW):
        slot_velocity = (
            slot_velocity + slot_weight[offset][None] * node_velocity[:, slot_node + offset]
        )
    returned_vals = lax.all_to_all(
        slot_velocity, ("grp", "dom"), split_axis=1, concat_axis=1, tiled=True
    )
    iface_velocity = returned_vals[:, slot_index]
    return (new_velocity, pressure, new_displacement, iface_velocity)


def solution(mesh):
    return jax.shard_map(
        local,
        mesh=mesh,
        in_specs=(
            P(None, "grp", "dom", None),
            P("grp", "dom", None),
            P(None, ("grp", "dom")),
            P(None, None, ("grp", "dom")),
            P(None, ("grp", "dom")),
            P(("grp", "dom")),
            P(("grp", "dom")),
            P(("grp", "dom"), None),
            P(("grp", "dom")),
            P(None, ("grp", "dom")),
            P(None, ("grp", "dom")),
        ),
        out_specs=(
            P(None, "grp", "dom", None),
            P("grp", "dom", None),
            P(None, ("grp", "dom")),
            P(None, ("grp", "dom")),
        ),
        check_vma=False,
    )
```

```python
import jax
import jax.numpy as jnp
from jax import lax
from jax.experimental import pallas as pl
from jax.experimental.pallas import tpu as pltpu
from jax.sharding import PartitionSpec as P

MESH = pl.DeviceIdType.MESH
NGRP, NDOM = 4, 32
NDEV = NGRP * NDOM
CX, CY, HZ = 16, 32, 128
PX, PY, OX, OY = CX + 4, CY + 16, 2, 8
SLOT = {0: 0, 2: 1, 1: 2}
SHIFT, HALF = 6.26, 6.24
TIME_STEP = 0.1
WALL_FRICTION = 0.5
SHELL_STEP = 0.5
RIM, RBFW, NBLK, NPTS = 64, 4, 32, 128
W_BASIS, W_WEIGHT, W_NODE, W_NEXT = 32, 47, 51, 32
PAIRS = [(i, j) for i in range(4) for j in range(i, 5)]


def rows_of(ref):
    return ref.reshape(PX * 2 * PY, HZ)


class Plane:
    def __init__(self, x, y, n):
        self.x, self.y, self.n = x, y, n

    def get(self, f, dx=0, dy=0):
        return [f[self.x + dx, h, self.y + dy:self.y + dy + self.n, :] for h in (0, 1)]

    def put(self, f, halves):
        for h in (0, 1):
            f[self.x, h, self.y:self.y + self.n, :] = halves[h]


class Strip:
    def __init__(self, y):
        self.y = y

    def at(self, dx, dy, h):
        return pl.ds(((OX + dx) * 2 + h) * PY + self.y + dy, CX, stride=2 * PY)

    def get(self, f, dx=0, dy=0):
        flat = rows_of(f)
        return [flat[self.at(dx, dy, h), :] for h in (0, 1)]

    def put(self, f, halves):
        flat = rows_of(f)
        for h in (0, 1):
            flat[self.at(0, 0, h), :] = halves[h]


def lanes(a):
    return lax.broadcasted_iota(jnp.int32, a.shape, 1)


def up(a):
    r0, r1 = (pltpu.roll(v, HZ - 1, 1) for v in a)
    edge = lanes(a[0]) == HZ - 1
    return [jnp.where(edge, r1, r0), jnp.where(edge, 0.0, r1)]


def down(a):
    r0, r1 = (pltpu.roll(v, 1, 1) for v in a)
    edge = lanes(a[0]) == 0
    return [jnp.where(edge, 0.0, r0), jnp.where(edge, r0, r1)]


def each(fn, *lists):
    return [fn(*vals) for vals in zip(*lists)]


def pairs_of(region, f):
    centre = region.get(f)
    return centre, (
        (region.get(f, 1, 0), region.get(f, -1, 0)),
        (region.get(f, 0, 1), region.get(f, 0, -1)),
        (up(centre), down(centre)),
    )


def predict(region, vel, c, out):
    others = [region.get(vel.at[SLOT[d]]) for d in range(3)]
    centre, sides = pairs_of(region, vel.at[SLOT[c]])
    res = []
    for h in (0, 1):
        lap = -6.0 * centre[h]
        adv = None
        for d in range(3):
            a, b = sides[d][0][h], sides[d][1][h]
            lap = lap + a + b
            term = others[d][h] * (0.5 * (a - b))
            adv = term if adv is None else adv + term
        res.append(centre[h] + TIME_STEP * (lap - adv))
    region.put(out.at[SLOT[c]], res)


def apply(region, damp, f):
    centre, sides = pairs_of(region, f)
    dv = region.get(damp)
    res = []
    for h in (0, 1):
        s = None
        for a, b in sides:
            s = a[h] + b[h] if s is None else s + a[h] + b[h]
        res.append(((dv[h] + (6.0 - SHIFT)) * centre[h] - s) * (1.0 / HALF))
    return res


def cheb(region, damp, f, before, out):
    res = apply(region, damp, f)
    if before is not None:
        res = each(lambda a, b: 2.0 * a - b, res, region.get(before))
    if out is not None:
        region.put(out, res)
    return res


def all_planes(fn, lo=OX, hi=OX + CX, parts=2):
    def body(x, carry):
        for k in range(parts):
            fn(Plane(x, OY + k * (CY // parts), CY // parts))
        return carry

    lax.fori_loop(lo, hi, body, 0)


def position():
    return lax.axis_index("grp"), lax.axis_index("dom")


def clear_outside(f):
    g, d = position()

    @pl.when(g == 0)
    def _():
        f[0:OX] = jnp.zeros((OX, 2, PY, HZ), jnp.float32)

    @pl.when(g == NGRP - 1)
    def _():
        f[OX + CX:PX] = jnp.zeros((PX - OX - CX, 2, PY, HZ), jnp.float32)

    @pl.when(d == 0)
    def _():
        f[:, :, 0:OY, :] = jnp.zeros((PX, 2, OY, HZ), jnp.float32)

    @pl.when(d == NDOM - 1)
    def _():
        f[:, :, OY + CY:PY, :] = jnp.zeros((PX, 2, PY - OY - CY, HZ), jnp.float32)


def neighbour(dg, dd):
    g, d = position()
    return lax.rem(g + dg + NGRP, NGRP), lax.rem(d + dd + NDOM, NDOM)


def sides_of(ref, lead, width):
    lo, hi = OX, OX + CX
    a, b = OY, OY + CY
    ys = slice(a, b)
    xs = slice(lo, hi)
    w = width
    return [
        ((1, 0), lead + (slice(hi - w, hi), slice(None), ys), lead + (slice(lo - w, lo), slice(None), ys)),
        ((-1, 0), lead + (slice(lo, lo + w), slice(None), ys), lead + (slice(hi, hi + w), slice(None), ys)),
        ((0, 1), lead + (xs, slice(None), slice(b - w, b)), lead + (xs, slice(None), slice(a - w, a))),
        ((0, -1), lead + (xs, slice(None), slice(a, a + w)), lead + (xs, slice(None), slice(b, b + w))),
    ]


def corners_of(ref, lead):
    out = []
    for dg in (1, -1):
        for dd in (1, -1):
            sx = OX + CX - 1 if dg == 1 else OX
            tx = OX - 1 if dg == 1 else OX + CX
            sy = OY + CY - 1 if dd == 1 else OY
            ty = OY - 1 if dd == 1 else OY + CY
            out.append((
                (dg, dd),
                lead + (slice(sx, sx + 1), slice(None), slice(sy, sy + 1)),
                lead + (slice(tx, tx + 1), slice(None), slice(ty, ty + 1)),
            ))
    return out


def start_all(ref, items, send, recv, base):
    copies = []
    for k, (way, src, dst) in enumerate(items):
        cp = pltpu.make_async_remote_copy(
            src_ref=ref.at[src], dst_ref=ref.at[dst],
            send_sem=send.at[base + k], recv_sem=recv.at[base + k],
            device_id=neighbour(*way), device_id_type=MESH,
        )
        cp.start()
        copies.append(cp)
    return copies


def greet_all():
    g, d = position()
    me = g * NDOM + d
    barrier = pltpu.get_barrier_semaphore()

    def body(i, carry):
        t = lax.rem(me + i, NDEV)
        pl.semaphore_signal(barrier, inc=1, device_id=(t // NDOM, lax.rem(t, NDOM)), device_id_type=MESH)
        return carry

    lax.fori_loop(1, NDEV, body, 0, unroll=8)
    return barrier


def exchange_start(out_ref, in_ref, own, send, recv):
    g, d = position()
    me = g * NDOM + d
    mine = pltpu.make_async_copy(out_ref.at[pl.ds(me, 1)], in_ref.at[pl.ds(me, 1)], own)
    mine.start()

    def body(i, carry):
        t = lax.rem(me + i, NDEV)
        pltpu.make_async_remote_copy(
            src_ref=out_ref.at[pl.ds(t, 1)], dst_ref=in_ref.at[pl.ds(me, 1)],
            send_sem=send, recv_sem=recv,
            device_id=(t // NDOM, lax.rem(t, NDOM)), device_id_type=MESH,
        ).start()
        return carry

    lax.fori_loop(1, NDEV, body, 0, unroll=8)
    return mine


def exchange_wait(mine, out_ref, in_ref, send, recv):
    rest = pl.ds(0, NDEV - 1)
    mine.wait()
    pltpu.make_async_copy(out_ref.at[rest], in_ref.at[rest], recv).wait()
    pltpu.make_async_copy(out_ref.at[rest], in_ref.at[rest], send).wait()


def iterate(gram):
    def times(v):
        out = [None] * 5

        def put(i, val):
            out[i] = val if out[i] is None else out[i] + val

        for j, val in enumerate(v):
            if val is None:
                continue
            put(j, SHIFT * val)
            if j == 0:
                put(1, HALF * val)
            else:
                put(j + 1, (0.5 * HALF) * val)
                put(j - 1, (0.5 * HALF) * val)
        return out

    worst = None

    def form(a, b):
        nonlocal worst
        total = size = None
        for i in range(5):
            for j in range(5):
                if a[i] is None or b[j] is None:
                    continue
                term = a[i] * b[j] * gram(min(i, j), max(i, j))
                total = term if total is None else total + term
                mag = jnp.abs(term)
                size = mag if size is None else size + mag
        ratio = total / size
        worst = ratio if worst is None else jnp.minimum(worst, ratio)
        return total

    def axpy(a, s, b):
        return [x if y is None else (s * y if x is None else x + s * y) for x, y in zip(a, b)]

    one = jnp.ones_like(gram(0, 0))
    r = [one, None, None, None, None]
    d = list(r)
    p = [None] * 5
    rr = gram(0, 0)
    for k in range(4):
        m = times(d)
        step = rr / form(d, m)
        p = axpy(p, step, d)
        if k == 3:
            break
        r = axpy(r, -step, m)
        new = form(r, r)
        d = axpy(r, new / rr, d)
        rr = new
    return p[:4], worst


def lane_of(shape):
    return lax.broadcasted_iota(jnp.int32, shape, 1)


def row_of(shape):
    return lax.broadcasted_iota(jnp.int32, shape, 0)


def thirds(x):
    a = x.astype(jnp.bfloat16)
    rest = x - a.astype(jnp.float32)
    b = rest.astype(jnp.bfloat16)
    return a, b, (rest - b.astype(jnp.float32)).astype(jnp.bfloat16)


def pick(onehot, x):
    width = x.shape[1]
    wide = jnp.concatenate(thirds(x), axis=1)
    out = jnp.dot(onehot, wide, preferred_element_type=jnp.float32)
    return out[:, :width] + out[:, width:2 * width] + out[:, 2 * width:]


def spread(src, dst, count, stride):
    for b in range(NBLK):
        dst[pl.ds(b, count, stride=stride), :] = src[:, b * HZ:(b + 1) * HZ]


def shell_gather(q, disp, conn, dofs):
    sub = row_of((8, HZ))
    for a in range(4):
        rel = conn[a, 8 * q:8 * q + 8, :] - HZ * (8 * q + sub)
        near = rel < HZ
        low = jnp.where(near, rel, rel - HZ)
        for c in range(3):
            here = jnp.take_along_axis(disp[c, 8 * q:8 * q + 8, :], low, axis=1, mode="promise_in_bounds")
            there = jnp.take_along_axis(disp[c, 8 * q + 1:8 * q + 9, :], low, axis=1, mode="promise_in_bounds")
            dofs[pl.ds(8 * q * 16 + 3 * a + c, 8, stride=16), :] = jnp.where(near, here, there)


def shell_product(q, stiff, dofs, force):
    sub = row_of((8, HZ))

    def body(i, carry):
        parts = []
        for b in range(8 * q, 8 * q + 8):
            z = slice(b * HZ, (b + 1) * HZ)
            top = stiff[i, 0:8, z] * dofs[b * 16:b * 16 + 8, :]
            low = stiff[i, 8:12, z] * dofs[b * 16 + 8:b * 16 + 12, :]
            parts.append(top + jnp.concatenate([low, jnp.zeros((4, HZ), jnp.float32)], axis=0))
        first = sub < 4
        parts = [
            jnp.where(first, parts[k], parts[k + 4]) + pltpu.roll(jnp.where(first, parts[k + 4], parts[k]), 4, 0)
            for k in range(4)
        ]
        for bit in (2, 1):
            keep = (sub & bit) == 0
            parts = [
                jnp.where(keep, parts[k] + pltpu.roll(parts[k], 8 - bit, 0),
                          parts[k + bit] + pltpu.roll(parts[k + bit], bit, 0))
                for k in range(bit)
            ]
        force[i, 8 * q:8 * q + 8, :] = parts[0]
        return carry

    lax.fori_loop(0, 12, body, 0)


def shell_scatter(q, conn, force, own, over):
    lane = lane_of((8, HZ))
    element = HZ * (8 * q + row_of((8, HZ))) + lane
    rel = [conn[a, 8 * q:8 * q + 8, :] - element for a in range(4)]
    vals = [[force[3 * a + c, 8 * q:8 * q + 8, :] for c in range(3)] for a in range(4)]

    def body(d, acc):
        hit = [r == d for r in rel]
        inside = lane >= d
        out = []
        for c in range(3):
            s = jnp.zeros((8, HZ), jnp.float32)
            for a in range(4):
                s = jnp.where(hit[a], vals[a][c], s)
            s = pltpu.roll(s, d, 1)
            out.append(acc[2 * c] + jnp.where(inside, s, 0.0))
            out.append(acc[2 * c + 1] + jnp.where(inside, 0.0, s))
        return tuple(out)

    acc = lax.fori_loop(0, RIM + 1, body, tuple(jnp.zeros((8, HZ), jnp.float32) for _ in range(6)), unroll=5)
    for c in range(3):
        own[c, 8 * q:8 * q + 8, :] = acc[2 * c]
        over[c, 8 * q + 1:8 * q + 9, :] = acc[2 * c + 1]


def sample(cells, f, mid0, mid1, dx, dy):
    def body(i, carry):
        for u in range(4):
            k = i * 4 + u
            cell = cells[k]
            x = lax.div(cell, CY * 2 * HZ) + OX
            y = lax.rem(lax.div(cell, 2 * HZ), CY) + OY
            h = lax.rem(lax.div(cell, HZ), 2)
            at = pl.ds(k, 1)
            mid0[at, :] = f[x, 0, pl.ds(y, 1), :]
            mid1[at, :] = f[x, 1, pl.ds(y, 1), :]
            dx[at, :] = f[x + 1, h, pl.ds(y, 1), :] - f[x - 1, h, pl.ds(y, 1), :]
            dy[at, :] = f[x, h, pl.ds(y + 1, 1), :] - f[x, h, pl.ds(y - 1, 1), :]
        return carry

    lax.fori_loop(0, NPTS // 4, body, 0)


def sample_centre(cells, fields, outs):
    def body(i, carry):
        for u in range(4):
            k = i * 4 + u
            cell = cells[k]
            x = lax.div(cell, CY * 2 * HZ) + OX
            y = lax.rem(lax.div(cell, 2 * HZ), CY) + OY
            h = lax.rem(lax.div(cell, HZ), 2)
            for f, o in zip(fields, outs):
                o[pl.ds(k, 1), :] = f[x, h, pl.ds(y, 1), :]
        return carry

    lax.fori_loop(0, NPTS // 4, body, 0)


def column(row):
    return jnp.transpose(jnp.broadcast_to(row, (HZ, HZ)))


def total_of(x):
    return jnp.sum(x, axis=1, keepdims=True)


def step_kernel(vel_hbm, damp_hbm, stiff_hbm, disp_in, conn_in, mass, cells, cell_row, owner, node, weight, normal,
                nv_hbm, p_hbm, disp_out, iface_out, flag_ref,
                vel, damp, pred, t0, t1, t2, t3, press, nvel, stiff,
                disp, conn, dofs, force, own, over, mid0, mid1, dx, dy, words, table, nodal,
                rows_out, rows_in, back_out, back_in, lsem, ksem, ssem, rsem, asem):
    barrier = greet_all()
    g, d = position()
    me = g * NDOM + d
    loads = []
    for h in (0, 1):
        z = slice(h * HZ, (h + 1) * HZ)
        for c in range(3):
            loads.append(pltpu.make_async_copy(
                vel_hbm.at[c, :, :, z], vel.at[SLOT[c], OX:OX + CX, h, OY:OY + CY, :], lsem.at[len(loads)]))
        loads.append(pltpu.make_async_copy(
            damp_hbm.at[:, :, z], damp.at[OX:OX + CX, h, OY:OY + CY, :], lsem.at[len(loads)]))
    for q in range(4):
        z = slice(q * 8 * HZ, (q + 1) * 8 * HZ)
        loads.append(pltpu.make_async_copy(stiff_hbm.at[:, :, z], stiff.at[:, :, z], ksem.at[q]))
    for cp in loads:
        cp.start()
    blocks = loads[8:]

    spread(disp_in, disp.reshape(3 * 40, HZ), 3, 40)
    spread(conn_in, conn.reshape(4 * NBLK, HZ), 4, NBLK)
    for q in range(3):
        shell_gather(q, disp, conn, dofs)
        blocks[q].wait()
        shell_product(q, stiff, dofs, force)

    square = (HZ, HZ)
    owns = owner[...] == row_of(square)
    first = jnp.min(jnp.where(owns, lane_of(square), HZ), axis=1, keepdims=True)
    for s in (0, 1):
        table[:, s * HZ:(s + 1) * HZ] = jnp.where(
            owns & ((lane_of(square) == first) == (s == 0)), 1.0, 0.0).astype(jnp.bfloat16)
    words[...] = jnp.zeros(square, jnp.float32)
    words[W_WEIGHT:W_WEIGHT + 4, :] = weight[...]
    words[W_NODE:W_NODE + 1, :] = node[...].astype(jnp.float32)
    words[...] = jnp.transpose(words[...])

    for cp in loads[:8]:
        cp.wait()
    pl.semaphore_wait(barrier, NDEV - 1)

    one = slice(None)
    f_x, f_y, f_z = SLOT[0], SLOT[1], SLOT[2]
    faces = corners_of(vel, (one,))
    wide_x, wide_y = sides_of(vel, (f_x,), 2)[:2], sides_of(vel, (f_y,), 2)[2:]
    thin_x, thin_y = sides_of(vel, (slice(1, 3),), 1)[:2], sides_of(vel, (slice(0, 2),), 1)[2:]
    copies = start_all(vel, faces + wide_x + wide_y + thin_x + thin_y, ssem, rsem, 0)
    copies += start_all(damp, sides_of(damp, (), 1), ssem, rsem, 12)
    before, after = lax.rem(me + NDEV - 1, NDEV), lax.rem(me + 1, NDEV)
    rim = pltpu.make_async_remote_copy(
        src_ref=disp.at[:, 0:1, :], dst_ref=disp.at[:, NBLK:NBLK + 1, :], send_sem=ssem.at[32], recv_sem=rsem.at[32],
        device_id=(lax.div(before, NDOM), lax.rem(before, NDOM)), device_id_type=MESH)
    rim.start()
    for q in range(3):
        shell_scatter(q, conn, force, own, over)
    for cp in copies:
        cp.wait()
    for c in range(3):
        clear_outside(vel.at[c])

    def pred_main(region):
        for c in range(3):
            predict(region, vel, c, pred)

    all_planes(pred_main)
    for x in (OX - 1, OX + CX):
        for k in range(2):
            predict(Plane(x, OY + 16 * k, 16), vel, 0, pred)
    for y in (OY - 1, OY + CY):
        predict(Strip(y), vel, 1, pred)
    clear_outside(pred.at[f_x])
    clear_outside(pred.at[f_y])

    def diverge(region):
        fx, fy, fz = pred.at[f_x], pred.at[f_y], region.get(pred.at[f_z])
        s = each(lambda a, b: 0.5 * (a - b), region.get(fx, 1, 0), region.get(fx, -1, 0))
        s = each(lambda s, a, b: s + 0.5 * (a - b), s, region.get(fy, 0, 1), region.get(fy, 0, -1))
        s = each(lambda s, a, b: -(s + 0.5 * (a - b)), s, up(fz), down(fz))
        region.put(t0, s)

    all_planes(diverge)

    def swap(f, base):
        return start_all(f, corners_of(f, ()) + sides_of(f, (), 2), ssem, rsem, base)

    def grow(f, before, out):
        all_planes(lambda region: cheb(region, damp, f, before, out), OX - 1, OX + CX + 1)
        for y in (OY - 1, OY + CY):
            cheb(Strip(y), damp, f, before, out)
        clear_outside(out)

    moving = swap(t0, 16)
    rim.wait()

    @pl.when(me == NDEV - 1)
    def _():
        disp[:, NBLK:NBLK + 1, :] = jnp.zeros((3, 1, HZ), jnp.float32)

    shell_gather(3, disp, conn, dofs)
    blocks[3].wait()
    shell_product(3, stiff, dofs, force)
    shell_scatter(3, conn, force, own, over)
    edge = pltpu.make_async_remote_copy(
        src_ref=over.at[:, NBLK:NBLK + 1, :], dst_ref=over.at[:, 0:1, :], send_sem=ssem.at[33], recv_sem=rsem.at[33],
        device_id=(lax.div(after, NDOM), lax.rem(after, NDOM)), device_id_type=MESH)
    edge.start()
    for cp in moving:
        cp.wait()
    clear_outside(t0)
    grow(t0, None, t1)
    all_planes(lambda region: cheb(region, damp, t1, t0, t2))

    moving = swap(t2, 24)
    z_all = column(cell_row[...]) & (2 * HZ - 1)
    lane = lane_of(square)
    hit0, hit1 = lane == z_all, lane + HZ == z_all
    hit = hit0 | hit1
    normals = [column(normal[c:c + 1, :]) for c in range(3)]

    def place(word, values):
        words[...] += jnp.where(lane == word, total_of(values), 0.0)

    def basis_words(j, f):
        sample(cells, f, mid0, mid1, dx, dy)
        a, b = mid0[...], mid1[...]
        value = jnp.where(hit0, a, 0.0) + jnp.where(hit1, b, 0.0)
        slope = (jnp.where(lane == z_all + 1, a, 0.0) + jnp.where(lane + HZ == z_all + 1, b, 0.0)
                 - jnp.where(lane == z_all - 1, a, 0.0) - jnp.where(lane + HZ == z_all - 1, b, 0.0))
        slopes = (jnp.where(hit, dx[...], 0.0), jnp.where(hit, dy[...], 0.0), slope)
        for c in range(3):
            place(W_BASIS + 3 * (j + 1) + c, -value * normals[c] - (0.5 * WALL_FRICTION) * slopes[c])

    sample_centre(cells, [pred.at[SLOT[c]] for c in range(3)], [mid0, mid1, dx])
    for c, ref in enumerate((mid0, mid1, dx)):
        place(W_BASIS + c, jnp.where(hit, WALL_FRICTION * ref[...], 0.0))
    basis_words(0, t0)
    basis_words(1, t1)
    for cp in moving:
        cp.wait()
    clear_outside(t2)
    basis_words(2, t2)
    grow(t2, t1, t3)

    def dots(x, acc):
        acc = list(acc)
        for k in range(2):
            region = Plane(x, OY + 16 * k, 16)
            ts = [region.get(t) for t in (t0, t1, t2, t3)]
            ts.append(cheb(region, damp, t3, t2, None))
            for n, (i, j) in enumerate(PAIRS):
                for h in (0, 1):
                    prod = ts[i][h] * ts[j][h]
                    acc[n] = acc[n] + (prod[0:8] + prod[8:16])
        return tuple(acc)

    acc = lax.fori_loop(OX, OX + CX, dots, tuple(jnp.zeros((8, HZ), jnp.float32) for _ in PAIRS))
    basis_words(3, t3)
    lane1 = lane_of((1, HZ))
    row = jnp.zeros((1, HZ), jnp.float32)
    for n in range(len(PAIRS)):
        row = row + jnp.where(lane1 == n, total_of(jnp.sum(acc[n], axis=0, keepdims=True)), 0.0)
    payload = words[...]
    both = jnp.concatenate([payload, pltpu.roll(payload, W_NEXT, 1)], axis=0)
    rows_out[...] = pick(table[...], both) + row
    mine = exchange_start(rows_out, rows_in, lsem.at[8], asem.at[0], asem.at[1])
    edge.wait()

    @pl.when(me == 0)
    def _():
        over[:, 0:1, :] = jnp.zeros((3, 1, HZ), jnp.float32)

    exchange_wait(mine, rows_out, rows_in, asem.at[0], asem.at[1])
    got = rows_in[...]
    total = jnp.sum(got, axis=0, keepdims=True)
    gram = {}
    for n, key in enumerate(PAIRS):
        gram[key] = jnp.broadcast_to(total_of(jnp.where(lane1 == n, total, 0.0)), (1, HZ))
    coef, worst = iterate(lambda i, j: gram[(i, j)])
    flag_ref[...] = jnp.broadcast_to(worst, (8, HZ))

    words[...] = jnp.transpose(got)
    lefts, lefts2, rights, rights2 = [], [], [], []
    for s in (0, 1):
        at = W_BASIS + s * W_NEXT
        traction = words[at:at + 3, :]
        for j in range(4):
            traction = traction + coef[j] * words[at + 3 * (j + 1):at + 3 * (j + 1) + 3, :]
        where = words[W_NODE + s * W_NEXT:W_NODE + s * W_NEXT + 1, :].astype(jnp.int32)
        high, low = where // HZ, where % HZ
        block = row_of((NBLK, HZ))
        lefts.append(jnp.concatenate([jnp.where(block == high, traction[c:c + 1], 0.0) for c in range(3)], axis=0))
        lefts2.append(jnp.concatenate([jnp.where(block == high + 1, traction[c:c + 1], 0.0) for c in range(3)], axis=0))
        right = right2 = jnp.zeros(square, jnp.float32)
        for j in range(RBFW):
            w = words[W_WEIGHT + s * W_NEXT + j:W_WEIGHT + s * W_NEXT + j + 1, :]
            right = jnp.where(row_of(square) == low + j, w, right)
            right2 = jnp.where(row_of(square) + HZ == low + j, w, right2)
        rights.append(right)
        rights2.append(right2)
    applied = lax.dot_general(
        jnp.concatenate(lefts + lefts2, axis=1), jnp.concatenate(rights + rights2, axis=1),
        (((1,), (1,)), ((), ())), precision=lax.Precision.HIGHEST, preferred_element_type=jnp.float32)
    for c in range(3):
        net = own[c] + over[c, 0:NBLK, :]
        moved = mass[...] * (applied[c * NBLK:(c + 1) * NBLK] - net)
        nodal[c, 0:NBLK, :] = moved
        nodal[c, NBLK:NBLK + 8, :] = jnp.zeros((8, HZ), jnp.float32)
        force[c] = disp[c, 0:NBLK, :] + SHELL_STEP * moved
    near = jnp.concatenate([nodal[c, 0:NBLK, :] for c in range(3)] + [nodal[c, 1:NBLK + 1, :] for c in range(3)], axis=1)
    stack = jnp.concatenate(thirds(near), axis=0)
    result = jnp.zeros(square, jnp.float32)
    for s in (0, 1):
        where = got[:, W_NODE + s * W_NEXT:W_NODE + s * W_NEXT + 1].astype(jnp.int32)
        high, low = where // HZ, where % HZ
        block = lax.rem(lane_of((HZ, 3 * NBLK)), NBLK)
        chosen = jnp.where(block == high, 1.0, 0.0).astype(jnp.bfloat16)
        vals = jnp.dot(chosen, stack, preferred_element_type=jnp.float32)
        here = there = jnp.zeros(square, jnp.float32)
        for j in range(RBFW):
            w = got[:, W_WEIGHT + s * W_NEXT + j:W_WEIGHT + s * W_NEXT + j + 1]
            here = jnp.where(lane == low + j, w, here)
            there = jnp.where(lane + HZ == low + j, w, there)
        for c in range(3):
            v = total_of(vals[:, c * HZ:(c + 1) * HZ] * here + vals[:, (3 + c) * HZ:(4 + c) * HZ] * there)
            result = jnp.where(lane == 3 * s + c, v, result)
    back_out[...] = result
    mine = exchange_start(back_out, back_in, lsem.at[8], asem.at[2], asem.at[3])

    def combine(region):
        res = None
        for c, t in zip(coef, (t0, t1, t2, t3)):
            vals = [c * v for v in region.get(t)]
            res = vals if res is None else each(lambda a, b: a + b, res, vals)
        region.put(press, res)

    all_planes(combine, OX - 1, OX + CX + 1)
    for y in (OY - 1, OY + CY):
        combine(Strip(y))

    def correct(region):
        _, sides = pairs_of(region, press)
        for c in range(3):
            prior = region.get(pred.at[SLOT[c]])
            new = each(lambda v, a, b: v - 0.5 * (a - b), prior, sides[c][0], sides[c][1])
            for h in (0, 1):
                nvel[c, region.x - OX, h, region.y - OY:region.y - OY + region.n, :] = new[h]

    all_planes(correct)
    stores = []
    for h in (0, 1):
        z = slice(h * HZ, (h + 1) * HZ)
        stores.append(pltpu.make_async_copy(nvel.at[:, :, h], nv_hbm.at[:, :, :, z], lsem.at[2 * h]))
        stores.append(pltpu.make_async_copy(
            press.at[OX:OX + CX, h, OY:OY + CY, :], p_hbm.at[:, :, z], lsem.at[2 * h + 1]))
    for cp in stores:
        cp.start()
    for b in range(NBLK):
        disp_out[:, b * HZ:(b + 1) * HZ] = force.reshape(12 * NBLK, HZ)[pl.ds(b, 3, stride=NBLK), :]
    exchange_wait(mine, back_out, back_in, asem.at[2], asem.at[3])
    answers = jnp.transpose(back_in[...])[0:8]
    answers = jnp.concatenate(thirds(answers), axis=0)
    found = [jnp.dot(answers, table[:, s * HZ:(s + 1) * HZ], preferred_element_type=jnp.float32) for s in (0, 1)]
    found = [f[0:8] + f[8:16] + f[16:24] for f in found]
    iface_out[...] = found[0][0:3] + found[1][3:6]
    for cp in stores:
        cp.wait()


def local(velocity, damping, displacement, stiffness, connectivity, inv_mass, iface_cell, iface_owner, iface_node,
          rbf_weight, normals):
    field = (PX, 2, PY, HZ)
    f32, i32 = jnp.float32, jnp.int32
    anywhere = pl.BlockSpec(memory_space=pl.ANY)
    vmem = pl.BlockSpec(memory_space=pltpu.VMEM)
    smem = pl.BlockSpec(memory_space=pltpu.SMEM)
    square = pltpu.VMEM((HZ, HZ), f32)
    outs = pl.pallas_call(
        step_kernel,
        out_shape=(
            jax.ShapeDtypeStruct(velocity.shape, f32),
            jax.ShapeDtypeStruct(damping.shape, f32),
            jax.ShapeDtypeStruct(displacement.shape, f32),
            jax.ShapeDtypeStruct(normals.shape, f32),
            jax.ShapeDtypeStruct((8, HZ), f32),
        ),
        in_specs=[anywhere] * 3 + [vmem] * 3 + [smem] + [vmem] * 5,
        out_specs=(anywhere, anywhere, vmem, vmem, vmem),
        scratch_shapes=[
            pltpu.VMEM((3,) + field, f32),
            pltpu.VMEM(field, f32),
            pltpu.VMEM((3,) + field, f32),
            pltpu.VMEM(field, f32),
            pltpu.VMEM(field, f32),
            pltpu.VMEM(field, f32),
            pltpu.VMEM(field, f32),
            pltpu.VMEM(field, f32),
            pltpu.VMEM((3, CX, 2, CY, HZ), f32),
            pltpu.VMEM((12, 12, NBLK * HZ), f32),
            pltpu.VMEM((3, 40, HZ), f32),
            pltpu.VMEM((4, NBLK, HZ), i32),
            pltpu.VMEM((NBLK * 16, HZ), f32),
            pltpu.VMEM((12, NBLK, HZ), f32),
            pltpu.VMEM((3, NBLK, HZ), f32),
            pltpu.VMEM((3, 40, HZ), f32),
            square, square, square, square, square,
            pltpu.VMEM((HZ, 2 * HZ), jnp.bfloat16),
            pltpu.VMEM((3, 40, HZ), f32),
            square, square, square, square,
            pltpu.SemaphoreType.DMA((9,)),
            pltpu.SemaphoreType.DMA((4,)),
            pltpu.SemaphoreType.DMA((34,)),
            pltpu.SemaphoreType.DMA((34,)),
            pltpu.SemaphoreType.DMA((4,)),
        ],
        compiler_params=pltpu.CompilerParams(
            collective_id=0, has_side_effects=True, vmem_limit_bytes=60 << 20),
        name="step",
    )(
        velocity, damping, stiffness, displacement, connectivity, inv_mass.reshape(NBLK, HZ), iface_cell,
        iface_cell.reshape(1, NPTS), iface_owner.reshape(1, NPTS), iface_node.reshape(1, NPTS), rbf_weight, normals,
    )
    return outs[:4]


def solution(mesh):
    return jax.shard_map(
        local,
        mesh=mesh,
        in_specs=(
            P(None, "grp", "dom", None),
            P("grp", "dom", None),
            P(None, ("grp", "dom")),
            P(None, None, ("grp", "dom")),
            P(None, ("grp", "dom")),
            P(("grp", "dom")),
            P(("grp", "dom")),
            P(("grp", "dom"), None),
            P(("grp", "dom")),
            P(None, ("grp", "dom")),
            P(None, ("grp", "dom")),
        ),
        out_specs=(
            P(None, "grp", "dom", None),
            P("grp", "dom", None),
            P(None, ("grp", "dom")),
            P(None, ("grp", "dom")),
        ),
        check_vma=False,
    )
```

```python
import jax
import jax.numpy as jnp
from jax import lax
from jax.experimental import pallas as pl
from jax.experimental.pallas import tpu as pltpu
from jax.sharding import PartitionSpec as P

MESH = pl.DeviceIdType.MESH
NGRP, NDOM = 4, 32
NDEV = NGRP * NDOM
CX, CY, HZ = 16, 32, 128
PX, PY, OX, OY = CX + 4, CY + 16, 2, 8
SLOT = {0: 0, 2: 1, 1: 2}
SHIFT, HALF = 6.26, 6.24
TIME_STEP = 0.1
WALL_FRICTION = 0.5
SHELL_STEP = 0.5
RIM, RBFW, NBLK, NPTS = 64, 4, 32, 128
W_BASIS, W_WEIGHT, W_NODE, W_NEXT = 32, 47, 51, 32
PAIRS = [(i, j) for i in range(4) for j in range(i, 5)]


def rows_of(ref):
    return ref.reshape(PX * 2 * PY, HZ)


class Plane:
    def __init__(self, x, y, n):
        self.x, self.y, self.n = x, y, n

    def get(self, f, dx=0, dy=0):
        return [f[self.x + dx, h, self.y + dy:self.y + dy + self.n, :] for h in (0, 1)]

    def put(self, f, halves):
        for h in (0, 1):
            f[self.x, h, self.y:self.y + self.n, :] = halves[h]


class Strip:
    def __init__(self, y):
        self.y = y

    def at(self, dx, dy, h):
        return pl.ds(((OX + dx) * 2 + h) * PY + self.y + dy, CX, stride=2 * PY)

    def get(self, f, dx=0, dy=0):
        flat = rows_of(f)
        return [flat[self.at(dx, dy, h), :] for h in (0, 1)]

    def put(self, f, halves):
        flat = rows_of(f)
        for h in (0, 1):
            flat[self.at(0, 0, h), :] = halves[h]


def lanes(a):
    return lax.broadcasted_iota(jnp.int32, a.shape, 1)


def up(a):
    r0, r1 = (pltpu.roll(v, HZ - 1, 1) for v in a)
    edge = lanes(a[0]) == HZ - 1
    return [jnp.where(edge, r1, r0), jnp.where(edge, 0.0, r1)]


def down(a):
    r0, r1 = (pltpu.roll(v, 1, 1) for v in a)
    edge = lanes(a[0]) == 0
    return [jnp.where(edge, 0.0, r0), jnp.where(edge, r0, r1)]


def each(fn, *lists):
    return [fn(*vals) for vals in zip(*lists)]


def pairs_of(region, f):
    centre = region.get(f)
    return centre, (
        (region.get(f, 1, 0), region.get(f, -1, 0)),
        (region.get(f, 0, 1), region.get(f, 0, -1)),
        (up(centre), down(centre)),
    )


def predict(region, vel, c, out):
    others = [region.get(vel.at[SLOT[d]]) for d in range(3)]
    centre, sides = pairs_of(region, vel.at[SLOT[c]])
    res = []
    for h in (0, 1):
        lap = -6.0 * centre[h]
        adv = None
        for d in range(3):
            a, b = sides[d][0][h], sides[d][1][h]
            lap = lap + a + b
            term = others[d][h] * (0.5 * (a - b))
            adv = term if adv is None else adv + term
        res.append(centre[h] + TIME_STEP * (lap - adv))
    region.put(out.at[SLOT[c]], res)


def apply(region, damp, f):
    centre, sides = pairs_of(region, f)
    dv = region.get(damp)
    res = []
    for h in (0, 1):
        s = None
        for a, b in sides:
            s = a[h] + b[h] if s is None else s + a[h] + b[h]
        res.append(((dv[h] + (6.0 - SHIFT)) * centre[h] - s) * (1.0 / HALF))
    return res


def cheb(region, damp, f, before, out):
    res = apply(region, damp, f)
    if before is not None:
        res = each(lambda a, b: 2.0 * a - b, res, region.get(before))
    if out is not None:
        region.put(out, res)
    return res


def all_planes(fn, lo=OX, hi=OX + CX, parts=2, unroll=2):
    def body(x, carry):
        for k in range(parts):
            fn(Plane(x, OY + k * (CY // parts), CY // parts))
        return carry

    lax.fori_loop(lo, hi, body, 0, unroll=unroll)


def position():
    return lax.axis_index("grp"), lax.axis_index("dom")


def clear_outside(f):
    g, d = position()

    @pl.when(g == 0)
    def _():
        f[0:OX] = jnp.zeros((OX, 2, PY, HZ), jnp.float32)

    @pl.when(g == NGRP - 1)
    def _():
        f[OX + CX:PX] = jnp.zeros((PX - OX - CX, 2, PY, HZ), jnp.float32)

    @pl.when(d == 0)
    def _():
        f[:, :, 0:OY, :] = jnp.zeros((PX, 2, OY, HZ), jnp.float32)

    @pl.when(d == NDOM - 1)
    def _():
        f[:, :, OY + CY:PY, :] = jnp.zeros((PX, 2, PY - OY - CY, HZ), jnp.float32)


def neighbour(dg, dd):
    g, d = position()
    return lax.rem(g + dg + NGRP, NGRP), lax.rem(d + dd + NDOM, NDOM)


def sides_of(ref, lead, width):
    lo, hi = OX, OX + CX
    a, b = OY, OY + CY
    ys = slice(a, b)
    xs = slice(lo, hi)
    w = width
    return [
        ((1, 0), lead + (slice(hi - w, hi), slice(None), ys), lead + (slice(lo - w, lo), slice(None), ys)),
        ((-1, 0), lead + (slice(lo, lo + w), slice(None), ys), lead + (slice(hi, hi + w), slice(None), ys)),
        ((0, 1), lead + (xs, slice(None), slice(b - w, b)), lead + (xs, slice(None), slice(a - w, a))),
        ((0, -1), lead + (xs, slice(None), slice(a, a + w)), lead + (xs, slice(None), slice(b, b + w))),
    ]


def corners_of(ref, lead):
    out = []
    for dg in (1, -1):
        for dd in (1, -1):
            sx = OX + CX - 1 if dg == 1 else OX
            tx = OX - 1 if dg == 1 else OX + CX
            sy = OY + CY - 1 if dd == 1 else OY
            ty = OY - 1 if dd == 1 else OY + CY
            out.append((
                (dg, dd),
                lead + (slice(sx, sx + 1), slice(None), slice(sy, sy + 1)),
                lead + (slice(tx, tx + 1), slice(None), slice(ty, ty + 1)),
            ))
    return out


def start_all(ref, items, send, recv, base):
    copies = []
    for k, (way, src, dst) in enumerate(items):
        cp = pltpu.make_async_remote_copy(
            src_ref=ref.at[src], dst_ref=ref.at[dst],
            send_sem=send.at[base + k], recv_sem=recv.at[base + k],
            device_id=neighbour(*way), device_id_type=MESH,
        )
        cp.start()
        copies.append(cp)
    return copies


def everyone(fn):
    g, d = position()
    for dg in range(NGRP):
        tg = lax.rem(g + dg, NGRP)

        def body(i, carry):
            fn(tg, lax.rem(d + i, NDOM))
            return carry

        lax.fori_loop(0 if dg else 1, NDOM, body, 0, unroll=16 if dg else 31)


def greet_all():
    barrier = pltpu.get_barrier_semaphore()
    everyone(lambda tg, td: pl.semaphore_signal(barrier, inc=1, device_id=(tg, td), device_id_type=MESH))
    return barrier


def exchange_start(out_ref, in_ref, own, send, recv):
    g, d = position()
    me = g * NDOM + d
    mine = pltpu.make_async_copy(out_ref.at[pl.ds(me, 1)], in_ref.at[pl.ds(me, 1)], own)
    mine.start()
    everyone(lambda tg, td: pltpu.make_async_remote_copy(
        src_ref=out_ref.at[pl.ds(tg * NDOM + td, 1)], dst_ref=in_ref.at[pl.ds(me, 1)],
        send_sem=send, recv_sem=recv, device_id=(tg, td), device_id_type=MESH,
    ).start())
    return mine


def exchange_wait(mine, out_ref, in_ref, send, recv):
    rest = pl.ds(0, NDEV - 1)
    mine.wait()
    pltpu.make_async_copy(out_ref.at[rest], in_ref.at[rest], recv).wait()
    pltpu.make_async_copy(out_ref.at[rest], in_ref.at[rest], send).wait()


def iterate(gram):
    def times(v):
        out = [None] * 5

        def put(i, val):
            out[i] = val if out[i] is None else out[i] + val

        for j, val in enumerate(v):
            if val is None:
                continue
            put(j, SHIFT * val)
            if j == 0:
                put(1, HALF * val)
            else:
                put(j + 1, (0.5 * HALF) * val)
                put(j - 1, (0.5 * HALF) * val)
        return out

    worst = None

    def form(a, b):
        nonlocal worst
        total = size = None
        for i in range(5):
            for j in range(5):
                if a[i] is None or b[j] is None:
                    continue
                term = a[i] * b[j] * gram(min(i, j), max(i, j))
                total = term if total is None else total + term
                mag = jnp.abs(term)
                size = mag if size is None else size + mag
        ratio = total / size
        worst = ratio if worst is None else jnp.minimum(worst, ratio)
        return total

    def axpy(a, s, b):
        return [x if y is None else (s * y if x is None else x + s * y) for x, y in zip(a, b)]

    one = jnp.ones_like(gram(0, 0))
    r = [one, None, None, None, None]
    d = list(r)
    p = [None] * 5
    rr = gram(0, 0)
    for k in range(4):
        m = times(d)
        step = rr / form(d, m)
        p = axpy(p, step, d)
        if k == 3:
            break
        r = axpy(r, -step, m)
        new = form(r, r)
        d = axpy(r, new / rr, d)
        rr = new
    return p[:4], worst


def lane_of(shape):
    return lax.broadcasted_iota(jnp.int32, shape, 1)


def row_of(shape):
    return lax.broadcasted_iota(jnp.int32, shape, 0)


def thirds(x):
    a = x.astype(jnp.bfloat16)
    rest = x - a.astype(jnp.float32)
    b = rest.astype(jnp.bfloat16)
    return a, b, (rest - b.astype(jnp.float32)).astype(jnp.bfloat16)


def pick(onehot, x):
    width = x.shape[1]
    wide = jnp.concatenate(thirds(x), axis=1)
    out = jnp.dot(onehot, wide, preferred_element_type=jnp.float32)
    return out[:, :width] + out[:, width:2 * width] + out[:, 2 * width:]


def spread(src, dst, count, stride):
    for b in range(NBLK):
        dst[pl.ds(b, count, stride=stride), :] = src[:, b * HZ:(b + 1) * HZ]


def shell_gather(q, disp, conn, dofs):
    sub = row_of((8, HZ))
    for a in range(4):
        rel = conn[a, 8 * q:8 * q + 8, :] - HZ * (8 * q + sub)
        near = rel < HZ
        low = jnp.where(near, rel, rel - HZ)
        for c in range(3):
            here = jnp.take_along_axis(disp[c, 8 * q:8 * q + 8, :], low, axis=1, mode="promise_in_bounds")
            there = jnp.take_along_axis(disp[c, 8 * q + 1:8 * q + 9, :], low, axis=1, mode="promise_in_bounds")
            dofs[pl.ds(8 * q * 16 + 3 * a + c, 8, stride=16), :] = jnp.where(near, here, there)


def shell_product(q, stiff, dofs, force):
    sub = row_of((8, HZ))

    def body(i, carry):
        parts = []
        for b in range(8 * q, 8 * q + 8):
            z = slice(b * HZ, (b + 1) * HZ)
            top = stiff[i, 0:8, z] * dofs[b * 16:b * 16 + 8, :]
            low = stiff[i, 8:12, z] * dofs[b * 16 + 8:b * 16 + 12, :]
            parts.append(top + jnp.concatenate([low, jnp.zeros((4, HZ), jnp.float32)], axis=0))
        first = sub < 4
        parts = [
            jnp.where(first, parts[k], parts[k + 4]) + pltpu.roll(jnp.where(first, parts[k + 4], parts[k]), 4, 0)
            for k in range(4)
        ]
        for bit in (2, 1):
            keep = (sub & bit) == 0
            parts = [
                jnp.where(keep, parts[k] + pltpu.roll(parts[k], 8 - bit, 0),
                          parts[k + bit] + pltpu.roll(parts[k + bit], bit, 0))
                for k in range(bit)
            ]
        force[i, 8 * q:8 * q + 8, :] = parts[0]
        return carry

    lax.fori_loop(0, 12, body, 0)


def shell_scatter(q, conn, force, own, over):
    lane = lane_of((8, HZ))
    element = HZ * (8 * q + row_of((8, HZ))) + lane
    rel = [conn[a, 8 * q:8 * q + 8, :] - element for a in range(4)]
    vals = [[force[3 * a + c, 8 * q:8 * q + 8, :] for c in range(3)] for a in range(4)]

    def body(d, acc):
        hit = [r == d for r in rel]
        inside = lane >= d
        out = []
        for c in range(3):
            s = jnp.zeros((8, HZ), jnp.float32)
            for a in range(4):
                s = jnp.where(hit[a], vals[a][c], s)
            s = pltpu.roll(s, d, 1)
            out.append(acc[2 * c] + jnp.where(inside, s, 0.0))
            out.append(acc[2 * c + 1] + jnp.where(inside, 0.0, s))
        return tuple(out)

    acc = lax.fori_loop(0, RIM + 1, body, tuple(jnp.zeros((8, HZ), jnp.float32) for _ in range(6)), unroll=5)
    for c in range(3):
        own[c, 8 * q:8 * q + 8, :] = acc[2 * c]
        over[c, 8 * q + 1:8 * q + 9, :] = acc[2 * c + 1]


def sample(cells, f, mid0, mid1, dx, dy):
    def body(i, carry):
        for u in range(4):
            k = i * 4 + u
            cell = cells[k]
            x, y, h = (cell >> 13) + OX, ((cell >> 8) & (CY - 1)) + OY, (cell >> 7) & 1
            at = pl.ds(k, 1)
            mid0[at, :] = f[x, 0, pl.ds(y, 1), :]
            mid1[at, :] = f[x, 1, pl.ds(y, 1), :]
            dx[at, :] = f[x + 1, h, pl.ds(y, 1), :] - f[x - 1, h, pl.ds(y, 1), :]
            dy[at, :] = f[x, h, pl.ds(y + 1, 1), :] - f[x, h, pl.ds(y - 1, 1), :]
        return carry

    lax.fori_loop(0, NPTS // 4, body, 0)


def sample_centre(cells, fields, outs):
    def body(i, carry):
        for u in range(4):
            k = i * 4 + u
            cell = cells[k]
            x, y, h = (cell >> 13) + OX, ((cell >> 8) & (CY - 1)) + OY, (cell >> 7) & 1
            for f, o in zip(fields, outs):
                o[pl.ds(k, 1), :] = f[x, h, pl.ds(y, 1), :]
        return carry

    lax.fori_loop(0, NPTS // 4, body, 0)


def column(row):
    return jnp.transpose(jnp.broadcast_to(row, (HZ, HZ)))


def total_of(x):
    return jnp.sum(x, axis=1, keepdims=True)


def step_kernel(vel_hbm, damp_hbm, stiff_hbm, disp_in, conn_in, mass, cells, cell_row, owner, node, weight, normal,
                nv_hbm, p_hbm, disp_out, iface_out, flag_ref,
                vel, damp, pred, t0, t1, t2, t3, press, nvel, stiff,
                disp, conn, dofs, force, own, over, mid0, mid1, dx, dy, words, table, nodal,
                rows_out, rows_in, back_out, back_in, lsem, ksem, ssem, rsem, asem):
    barrier = greet_all()
    g, d = position()
    me = g * NDOM + d
    loads = []
    for h in (0, 1):
        z = slice(h * HZ, (h + 1) * HZ)
        for c in range(3):
            loads.append(pltpu.make_async_copy(
                vel_hbm.at[c, :, :, z], vel.at[SLOT[c], OX:OX + CX, h, OY:OY + CY, :], lsem.at[len(loads)]))
        loads.append(pltpu.make_async_copy(
            damp_hbm.at[:, :, z], damp.at[OX:OX + CX, h, OY:OY + CY, :], lsem.at[len(loads)]))
    for q in range(4):
        z = slice(q * 8 * HZ, (q + 1) * 8 * HZ)
        loads.append(pltpu.make_async_copy(stiff_hbm.at[:, :, z], stiff.at[:, :, z], ksem.at[q]))
    for cp in loads:
        cp.start()
    blocks = loads[8:]

    spread(disp_in, disp.reshape(3 * 40, HZ), 3, 40)
    spread(conn_in, conn.reshape(4 * NBLK, HZ), 4, NBLK)
    square = (HZ, HZ)
    for cp in loads[:8]:
        cp.wait()
    pl.semaphore_wait(barrier, NDEV - 1)

    one = slice(None)
    f_x, f_y, f_z = SLOT[0], SLOT[1], SLOT[2]
    faces = corners_of(vel, (one,))
    wide_x, wide_y = sides_of(vel, (f_x,), 2)[:2], sides_of(vel, (f_y,), 2)[2:]
    thin_x, thin_y = sides_of(vel, (slice(1, 3),), 1)[:2], sides_of(vel, (slice(0, 2),), 1)[2:]
    copies = start_all(vel, faces + wide_x + wide_y + thin_x + thin_y, ssem, rsem, 0)
    copies += start_all(damp, sides_of(damp, (), 1), ssem, rsem, 12)
    before, after = lax.rem(me + NDEV - 1, NDEV), lax.rem(me + 1, NDEV)
    rim = pltpu.make_async_remote_copy(
        src_ref=disp.at[:, 0:1, :], dst_ref=disp.at[:, NBLK:NBLK + 1, :], send_sem=ssem.at[32], recv_sem=rsem.at[32],
        device_id=(lax.div(before, NDOM), lax.rem(before, NDOM)), device_id_type=MESH)
    rim.start()
    for q in range(3):
        shell_gather(q, disp, conn, dofs)
        blocks[q].wait()
        shell_product(q, stiff, dofs, force)
    for cp in copies:
        cp.wait()
    for c in range(3):
        clear_outside(vel.at[c])

    def pred_main(region):
        for c in range(3):
            predict(region, vel, c, pred)

    all_planes(pred_main)
    for x in (OX - 1, OX + CX):
        for k in range(2):
            predict(Plane(x, OY + 16 * k, 16), vel, 0, pred)
    for y in (OY - 1, OY + CY):
        predict(Strip(y), vel, 1, pred)
    clear_outside(pred.at[f_x])
    clear_outside(pred.at[f_y])

    def diverge(region):
        fx, fy, fz = pred.at[f_x], pred.at[f_y], region.get(pred.at[f_z])
        s = each(lambda a, b: 0.5 * (a - b), region.get(fx, 1, 0), region.get(fx, -1, 0))
        s = each(lambda s, a, b: s + 0.5 * (a - b), s, region.get(fy, 0, 1), region.get(fy, 0, -1))
        s = each(lambda s, a, b: -(s + 0.5 * (a - b)), s, up(fz), down(fz))
        region.put(t0, s)

    all_planes(diverge)

    def swap(f, base):
        return start_all(f, corners_of(f, ()) + sides_of(f, (), 2), ssem, rsem, base)

    def grow(f, before, out):
        all_planes(lambda region: cheb(region, damp, f, before, out), OX - 1, OX + CX + 1)
        for y in (OY - 1, OY + CY):
            cheb(Strip(y), damp, f, before, out)
        clear_outside(out)

    moving = swap(t0, 16)
    rim.wait()

    @pl.when(me == NDEV - 1)
    def _():
        disp[:, NBLK:NBLK + 1, :] = jnp.zeros((3, 1, HZ), jnp.float32)

    shell_gather(3, disp, conn, dofs)
    blocks[3].wait()
    shell_product(3, stiff, dofs, force)
    shell_scatter(3, conn, force, own, over)
    edge = pltpu.make_async_remote_copy(
        src_ref=over.at[:, NBLK:NBLK + 1, :], dst_ref=over.at[:, 0:1, :], send_sem=ssem.at[33], recv_sem=rsem.at[33],
        device_id=(lax.div(after, NDOM), lax.rem(after, NDOM)), device_id_type=MESH)
    edge.start()
    shell_scatter(0, conn, force, own, over)
    for cp in moving:
        cp.wait()
    clear_outside(t0)
    grow(t0, None, t1)
    all_planes(lambda region: cheb(region, damp, t1, t0, t2))

    moving = swap(t2, 24)
    owns = owner[...] == row_of(square)
    first = jnp.min(jnp.where(owns, lane_of(square), HZ), axis=1, keepdims=True)
    for s in (0, 1):
        table[:, s * HZ:(s + 1) * HZ] = jnp.where(
            owns & ((lane_of(square) == first) == (s == 0)), 1.0, 0.0).astype(jnp.bfloat16)
    words[...] = jnp.zeros(square, jnp.float32)
    words[W_WEIGHT:W_WEIGHT + 4, :] = weight[...]
    words[W_NODE:W_NODE + 1, :] = node[...].astype(jnp.float32)
    words[...] = jnp.transpose(words[...])
    z_all = column(cell_row[...]) & (2 * HZ - 1)
    lane = lane_of(square)
    hit0, hit1 = lane == z_all, lane + HZ == z_all
    hit = hit0 | hit1
    normals = [column(normal[c:c + 1, :]) for c in range(3)]

    def place(word, values):
        words[...] += jnp.where(lane == word, total_of(values), 0.0)

    def basis_words(j, f):
        sample(cells, f, mid0, mid1, dx, dy)
        a, b = mid0[...], mid1[...]
        value = jnp.where(hit0, a, 0.0) + jnp.where(hit1, b, 0.0)
        slope = (jnp.where(lane == z_all + 1, a, 0.0) + jnp.where(lane + HZ == z_all + 1, b, 0.0)
                 - jnp.where(lane == z_all - 1, a, 0.0) - jnp.where(lane + HZ == z_all - 1, b, 0.0))
        slopes = (jnp.where(hit, dx[...], 0.0), jnp.where(hit, dy[...], 0.0), slope)
        for c in range(3):
            place(W_BASIS + 3 * (j + 1) + c, -value * normals[c] - (0.5 * WALL_FRICTION) * slopes[c])

    sample_centre(cells, [pred.at[SLOT[c]] for c in range(3)], [mid0, mid1, dx])
    for c, ref in enumerate((mid0, mid1, dx)):
        place(W_BASIS + c, jnp.where(hit, WALL_FRICTION * ref[...], 0.0))
    basis_words(0, t0)
    basis_words(1, t1)
    for cp in moving:
        cp.wait()
    clear_outside(t2)
    basis_words(2, t2)
    grow(t2, t1, t3)

    def dots(x, acc):
        acc = list(acc)
        for k in range(2):
            region = Plane(x, OY + 16 * k, 16)
            ts = [region.get(t) for t in (t0, t1, t2, t3)]
            ts.append(cheb(region, damp, t3, t2, None))
            for n, (i, j) in enumerate(PAIRS):
                for h in (0, 1):
                    prod = ts[i][h] * ts[j][h]
                    acc[n] = acc[n] + (prod[0:8] + prod[8:16])
        return tuple(acc)

    acc = lax.fori_loop(OX, OX + CX, dots, tuple(jnp.zeros((8, HZ), jnp.float32) for _ in PAIRS))
    basis_words(3, t3)
    lane1 = lane_of((1, HZ))
    row = jnp.zeros((1, HZ), jnp.float32)
    for n in range(len(PAIRS)):
        row = row + jnp.where(lane1 == n, total_of(jnp.sum(acc[n], axis=0, keepdims=True)), 0.0)
    payload = words[...]
    both = jnp.concatenate([payload, pltpu.roll(payload, W_NEXT, 1)], axis=0)
    rows_out[...] = pick(table[...], both) + row
    mine = exchange_start(rows_out, rows_in, lsem.at[8], asem.at[0], asem.at[1])
    shell_scatter(1, conn, force, own, over)
    shell_scatter(2, conn, force, own, over)
    edge.wait()

    @pl.when(me == 0)
    def _():
        over[:, 0:1, :] = jnp.zeros((3, 1, HZ), jnp.float32)

    exchange_wait(mine, rows_out, rows_in, asem.at[0], asem.at[1])
    got = rows_in[...]
    total = jnp.sum(got, axis=0, keepdims=True)
    gram = {}
    for n, key in enumerate(PAIRS):
        gram[key] = jnp.broadcast_to(total_of(jnp.where(lane1 == n, total, 0.0)), (1, HZ))
    coef, worst = iterate(lambda i, j: gram[(i, j)])
    flag_ref[0, 0] = jnp.where(worst > GUARD, 1, 0).astype(jnp.int32)[0, 0]

    words[...] = jnp.transpose(got)
    lefts, lefts2, rights, rights2 = [], [], [], []
    for s in (0, 1):
        at = W_BASIS + s * W_NEXT
        traction = words[at:at + 3, :]
        for j in range(4):
            traction = traction + coef[j] * words[at + 3 * (j + 1):at + 3 * (j + 1) + 3, :]
        where = words[W_NODE + s * W_NEXT:W_NODE + s * W_NEXT + 1, :].astype(jnp.int32)
        high, low = where // HZ, where % HZ
        block = row_of((NBLK, HZ))
        lefts.append(jnp.concatenate([jnp.where(block == high, traction[c:c + 1], 0.0) for c in range(3)], axis=0))
        lefts2.append(jnp.concatenate([jnp.where(block == high + 1, traction[c:c + 1], 0.0) for c in range(3)], axis=0))
        right = right2 = jnp.zeros(square, jnp.float32)
        for j in range(RBFW):
            w = words[W_WEIGHT + s * W_NEXT + j:W_WEIGHT + s * W_NEXT + j + 1, :]
            right = jnp.where(row_of(square) == low + j, w, right)
            right2 = jnp.where(row_of(square) + HZ == low + j, w, right2)
        rights.append(right)
        rights2.append(right2)
    applied = lax.dot_general(
        jnp.concatenate(lefts + lefts2, axis=1), jnp.concatenate(rights + rights2, axis=1),
        (((1,), (1,)), ((), ())), precision=lax.Precision.HIGHEST, preferred_element_type=jnp.float32)
    for c in range(3):
        net = own[c] + over[c, 0:NBLK, :]
        moved = mass[...] * (applied[c * NBLK:(c + 1) * NBLK] - net)
        nodal[c, 0:NBLK, :] = moved
        nodal[c, NBLK:NBLK + 8, :] = jnp.zeros((8, HZ), jnp.float32)
        force[c] = disp[c, 0:NBLK, :] + SHELL_STEP * moved
    near = jnp.concatenate([nodal[c, 0:NBLK, :] for c in range(3)] + [nodal[c, 1:NBLK + 1, :] for c in range(3)], axis=1)
    stack = jnp.concatenate(thirds(near), axis=0)
    result = jnp.zeros(square, jnp.float32)
    for s in (0, 1):
        where = got[:, W_NODE + s * W_NEXT:W_NODE + s * W_NEXT + 1].astype(jnp.int32)
        high, low = where // HZ, where % HZ
        block = lax.rem(lane_of((HZ, 3 * NBLK)), NBLK)
        chosen = jnp.where(block == high, 1.0, 0.0).astype(jnp.bfloat16)
        vals = jnp.dot(chosen, stack, preferred_element_type=jnp.float32)
        here = there = jnp.zeros(square, jnp.float32)
        for j in range(RBFW):
            w = got[:, W_WEIGHT + s * W_NEXT + j:W_WEIGHT + s * W_NEXT + j + 1]
            here = jnp.where(lane == low + j, w, here)
            there = jnp.where(lane + HZ == low + j, w, there)
        for c in range(3):
            v = total_of(vals[:, c * HZ:(c + 1) * HZ] * here + vals[:, (3 + c) * HZ:(4 + c) * HZ] * there)
            result = jnp.where(lane == 3 * s + c, v, result)
    back_out[...] = result
    mine = exchange_start(back_out, back_in, lsem.at[8], asem.at[2], asem.at[3])

    def combine(region):
        res = None
        for c, t in zip(coef, (t0, t1, t2, t3)):
            vals = [c * v for v in region.get(t)]
            res = vals if res is None else each(lambda a, b: a + b, res, vals)
        region.put(press, res)

    all_planes(combine, OX - 1, OX + CX + 1)
    for y in (OY - 1, OY + CY):
        combine(Strip(y))

    def correct(region):
        _, sides = pairs_of(region, press)
        for c in range(3):
            prior = region.get(pred.at[SLOT[c]])
            new = each(lambda v, a, b: v - 0.5 * (a - b), prior, sides[c][0], sides[c][1])
            for h in (0, 1):
                nvel[c, region.x - OX, h, region.y - OY:region.y - OY + region.n, :] = new[h]

    all_planes(correct)
    stores = []
    for h in (0, 1):
        z = slice(h * HZ, (h + 1) * HZ)
        stores.append(pltpu.make_async_copy(nvel.at[:, :, h], nv_hbm.at[:, :, :, z], lsem.at[2 * h]))
        stores.append(pltpu.make_async_copy(
            press.at[OX:OX + CX, h, OY:OY + CY, :], p_hbm.at[:, :, z], lsem.at[2 * h + 1]))
    for cp in stores:
        cp.start()
    for b in range(NBLK):
        disp_out[:, b * HZ:(b + 1) * HZ] = force.reshape(12 * NBLK, HZ)[pl.ds(b, 3, stride=NBLK), :]
    exchange_wait(mine, back_out, back_in, asem.at[2], asem.at[3])
    answers = jnp.transpose(back_in[...])[0:8]
    answers = jnp.concatenate(thirds(answers), axis=0)
    found = [jnp.dot(answers, table[:, s * HZ:(s + 1) * HZ], preferred_element_type=jnp.float32) for s in (0, 1)]
    found = [f[0:8] + f[8:16] + f[16:24] for f in found]
    iface_out[...] = found[0][0:3] + found[1][3:6]
    for cp in stores:
        cp.wait()


def fused(velocity, damping, displacement, stiffness, connectivity, inv_mass, iface_cell, iface_owner, iface_node,
          rbf_weight, normals):
    field = (PX, 2, PY, HZ)
    f32, i32 = jnp.float32, jnp.int32
    anywhere = pl.BlockSpec(memory_space=pl.ANY)
    vmem = pl.BlockSpec(memory_space=pltpu.VMEM)
    smem = pl.BlockSpec(memory_space=pltpu.SMEM)
    square = pltpu.VMEM((HZ, HZ), f32)
    outs = pl.pallas_call(
        step_kernel,
        out_shape=(
            jax.ShapeDtypeStruct(velocity.shape, f32),
            jax.ShapeDtypeStruct(damping.shape, f32),
            jax.ShapeDtypeStruct(displacement.shape, f32),
            jax.ShapeDtypeStruct(normals.shape, f32),
            jax.ShapeDtypeStruct((1, 1), i32),
        ),
        in_specs=[anywhere] * 3 + [vmem] * 3 + [smem] + [vmem] * 5,
        out_specs=(anywhere, anywhere, vmem, vmem, smem),
        scratch_shapes=[
            pltpu.VMEM((3,) + field, f32),
            pltpu.VMEM(field, f32),
            pltpu.VMEM((3,) + field, f32),
            pltpu.VMEM(field, f32),
            pltpu.VMEM(field, f32),
            pltpu.VMEM(field, f32),
            pltpu.VMEM(field, f32),
            pltpu.VMEM(field, f32),
            pltpu.VMEM((3, CX, 2, CY, HZ), f32),
            pltpu.VMEM((12, 12, NBLK * HZ), f32),
            pltpu.VMEM((3, 40, HZ), f32),
            pltpu.VMEM((4, NBLK, HZ), i32),
            pltpu.VMEM((NBLK * 16, HZ), f32),
            pltpu.VMEM((12, NBLK, HZ), f32),
            pltpu.VMEM((3, NBLK, HZ), f32),
            pltpu.VMEM((3, 40, HZ), f32),
            square, square, square, square, square,
            pltpu.VMEM((HZ, 2 * HZ), jnp.bfloat16),
            pltpu.VMEM((3, 40, HZ), f32),
            square, square, square, square,
            pltpu.SemaphoreType.DMA((9,)),
            pltpu.SemaphoreType.DMA((4,)),
            pltpu.SemaphoreType.DMA((34,)),
            pltpu.SemaphoreType.DMA((34,)),
            pltpu.SemaphoreType.DMA((4,)),
        ],
        compiler_params=pltpu.CompilerParams(
            collective_id=0, has_side_effects=True, vmem_limit_bytes=60 << 20),
        name="step",
    )(
        velocity, damping, stiffness, displacement, connectivity, inv_mass.reshape(NBLK, HZ), iface_cell,
        iface_cell.reshape(1, NPTS), iface_owner.reshape(1, NPTS), iface_node.reshape(1, NPTS), rbf_weight, normals,
    )
    return outs


ITERS = 4
VISCOSITY = 1.0
GUARD = 4e-4
UNIT_STEPS = ((1, 0, 0), (0, 1, 0), (0, 0, 1))


def with_halo(block, sides, width):
    for axis, dim in sides:
        count = lax.axis_size(axis)
        forward = [(i, i + 1) for i in range(count - 1)]
        backward = [(target, source) for source, target in forward]
        low = lax.ppermute(
            lax.slice_in_dim(block, block.shape[dim] - width, None, axis=dim), axis, forward
        )
        high = lax.ppermute(lax.slice_in_dim(block, 0, width, axis=dim), axis, backward)
        block = jnp.concatenate([low, block, high], axis=dim)
    return block


def from_behind(value, axis, steps):
    count = lax.axis_size(axis)
    leading, last = (max(0, -steps), min(count, count - steps))
    return lax.ppermute(value, axis, [(source, source + steps) for source in range(leading, last)])


def window_at(padded, offsets):
    size_x = padded.shape[-3] - 2
    size_y = padded.shape[-2] - 2
    size_z = padded.shape[-1] - 2
    return padded[
        ...,
        1 + offsets[0] : 1 + offsets[0] + size_x,
        1 + offsets[1] : 1 + offsets[1] + size_y,
        1 + offsets[2] : 1 + offsets[2] + size_z,
    ]


def backward(unit_step):
    return tuple((-value for value in unit_step))


def pad_depth(source):
    spec = [(0, 0)] * (source.ndim - 1) + [(1, 1)]
    return jnp.pad(source, spec)


def predictor(padded):
    centre = window_at(padded, (0, 0, 0))
    laplace = -6.0 * centre
    advect = jnp.zeros_like(centre)
    for axis_num, unit_step in enumerate(UNIT_STEPS):
        forward = window_at(padded, unit_step)
        behind_cells = window_at(padded, backward(unit_step))
        laplace = laplace + forward + behind_cells
        advect = advect + centre[axis_num : axis_num + 1] * (0.5 * (forward - behind_cells))
    return centre + TIME_STEP * (VISCOSITY * laplace - advect)


def divergence(padded):
    summed = jnp.zeros(window_at(padded[0], (0, 0, 0)).shape, jnp.float32)
    for axis_num, unit_step in enumerate(UNIT_STEPS):
        component = padded[axis_num]
        summed = summed + 0.5 * (
            window_at(component, unit_step) - window_at(component, backward(unit_step))
        )
    return -summed


def padded_cells(source):
    extended = with_halo(source, (("grp", 0), ("dom", 1)), 1)
    return pad_depth(extended)


def operate(source, damping):
    padded = padded_cells(source)
    centre = window_at(padded, (0, 0, 0))
    beside = jnp.zeros_like(centre)
    for unit_step in UNIT_STEPS:
        beside = beside + window_at(padded, unit_step) + window_at(padded, backward(unit_step))
    return (6.0 + damping) * centre - beside


def squares(residual):
    return lax.psum(jnp.sum(residual * residual), ("grp", "dom"))


def plain(
    velocity,
    damping,
    displacement,
    stiffness,
    connectivity,
    inv_mass,
    iface_cell,
    iface_owner,
    iface_node,
    rbf_weight,
    normals,
):
    shell_nodes = displacement.shape[1]
    rim_values = from_behind(displacement[:, :RIM], ("grp", "dom"), -1)
    extended_disp = jnp.concatenate([displacement, rim_values], axis=1)
    element_count = connectivity.shape[1]
    corner_values = extended_disp[:, connectivity]
    element_dofs = jnp.transpose(corner_values, (1, 0, 2)).reshape(12, element_count)
    element_force = jnp.sum(stiffness * element_dofs[None], axis=1).reshape(4, 3, element_count)
    node_force = jnp.zeros((3, shell_nodes + RIM), jnp.float32)
    for corner in range(4):
        node_force = node_force.at[:, connectivity[corner]].add(element_force[corner])
    rim_force = from_behind(node_force[:, shell_nodes:], ("grp", "dom"), 1)
    stiff_force = node_force[:, :shell_nodes] + jnp.pad(rim_force, ((0, 0), (0, shell_nodes - RIM)))
    extended = with_halo(velocity, (("grp", 1), ("dom", 2)), 1)
    predicted = predictor(pad_depth(extended))
    star_wide = with_halo(predicted, (("grp", 1), ("dom", 2)), 1)
    star_padded = pad_depth(star_wide)
    right_side = divergence(star_padded)
    pressure = jnp.zeros_like(right_side)
    residual = right_side
    direction = right_side
    norm_now = squares(residual)
    for sweep in range(ITERS):
        mapped = operate(direction, damping)
        step_size = norm_now / lax.psum(jnp.sum(direction * mapped), ("grp", "dom"))
        pressure = pressure + step_size * direction
        residual = residual - step_size * mapped
        norm_next = squares(residual)
        direction = residual + norm_next / norm_now * direction
        norm_now = norm_next
    pressure_wide = padded_cells(pressure)
    new_velocity = predicted - jnp.stack(
        [
            0.5
            * (window_at(pressure_wide, unit_step) - window_at(pressure_wide, backward(unit_step)))
            for unit_step in UNIT_STEPS
        ]
    )
    pressure_at = pressure.reshape(-1)[iface_cell]
    velocity_at = new_velocity.reshape(3, -1)[:, iface_cell]
    traction = -pressure_at[None] * normals + WALL_FRICTION * velocity_at
    owner_dev = iface_owner[:, 0]
    point_count = owner_dev.shape[0]
    devices = lax.axis_size("grp") * lax.axis_size("dom")
    owner_cap = max(2, 2 * point_count // devices)
    order_index = lax.iota(jnp.int32, point_count)
    earlier = (owner_dev[None, :] == owner_dev[:, None]) & (
        order_index[None, :] < order_index[:, None]
    )
    slot_rank = jnp.sum(earlier.astype(jnp.int32), axis=1)
    slot_index = owner_dev * owner_cap + slot_rank
    slot_count = devices * owner_cap
    payload = jnp.concatenate([traction, rbf_weight, iface_node.astype(jnp.float32)[None]], axis=0)
    outgoing = jnp.zeros((payload.shape[0], slot_count), jnp.float32).at[:, slot_index].set(payload)
    received = lax.all_to_all(outgoing, ("grp", "dom"), split_axis=1, concat_axis=1, tiled=True)
    slot_traction = received[:3]
    slot_weight = received[3 : 3 + RBFW]
    slot_node = received[3 + RBFW].astype(jnp.int32)
    applied = jnp.zeros((3, shell_nodes), jnp.float32)
    for offset in range(RBFW):
        applied = applied.at[:, slot_node + offset].add(slot_weight[offset][None] * slot_traction)
    node_velocity = inv_mass[None] * (applied - stiff_force)
    new_displacement = displacement + SHELL_STEP * node_velocity
    slot_velocity = jnp.zeros((3, slot_count), jnp.float32)
    for offset in range(RBFW):
        slot_velocity = (
            slot_velocity + slot_weight[offset][None] * node_velocity[:, slot_node + offset]
        )
    returned_vals = lax.all_to_all(
        slot_velocity, ("grp", "dom"), split_axis=1, concat_axis=1, tiled=True
    )
    iface_velocity = returned_vals[:, slot_index]
    return (new_velocity, pressure, new_displacement, iface_velocity)


def relay_kernel(*refs):
    count = (len(refs) - 2) // 3
    ins, outs, held = refs[:count], refs[count:2 * count], refs[2 * count:3 * count]
    come, go = refs[-2:]
    pieces = []
    for a, b, c in zip(ins, outs, held):
        if len(a.shape) > 2:
            pieces += [(a.at[k], b.at[k], c.at[k]) for k in range(a.shape[0])]
        else:
            pieces.append((a, b, c))
    arrive = [pltpu.make_async_copy(a, c, come.at[n]) for n, (a, b, c) in enumerate(pieces)]
    leave = [pltpu.make_async_copy(c, b, go.at[n]) for n, (a, b, c) in enumerate(pieces)]
    for cp in arrive:
        cp.start()
    for x, y in zip(arrive, leave):
        x.wait()
        y.start()
    for y in leave:
        y.wait()


def relay(new_velocity, pressure, new_displacement, iface_velocity):
    arrays = (new_velocity, pressure.reshape(4, CX // 4, CY, 2 * HZ), new_displacement, iface_velocity)
    anywhere = pl.BlockSpec(memory_space=pl.ANY)
    count = 3 + 4 + 2
    outs = pl.pallas_call(
        relay_kernel,
        out_shape=tuple(jax.ShapeDtypeStruct(a.shape, a.dtype) for a in arrays),
        in_specs=[anywhere] * len(arrays),
        out_specs=(anywhere,) * len(arrays),
        scratch_shapes=[pltpu.VMEM(a.shape, a.dtype) for a in arrays]
        + [pltpu.SemaphoreType.DMA((count,)), pltpu.SemaphoreType.DMA((count,))],
        compiler_params=pltpu.CompilerParams(vmem_limit_bytes=60 << 20),
        name="relay",
    )(*arrays)
    return outs[0], outs[1].reshape(pressure.shape), outs[2], outs[3]


def local(*args):
    *outs, sound = fused(*args)
    return lax.cond(sound.reshape(()) > 0, lambda: relay(*outs), lambda: plain(*args))


def solution(mesh):
    return jax.shard_map(
        local,
        mesh=mesh,
        in_specs=(
            P(None, "grp", "dom", None),
            P("grp", "dom", None),
            P(None, ("grp", "dom")),
            P(None, None, ("grp", "dom")),
            P(None, ("grp", "dom")),
            P(("grp", "dom")),
            P(("grp", "dom")),
            P(("grp", "dom"), None),
            P(("grp", "dom")),
            P(None, ("grp", "dom")),
            P(None, ("grp", "dom")),
        ),
        out_specs=(
            P(None, "grp", "dom", None),
            P("grp", "dom", None),
            P(None, ("grp", "dom")),
            P(None, ("grp", "dom")),
        ),
        check_vma=False,
    )
```

```python
import jax
import jax.numpy as jnp
from jax import lax
from jax.experimental import pallas as pl
from jax.experimental.pallas import tpu as pltpu
from jax.sharding import PartitionSpec as P

MESH = pl.DeviceIdType.MESH
NGRP, NDOM = 4, 32
NDEV = NGRP * NDOM
CX, CY, HZ = 16, 32, 128
PX, PY, OX, OY = CX + 4, CY + 16, 2, 8
SLOT = {0: 0, 2: 1, 1: 2}
SHIFT, HALF = 6.26, 6.24
TIME_STEP = 0.1
WALL_FRICTION = 0.5
SHELL_STEP = 0.5
RIM, RBFW, NBLK, NPTS = 64, 4, 32, 128
W_BASIS, W_WEIGHT, W_NODE, W_NEXT = 32, 47, 51, 32
PAIRS = [(i, j) for i in range(4) for j in range(i, 5)]


def rows_of(ref):
    return ref.reshape(PX * 2 * PY, HZ)


class Plane:
    def __init__(self, x, y, n):
        self.x, self.y, self.n = x, y, n

    def get(self, f, dx=0, dy=0):
        return [f[self.x + dx, h, self.y + dy:self.y + dy + self.n, :] for h in (0, 1)]

    def put(self, f, halves):
        for h in (0, 1):
            f[self.x, h, self.y:self.y + self.n, :] = halves[h]


class Inner:
    def __init__(self, x, k):
        self.x, self.k, self.n = x, k, CY // 2
        self.y = OY + k * self.n

    def get(self, f, dx=0, dy=0):
        if dy == (1 if self.k else -1):
            own = [f[self.x + dx, h, self.y:self.y + self.n, :] for h in (0, 1)]
            return [pltpu.roll(v, 1 if dy < 0 else self.n - 1, 0) for v in own]
        return [f[self.x + dx, h, self.y + dy:self.y + dy + self.n, :] for h in (0, 1)]

    def put(self, f, halves):
        for h in (0, 1):
            f[self.x, h, self.y:self.y + self.n, :] = halves[h]


class Strip:
    def __init__(self, y):
        self.y = y

    def at(self, dx, dy, h):
        return pl.ds(((OX + dx) * 2 + h) * PY + self.y + dy, CX, stride=2 * PY)

    def get(self, f, dx=0, dy=0):
        flat = rows_of(f)
        return [flat[self.at(dx, dy, h), :] for h in (0, 1)]

    def put(self, f, halves):
        flat = rows_of(f)
        for h in (0, 1):
            flat[self.at(0, 0, h), :] = halves[h]


def lanes(a):
    return lax.broadcasted_iota(jnp.int32, a.shape, 1)


def up(a):
    r0, r1 = (pltpu.roll(v, HZ - 1, 1) for v in a)
    edge = lanes(a[0]) == HZ - 1
    return [jnp.where(edge, r1, r0), jnp.where(edge, 0.0, r1)]


def down(a):
    r0, r1 = (pltpu.roll(v, 1, 1) for v in a)
    edge = lanes(a[0]) == 0
    return [jnp.where(edge, 0.0, r0), jnp.where(edge, r0, r1)]


def each(fn, *lists):
    return [fn(*vals) for vals in zip(*lists)]


def pairs_of(region, f):
    centre = region.get(f)
    return centre, (
        (region.get(f, 1, 0), region.get(f, -1, 0)),
        (region.get(f, 0, 1), region.get(f, 0, -1)),
        (up(centre), down(centre)),
    )


def predict(region, vel, c, out):
    others = [region.get(vel.at[SLOT[d]]) for d in range(3)]
    centre, sides = pairs_of(region, vel.at[SLOT[c]])
    res = []
    for h in (0, 1):
        lap = -6.0 * centre[h]
        adv = None
        for d in range(3):
            a, b = sides[d][0][h], sides[d][1][h]
            lap = lap + a + b
            term = others[d][h] * (0.5 * (a - b))
            adv = term if adv is None else adv + term
        res.append(centre[h] + TIME_STEP * (lap - adv))
    region.put(out.at[SLOT[c]], res)


def apply(region, damp, f):
    centre, sides = pairs_of(region, f)
    dv = region.get(damp)
    res = []
    for h in (0, 1):
        s = None
        for a, b in sides:
            s = a[h] + b[h] if s is None else s + a[h] + b[h]
        res.append(((dv[h] + (6.0 - SHIFT)) * centre[h] - s) * (1.0 / HALF))
    return res


def cheb(region, damp, f, before, out):
    res = apply(region, damp, f)
    if before is not None:
        res = each(lambda a, b: 2.0 * a - b, res, region.get(before))
    if out is not None:
        region.put(out, res)
    return res


def all_planes(fn, lo=OX, hi=OX + CX, parts=2, unroll=2):
    def body(x, carry):
        for k in range(parts):
            fn(Plane(x, OY + k * (CY // parts), CY // parts))
        return carry

    lax.fori_loop(lo, hi, body, 0, unroll=unroll)


def inner_planes(fn):
    def body(x, carry):
        for k in range(2):
            fn(Inner(x, k))
        return carry

    lax.fori_loop(OX + 1, OX + CX - 1, body, 0, unroll=2)


def edge_planes(fn, out):
    def body(i, carry):
        for k in range(2):
            for base in (OX - out, OX + CX - 1):
                fn(Plane(base + i, OY + k * (CY // 2), CY // 2))
        return carry

    lax.fori_loop(0, 1 + out, body, 0, unroll=1 + out)


def position():
    return lax.axis_index("grp"), lax.axis_index("dom")


def clear_outside(f):
    g, d = position()

    @pl.when(g == 0)
    def _():
        f[0:OX] = jnp.zeros((OX, 2, PY, HZ), jnp.float32)

    @pl.when(g == NGRP - 1)
    def _():
        f[OX + CX:PX] = jnp.zeros((PX - OX - CX, 2, PY, HZ), jnp.float32)

    @pl.when(d == 0)
    def _():
        f[:, :, 0:OY, :] = jnp.zeros((PX, 2, OY, HZ), jnp.float32)

    @pl.when(d == NDOM - 1)
    def _():
        f[:, :, OY + CY:PY, :] = jnp.zeros((PX, 2, PY - OY - CY, HZ), jnp.float32)


def neighbour(dg, dd):
    g, d = position()
    return lax.rem(g + dg + NGRP, NGRP), lax.rem(d + dd + NDOM, NDOM)


def sides_of(ref, lead, width):
    lo, hi = OX, OX + CX
    a, b = OY, OY + CY
    ys = slice(a, b)
    xs = slice(lo, hi)
    w = width
    return [
        ((1, 0), lead + (slice(hi - w, hi), slice(None), ys), lead + (slice(lo - w, lo), slice(None), ys)),
        ((-1, 0), lead + (slice(lo, lo + w), slice(None), ys), lead + (slice(hi, hi + w), slice(None), ys)),
        ((0, 1), lead + (xs, slice(None), slice(b - w, b)), lead + (xs, slice(None), slice(a - w, a))),
        ((0, -1), lead + (xs, slice(None), slice(a, a + w)), lead + (xs, slice(None), slice(b, b + w))),
    ]


def corners_of(ref, lead):
    out = []
    for dg in (1, -1):
        for dd in (1, -1):
            sx = OX + CX - 1 if dg == 1 else OX
            tx = OX - 1 if dg == 1 else OX + CX
            sy = OY + CY - 1 if dd == 1 else OY
            ty = OY - 1 if dd == 1 else OY + CY
            out.append((
                (dg, dd),
                lead + (slice(sx, sx + 1), slice(None), slice(sy, sy + 1)),
                lead + (slice(tx, tx + 1), slice(None), slice(ty, ty + 1)),
            ))
    return out


def start_all(ref, items, send, recv, base):
    copies = []
    for k, (way, src, dst) in enumerate(items):
        cp = pltpu.make_async_remote_copy(
            src_ref=ref.at[src], dst_ref=ref.at[dst],
            send_sem=send.at[base + k], recv_sem=recv.at[base + k],
            device_id=neighbour(*way), device_id_type=MESH,
        )
        cp.start()
        copies.append(cp)
    return copies


def everyone(fn):
    g, d = position()
    for dg in (2, 1, 3, 0):
        tg = lax.rem(g + dg, NGRP)

        def body(i, carry):
            fn(tg, lax.rem(d + i, NDOM))
            return carry

        if dg:
            lax.fori_loop(8, 8 + NDOM, body, 0, unroll=16)
        else:
            lax.fori_loop(8, NDOM, body, 0, unroll=12)
            lax.fori_loop(1, 8, body, 0, unroll=7)


def greet_near():
    barrier = pltpu.get_barrier_semaphore()
    for dg in (-1, 0, 1):
        for dd in (-1, 0, 1):
            if dg or dd:
                pl.semaphore_signal(barrier, inc=1, device_id=neighbour(dg, dd), device_id_type=MESH)
    return barrier


def pass_on(token, reach):
    for dd in (reach, -reach):
        pl.semaphore_signal(token, inc=1, device_id=neighbour(0, dd), device_id_type=MESH)


def exchange_start(out_ref, in_ref, own, send, recv):
    g, d = position()
    me = g * NDOM + d
    mine = pltpu.make_async_copy(out_ref.at[pl.ds(me, 1)], in_ref.at[pl.ds(me, 1)], own)
    mine.start()
    everyone(lambda tg, td: pltpu.make_async_remote_copy(
        src_ref=out_ref.at[pl.ds(tg * NDOM + td, 1)], dst_ref=in_ref.at[pl.ds(me, 1)],
        send_sem=send, recv_sem=recv, device_id=(tg, td), device_id_type=MESH,
    ).start())
    return mine


def exchange_wait(mine, out_ref, in_ref, send, recv):
    rest = pl.ds(0, NDEV - 1)
    mine.wait()
    pltpu.make_async_copy(out_ref.at[rest], in_ref.at[rest], recv).wait()
    pltpu.make_async_copy(out_ref.at[rest], in_ref.at[rest], send).wait()


def iterate(gram):
    def times(v):
        out = [None] * 5

        def put(i, val):
            out[i] = val if out[i] is None else out[i] + val

        for j, val in enumerate(v):
            if val is None:
                continue
            put(j, SHIFT * val)
            if j == 0:
                put(1, HALF * val)
            else:
                put(j + 1, (0.5 * HALF) * val)
                put(j - 1, (0.5 * HALF) * val)
        return out

    worst = None

    def form(a, b):
        nonlocal worst
        total = size = None
        for i in range(5):
            for j in range(5):
                if a[i] is None or b[j] is None:
                    continue
                term = a[i] * b[j] * gram(min(i, j), max(i, j))
                total = term if total is None else total + term
                mag = jnp.abs(term)
                size = mag if size is None else size + mag
        ratio = total / size
        worst = ratio if worst is None else jnp.minimum(worst, ratio)
        return total

    def axpy(a, s, b):
        return [x if y is None else (s * y if x is None else x + s * y) for x, y in zip(a, b)]

    one = jnp.ones_like(gram(0, 0))
    r = [one, None, None, None, None]
    d = list(r)
    p = [None] * 5
    rr = gram(0, 0)
    for k in range(4):
        m = times(d)
        step = rr / form(d, m)
        p = axpy(p, step, d)
        if k == 3:
            break
        r = axpy(r, -step, m)
        new = form(r, r)
        d = axpy(r, new / rr, d)
        rr = new
    return p[:4], worst


def lane_of(shape):
    return lax.broadcasted_iota(jnp.int32, shape, 1)


def row_of(shape):
    return lax.broadcasted_iota(jnp.int32, shape, 0)


def thirds(x):
    a = x.astype(jnp.bfloat16)
    rest = x - a.astype(jnp.float32)
    b = rest.astype(jnp.bfloat16)
    return a, b, (rest - b.astype(jnp.float32)).astype(jnp.bfloat16)


def pick(onehot, x):
    width = x.shape[1]
    wide = jnp.concatenate(thirds(x), axis=1)
    out = jnp.dot(onehot, wide, preferred_element_type=jnp.float32)
    return out[:, :width] + out[:, width:2 * width] + out[:, 2 * width:]


def spread(src, dst, count, stride):
    for b in range(NBLK):
        dst[pl.ds(b, count, stride=stride), :] = src[:, b * HZ:(b + 1) * HZ]


def shell_gather(q, disp, conn, dofs):
    sub = row_of((8, HZ))
    for a in range(4):
        rel = conn[a, 8 * q:8 * q + 8, :] - HZ * (8 * q + sub)
        near = rel < HZ
        low = jnp.where(near, rel, rel - HZ)
        for c in range(3):
            here = jnp.take_along_axis(disp[c, 8 * q:8 * q + 8, :], low, axis=1, mode="promise_in_bounds")
            there = jnp.take_along_axis(disp[c, 8 * q + 1:8 * q + 9, :], low, axis=1, mode="promise_in_bounds")
            dofs[pl.ds(8 * q * 16 + 3 * a + c, 8, stride=16), :] = jnp.where(near, here, there)


def shell_product(q, stiff, dofs, force):
    sub = row_of((8, HZ))

    def body(i, carry):
        parts = []
        for b in range(8 * q, 8 * q + 8):
            z = slice(b * HZ, (b + 1) * HZ)
            top = stiff[i, 0:8, z] * dofs[b * 16:b * 16 + 8, :]
            low = stiff[i, 8:12, z] * dofs[b * 16 + 8:b * 16 + 12, :]
            parts.append(top + jnp.concatenate([low, jnp.zeros((4, HZ), jnp.float32)], axis=0))
        first = sub < 4
        parts = [
            jnp.where(first, parts[k], parts[k + 4]) + pltpu.roll(jnp.where(first, parts[k + 4], parts[k]), 4, 0)
            for k in range(4)
        ]
        for bit in (2, 1):
            keep = (sub & bit) == 0
            parts = [
                jnp.where(keep, parts[k] + pltpu.roll(parts[k], 8 - bit, 0),
                          parts[k + bit] + pltpu.roll(parts[k + bit], bit, 0))
                for k in range(bit)
            ]
        force[i, 8 * q:8 * q + 8, :] = parts[0]
        return carry

    lax.fori_loop(0, 12, body, 0)


def shell_scatter(q, conn, force, own, over):
    lane = lane_of((8, HZ))
    element = HZ * (8 * q + row_of((8, HZ))) + lane
    rel = [conn[a, 8 * q:8 * q + 8, :] - element for a in range(4)]
    vals = [[force[3 * a + c, 8 * q:8 * q + 8, :] for c in range(3)] for a in range(4)]

    def body(d, acc):
        hit = [r == d for r in rel]
        inside = lane >= d
        out = []
        for c in range(3):
            s = jnp.zeros((8, HZ), jnp.float32)
            for a in range(4):
                s = jnp.where(hit[a], vals[a][c], s)
            s = pltpu.roll(s, d, 1)
            out.append(acc[2 * c] + jnp.where(inside, s, 0.0))
            out.append(acc[2 * c + 1] + jnp.where(inside, 0.0, s))
        return tuple(out)

    acc = lax.fori_loop(0, RIM + 1, body, tuple(jnp.zeros((8, HZ), jnp.float32) for _ in range(6)), unroll=5)
    for c in range(3):
        own[c, 8 * q:8 * q + 8, :] = acc[2 * c]
        over[c, 8 * q + 1:8 * q + 9, :] = acc[2 * c + 1]


def sample(cells, f, mid0, mid1, dx, dy):
    def body(i, carry):
        for u in range(4):
            k = i * 4 + u
            cell = cells[k]
            x, y, h = (cell >> 13) + OX, ((cell >> 8) & (CY - 1)) + OY, (cell >> 7) & 1
            at = pl.ds(k, 1)
            mid0[at, :] = f[x, 0, pl.ds(y, 1), :]
            mid1[at, :] = f[x, 1, pl.ds(y, 1), :]
            dx[at, :] = f[x + 1, h, pl.ds(y, 1), :] - f[x - 1, h, pl.ds(y, 1), :]
            dy[at, :] = f[x, h, pl.ds(y + 1, 1), :] - f[x, h, pl.ds(y - 1, 1), :]
        return carry

    lax.fori_loop(0, NPTS // 4, body, 0)


def sample_centre(cells, fields, outs):
    def body(i, carry):
        for u in range(4):
            k = i * 4 + u
            cell = cells[k]
            x, y, h = (cell >> 13) + OX, ((cell >> 8) & (CY - 1)) + OY, (cell >> 7) & 1
            for f, o in zip(fields, outs):
                o[pl.ds(k, 1), :] = f[x, h, pl.ds(y, 1), :]
        return carry

    lax.fori_loop(0, NPTS // 4, body, 0)


def column(row):
    return jnp.transpose(jnp.broadcast_to(row, (HZ, HZ)))


def total_of(x):
    return jnp.sum(x, axis=1, keepdims=True)


def step_kernel(vel_hbm, damp_hbm, stiff_hbm, disp_in, conn_in, mass, cells, cell_row, owner, node, weight, normal,
                nv_hbm, p_hbm, disp_out, iface_out, flag_ref,
                vel, damp, pred, t0, t1, t2, t3, press, nvel, stiff,
                disp, conn, dofs, force, own, over, mid0, mid1, dx, dy, words, table, nodal,
                rows_out, rows_in, back_out, back_in, lsem, ksem, ssem, rsem, asem, tokens):
    barrier = greet_near()
    g, d = position()
    me = g * NDOM + d
    loads = []
    for h in (0, 1):
        z = slice(h * HZ, (h + 1) * HZ)
        for c in range(3):
            loads.append(pltpu.make_async_copy(
                vel_hbm.at[c, :, :, z], vel.at[SLOT[c], OX:OX + CX, h, OY:OY + CY, :], lsem.at[len(loads)]))
        loads.append(pltpu.make_async_copy(
            damp_hbm.at[:, :, z], damp.at[OX:OX + CX, h, OY:OY + CY, :], lsem.at[len(loads)]))
    for q in range(4):
        z = slice(q * 8 * HZ, (q + 1) * 8 * HZ)
        loads.append(pltpu.make_async_copy(stiff_hbm.at[:, :, z], stiff.at[:, :, z], ksem.at[q]))
    for cp in loads:
        cp.start()
    blocks = loads[8:]

    spread(disp_in, disp.reshape(3 * 40, HZ), 3, 40)
    spread(conn_in, conn.reshape(4 * NBLK, HZ), 4, NBLK)
    square = (HZ, HZ)
    for cp in loads[:8]:
        cp.wait()
    pl.semaphore_wait(barrier, 8)

    one = slice(None)
    f_x, f_y, f_z = SLOT[0], SLOT[1], SLOT[2]
    faces = corners_of(vel, (one,))
    wide_x, wide_y = sides_of(vel, (f_x,), 2)[:2], sides_of(vel, (f_y,), 2)[2:]
    thin_x, thin_y = sides_of(vel, (slice(1, 3),), 1)[:2], sides_of(vel, (slice(0, 2),), 1)[2:]
    copies = start_all(vel, faces + wide_x + wide_y + thin_x + thin_y, ssem, rsem, 0)
    damps = start_all(damp, sides_of(damp, (), 1), ssem, rsem, 12)
    before, after = lax.rem(me + NDEV - 1, NDEV), lax.rem(me + 1, NDEV)
    rim = pltpu.make_async_remote_copy(
        src_ref=disp.at[:, 0:1, :], dst_ref=disp.at[:, NBLK:NBLK + 1, :], send_sem=ssem.at[32], recv_sem=rsem.at[32],
        device_id=(lax.div(before, NDOM), lax.rem(before, NDOM)), device_id_type=MESH)
    rim.start()
    for q in range(3):
        shell_gather(q, disp, conn, dofs)
        blocks[q].wait()
        shell_product(q, stiff, dofs, force)

    def pred_main(region):
        for c in range(3):
            predict(region, vel, c, pred)

    inner_planes(pred_main)
    for cp in copies:
        cp.wait()
    pass_on(tokens.at[0], 2)
    for c in range(3):
        clear_outside(vel.at[c])

    edge_planes(pred_main, 0)
    for y in (OY, OY + CY - 1):
        pred_main(Strip(y))
    for x in (OX - 1, OX + CX):
        for k in range(2):
            predict(Plane(x, OY + 16 * k, 16), vel, 0, pred)
    for y in (OY - 1, OY + CY):
        predict(Strip(y), vel, 1, pred)
    clear_outside(pred.at[f_x])
    clear_outside(pred.at[f_y])

    def diverge(region):
        fx, fy, fz = pred.at[f_x], pred.at[f_y], region.get(pred.at[f_z])
        s = each(lambda a, b: 0.5 * (a - b), region.get(fx, 1, 0), region.get(fx, -1, 0))
        s = each(lambda s, a, b: s + 0.5 * (a - b), s, region.get(fy, 0, 1), region.get(fy, 0, -1))
        s = each(lambda s, a, b: -(s + 0.5 * (a - b)), s, up(fz), down(fz))
        region.put(t0, s)

    all_planes(diverge)

    def swap(f, base):
        return start_all(f, corners_of(f, ()) + sides_of(f, (), 2), ssem, rsem, base)

    def grow_inner(f, before, out):
        inner_planes(lambda region: cheb(region, damp, f, before, out))

    def grow_edge(f, before, out):
        edge_planes(lambda region: cheb(region, damp, f, before, out), 1)
        for y in (OY - 1, OY, OY + CY - 1, OY + CY):
            cheb(Strip(y), damp, f, before, out)
        clear_outside(out)

    moving = swap(t0, 16)
    pl.semaphore_wait(tokens.at[0], 2)
    pass_on(tokens.at[1], 4)
    for cp in damps:
        cp.wait()
    rim.wait()

    @pl.when(me == NDEV - 1)
    def _():
        disp[:, NBLK:NBLK + 1, :] = jnp.zeros((3, 1, HZ), jnp.float32)

    shell_gather(3, disp, conn, dofs)
    blocks[3].wait()
    shell_product(3, stiff, dofs, force)
    shell_scatter(3, conn, force, own, over)
    edge = pltpu.make_async_remote_copy(
        src_ref=over.at[:, NBLK:NBLK + 1, :], dst_ref=over.at[:, 0:1, :], send_sem=ssem.at[33], recv_sem=rsem.at[33],
        device_id=(lax.div(after, NDOM), lax.rem(after, NDOM)), device_id_type=MESH)
    edge.start()
    shell_scatter(0, conn, force, own, over)
    grow_inner(t0, None, t1)
    for cp in moving:
        cp.wait()
    clear_outside(t0)
    pl.semaphore_wait(tokens.at[1], 2)
    pass_on(tokens.at[2], 8)
    grow_edge(t0, None, t1)
    all_planes(lambda region: cheb(region, damp, t1, t0, t2))

    moving = swap(t2, 24)
    owns = owner[...] == row_of(square)
    first = jnp.min(jnp.where(owns, lane_of(square), HZ), axis=1, keepdims=True)
    for s in (0, 1):
        table[:, s * HZ:(s + 1) * HZ] = jnp.where(
            owns & ((lane_of(square) == first) == (s == 0)), 1.0, 0.0).astype(jnp.bfloat16)
    words[...] = jnp.zeros(square, jnp.float32)
    words[W_WEIGHT:W_WEIGHT + 4, :] = weight[...]
    words[W_NODE:W_NODE + 1, :] = node[...].astype(jnp.float32)
    words[...] = jnp.transpose(words[...])
    z_all = column(cell_row[...]) & (2 * HZ - 1)
    lane = lane_of(square)
    hit0, hit1 = lane == z_all, lane + HZ == z_all
    hit = hit0 | hit1
    normals = [column(normal[c:c + 1, :]) for c in range(3)]

    def place(word, values):
        words[...] += jnp.where(lane == word, total_of(values), 0.0)

    def basis_words(j, f):
        sample(cells, f, mid0, mid1, dx, dy)
        a, b = mid0[...], mid1[...]
        value = jnp.where(hit0, a, 0.0) + jnp.where(hit1, b, 0.0)
        slope = (jnp.where(lane == z_all + 1, a, 0.0) + jnp.where(lane + HZ == z_all + 1, b, 0.0)
                 - jnp.where(lane == z_all - 1, a, 0.0) - jnp.where(lane + HZ == z_all - 1, b, 0.0))
        slopes = (jnp.where(hit, dx[...], 0.0), jnp.where(hit, dy[...], 0.0), slope)
        for c in range(3):
            place(W_BASIS + 3 * (j + 1) + c, -value * normals[c] - (0.5 * WALL_FRICTION) * slopes[c])

    sample_centre(cells, [pred.at[SLOT[c]] for c in range(3)], [mid0, mid1, dx])
    for c, ref in enumerate((mid0, mid1, dx)):
        place(W_BASIS + c, jnp.where(hit, WALL_FRICTION * ref[...], 0.0))
    basis_words(0, t0)
    basis_words(1, t1)
    grow_inner(t2, t1, t3)
    for cp in moving:
        cp.wait()
    clear_outside(t2)
    basis_words(2, t2)
    grow_edge(t2, t1, t3)

    def dots(x, acc):
        acc = list(acc)
        for k in range(2):
            region = Plane(x, OY + 16 * k, 16)
            ts = [region.get(t) for t in (t0, t1, t2, t3)]
            ts.append(cheb(region, damp, t3, t2, None))
            for n, (i, j) in enumerate(PAIRS):
                for h in (0, 1):
                    prod = ts[i][h] * ts[j][h]
                    acc[n] = acc[n] + (prod[0:8] + prod[8:16])
        return tuple(acc)

    acc = lax.fori_loop(OX, OX + CX, dots, tuple(jnp.zeros((8, HZ), jnp.float32) for _ in PAIRS))
    basis_words(3, t3)
    lane1 = lane_of((1, HZ))
    row = jnp.zeros((1, HZ), jnp.float32)
    for n in range(len(PAIRS)):
        row = row + jnp.where(lane1 == n, total_of(jnp.sum(acc[n], axis=0, keepdims=True)), 0.0)
    payload = words[...]
    both = jnp.concatenate([payload, pltpu.roll(payload, W_NEXT, 1)], axis=0)
    rows_out[...] = pick(table[...], both) + row
    pl.semaphore_wait(tokens.at[2], 2)
    mine = exchange_start(rows_out, rows_in, lsem.at[8], asem.at[0], asem.at[1])
    shell_scatter(1, conn, force, own, over)
    shell_scatter(2, conn, force, own, over)
    edge.wait()

    @pl.when(me == 0)
    def _():
        over[:, 0:1, :] = jnp.zeros((3, 1, HZ), jnp.float32)

    exchange_wait(mine, rows_out, rows_in, asem.at[0], asem.at[1])
    got = rows_in[...]
    total = jnp.sum(got, axis=0, keepdims=True)
    gram = {}
    for n, key in enumerate(PAIRS):
        gram[key] = jnp.broadcast_to(total_of(jnp.where(lane1 == n, total, 0.0)), (1, HZ))
    coef, worst = iterate(lambda i, j: gram[(i, j)])
    flag_ref[0, 0] = jnp.where(worst > GUARD, 1, 0).astype(jnp.int32)[0, 0]

    words[...] = jnp.transpose(got)
    lefts, lefts2, rights, rights2 = [], [], [], []
    for s in (0, 1):
        at = W_BASIS + s * W_NEXT
        traction = words[at:at + 3, :]
        for j in range(4):
            traction = traction + coef[j] * words[at + 3 * (j + 1):at + 3 * (j + 1) + 3, :]
        where = words[W_NODE + s * W_NEXT:W_NODE + s * W_NEXT + 1, :].astype(jnp.int32)
        high, low = where // HZ, where % HZ
        block = row_of((NBLK, HZ))
        lefts.append(jnp.concatenate([jnp.where(block == high, traction[c:c + 1], 0.0) for c in range(3)], axis=0))
        lefts2.append(jnp.concatenate([jnp.where(block == high + 1, traction[c:c + 1], 0.0) for c in range(3)], axis=0))
        right = right2 = jnp.zeros(square, jnp.float32)
        for j in range(RBFW):
            w = words[W_WEIGHT + s * W_NEXT + j:W_WEIGHT + s * W_NEXT + j + 1, :]
            right = jnp.where(row_of(square) == low + j, w, right)
            right2 = jnp.where(row_of(square) + HZ == low + j, w, right2)
        rights.append(right)
        rights2.append(right2)
    applied = lax.dot_general(
        jnp.concatenate(lefts + lefts2, axis=1), jnp.concatenate(rights + rights2, axis=1),
        (((1,), (1,)), ((), ())), precision=lax.Precision.HIGHEST, preferred_element_type=jnp.float32)
    for c in range(3):
        net = own[c] + over[c, 0:NBLK, :]
        moved = mass[...] * (applied[c * NBLK:(c + 1) * NBLK] - net)
        nodal[c, 0:NBLK, :] = moved
        nodal[c, NBLK:NBLK + 8, :] = jnp.zeros((8, HZ), jnp.float32)
        force[c] = disp[c, 0:NBLK, :] + SHELL_STEP * moved
    near = jnp.concatenate([nodal[c, 0:NBLK, :] for c in range(3)] + [nodal[c, 1:NBLK + 1, :] for c in range(3)], axis=1)
    stack = jnp.concatenate(thirds(near), axis=0)
    result = jnp.zeros(square, jnp.float32)
    for s in (0, 1):
        where = got[:, W_NODE + s * W_NEXT:W_NODE + s * W_NEXT + 1].astype(jnp.int32)
        high, low = where // HZ, where % HZ
        block = lax.rem(lane_of((HZ, 3 * NBLK)), NBLK)
        chosen = jnp.where(block == high, 1.0, 0.0).astype(jnp.bfloat16)
        vals = jnp.dot(chosen, stack, preferred_element_type=jnp.float32)
        here = there = jnp.zeros(square, jnp.float32)
        for j in range(RBFW):
            w = got[:, W_WEIGHT + s * W_NEXT + j:W_WEIGHT + s * W_NEXT + j + 1]
            here = jnp.where(lane == low + j, w, here)
            there = jnp.where(lane + HZ == low + j, w, there)
        for c in range(3):
            v = total_of(vals[:, c * HZ:(c + 1) * HZ] * here + vals[:, (3 + c) * HZ:(4 + c) * HZ] * there)
            result = jnp.where(lane == 3 * s + c, v, result)
    back_out[...] = result
    mine = exchange_start(back_out, back_in, lsem.at[8], asem.at[2], asem.at[3])

    def combine(region):
        res = None
        for c, t in zip(coef, (t0, t1, t2, t3)):
            vals = [c * v for v in region.get(t)]
            res = vals if res is None else each(lambda a, b: a + b, res, vals)
        region.put(press, res)

    all_planes(combine, OX - 1, OX + CX + 1)
    for y in (OY - 1, OY + CY):
        combine(Strip(y))

    def correct(region):
        _, sides = pairs_of(region, press)
        for c in range(3):
            prior = region.get(pred.at[SLOT[c]])
            new = each(lambda v, a, b: v - 0.5 * (a - b), prior, sides[c][0], sides[c][1])
            for h in (0, 1):
                nvel[c, region.x - OX, h, region.y - OY:region.y - OY + region.n, :] = new[h]

    all_planes(correct)
    stores = []
    for h in (0, 1):
        z = slice(h * HZ, (h + 1) * HZ)
        stores.append(pltpu.make_async_copy(nvel.at[:, :, h], nv_hbm.at[:, :, :, z], lsem.at[2 * h]))
        stores.append(pltpu.make_async_copy(
            press.at[OX:OX + CX, h, OY:OY + CY, :], p_hbm.at[:, :, z], lsem.at[2 * h + 1]))
    for cp in stores:
        cp.start()
    for b in range(NBLK):
        disp_out[:, b * HZ:(b + 1) * HZ] = force.reshape(12 * NBLK, HZ)[pl.ds(b, 3, stride=NBLK), :]
    exchange_wait(mine, back_out, back_in, asem.at[2], asem.at[3])
    answers = jnp.transpose(back_in[...])[0:8]
    answers = jnp.concatenate(thirds(answers), axis=0)
    found = [jnp.dot(answers, table[:, s * HZ:(s + 1) * HZ], preferred_element_type=jnp.float32) for s in (0, 1)]
    found = [f[0:8] + f[8:16] + f[16:24] for f in found]
    iface_out[...] = found[0][0:3] + found[1][3:6]
    for cp in stores:
        cp.wait()


def fused(velocity, damping, displacement, stiffness, connectivity, inv_mass, iface_cell, iface_owner, iface_node,
          rbf_weight, normals):
    field = (PX, 2, PY, HZ)
    f32, i32 = jnp.float32, jnp.int32
    anywhere = pl.BlockSpec(memory_space=pl.ANY)
    vmem = pl.BlockSpec(memory_space=pltpu.VMEM)
    smem = pl.BlockSpec(memory_space=pltpu.SMEM)
    square = pltpu.VMEM((HZ, HZ), f32)
    outs = pl.pallas_call(
        step_kernel,
        out_shape=(
            jax.ShapeDtypeStruct(velocity.shape, f32),
            jax.ShapeDtypeStruct(damping.shape, f32),
            jax.ShapeDtypeStruct(displacement.shape, f32),
            jax.ShapeDtypeStruct(normals.shape, f32),
            jax.ShapeDtypeStruct((1, 1), i32),
        ),
        in_specs=[anywhere] * 3 + [vmem] * 3 + [smem] + [vmem] * 5,
        out_specs=(anywhere, anywhere, vmem, vmem, smem),
        scratch_shapes=[
            pltpu.VMEM((3,) + field, f32),
            pltpu.VMEM(field, f32),
            pltpu.VMEM((3,) + field, f32),
            pltpu.VMEM(field, f32),
            pltpu.VMEM(field, f32),
            pltpu.VMEM(field, f32),
            pltpu.VMEM(field, f32),
            pltpu.VMEM(field, f32),
            pltpu.VMEM((3, CX, 2, CY, HZ), f32),
            pltpu.VMEM((12, 12, NBLK * HZ), f32),
            pltpu.VMEM((3, 40, HZ), f32),
            pltpu.VMEM((4, NBLK, HZ), i32),
            pltpu.VMEM((NBLK * 16, HZ), f32),
            pltpu.VMEM((12, NBLK, HZ), f32),
            pltpu.VMEM((3, NBLK, HZ), f32),
            pltpu.VMEM((3, 40, HZ), f32),
            square, square, square, square, square,
            pltpu.VMEM((HZ, 2 * HZ), jnp.bfloat16),
            pltpu.VMEM((3, 40, HZ), f32),
            square, square, square, square,
            pltpu.SemaphoreType.DMA((9,)),
            pltpu.SemaphoreType.DMA((4,)),
            pltpu.SemaphoreType.DMA((34,)),
            pltpu.SemaphoreType.DMA((34,)),
            pltpu.SemaphoreType.DMA((4,)),
            pltpu.SemaphoreType.REGULAR((3,)),
        ],
        compiler_params=pltpu.CompilerParams(
            collective_id=0, has_side_effects=True, vmem_limit_bytes=60 << 20),
        name="step",
    )(
        velocity, damping, stiffness, displacement, connectivity, inv_mass.reshape(NBLK, HZ), iface_cell,
        iface_cell.reshape(1, NPTS), iface_owner.reshape(1, NPTS), iface_node.reshape(1, NPTS), rbf_weight, normals,
    )
    return outs


ITERS = 4
VISCOSITY = 1.0
GUARD = 4e-4
UNIT_STEPS = ((1, 0, 0), (0, 1, 0), (0, 0, 1))


def with_halo(block, sides, width):
    for axis, dim in sides:
        count = lax.axis_size(axis)
        forward = [(i, i + 1) for i in range(count - 1)]
        backward = [(target, source) for source, target in forward]
        low = lax.ppermute(
            lax.slice_in_dim(block, block.shape[dim] - width, None, axis=dim), axis, forward
        )
        high = lax.ppermute(lax.slice_in_dim(block, 0, width, axis=dim), axis, backward)
        block = jnp.concatenate([low, block, high], axis=dim)
    return block


def from_behind(value, axis, steps):
    count = lax.axis_size(axis)
    leading, last = (max(0, -steps), min(count, count - steps))
    return lax.ppermute(value, axis, [(source, source + steps) for source in range(leading, last)])


def window_at(padded, offsets):
    size_x = padded.shape[-3] - 2
    size_y = padded.shape[-2] - 2
    size_z = padded.shape[-1] - 2
    return padded[
        ...,
        1 + offsets[0] : 1 + offsets[0] + size_x,
        1 + offsets[1] : 1 + offsets[1] + size_y,
        1 + offsets[2] : 1 + offsets[2] + size_z,
    ]


def backward(unit_step):
    return tuple((-value for value in unit_step))


def pad_depth(source):
    spec = [(0, 0)] * (source.ndim - 1) + [(1, 1)]
    return jnp.pad(source, spec)


def predictor(padded):
    centre = window_at(padded, (0, 0, 0))
    laplace = -6.0 * centre
    advect = jnp.zeros_like(centre)
    for axis_num, unit_step in enumerate(UNIT_STEPS):
        forward = window_at(padded, unit_step)
        behind_cells = window_at(padded, backward(unit_step))
        laplace = laplace + forward + behind_cells
        advect = advect + centre[axis_num : axis_num + 1] * (0.5 * (forward - behind_cells))
    return centre + TIME_STEP * (VISCOSITY * laplace - advect)


def divergence(padded):
    summed = jnp.zeros(window_at(padded[0], (0, 0, 0)).shape, jnp.float32)
    for axis_num, unit_step in enumerate(UNIT_STEPS):
        component = padded[axis_num]
        summed = summed + 0.5 * (
            window_at(component, unit_step) - window_at(component, backward(unit_step))
        )
    return -summed


def padded_cells(source):
    extended = with_halo(source, (("grp", 0), ("dom", 1)), 1)
    return pad_depth(extended)


def operate(source, damping):
    padded = padded_cells(source)
    centre = window_at(padded, (0, 0, 0))
    beside = jnp.zeros_like(centre)
    for unit_step in UNIT_STEPS:
        beside = beside + window_at(padded, unit_step) + window_at(padded, backward(unit_step))
    return (6.0 + damping) * centre - beside


def squares(residual):
    return lax.psum(jnp.sum(residual * residual), ("grp", "dom"))


def plain(
    velocity,
    damping,
    displacement,
    stiffness,
    connectivity,
    inv_mass,
    iface_cell,
    iface_owner,
    iface_node,
    rbf_weight,
    normals,
):
    shell_nodes = displacement.shape[1]
    rim_values = from_behind(displacement[:, :RIM], ("grp", "dom"), -1)
    extended_disp = jnp.concatenate([displacement, rim_values], axis=1)
    element_count = connectivity.shape[1]
    corner_values = extended_disp[:, connectivity]
    element_dofs = jnp.transpose(corner_values, (1, 0, 2)).reshape(12, element_count)
    element_force = jnp.sum(stiffness * element_dofs[None], axis=1).reshape(4, 3, element_count)
    node_force = jnp.zeros((3, shell_nodes + RIM), jnp.float32)
    for corner in range(4):
        node_force = node_force.at[:, connectivity[corner]].add(element_force[corner])
    rim_force = from_behind(node_force[:, shell_nodes:], ("grp", "dom"), 1)
    stiff_force = node_force[:, :shell_nodes] + jnp.pad(rim_force, ((0, 0), (0, shell_nodes - RIM)))
    extended = with_halo(velocity, (("grp", 1), ("dom", 2)), 1)
    predicted = predictor(pad_depth(extended))
    star_wide = with_halo(predicted, (("grp", 1), ("dom", 2)), 1)
    star_padded = pad_depth(star_wide)
    right_side = divergence(star_padded)
    pressure = jnp.zeros_like(right_side)
    residual = right_side
    direction = right_side
    norm_now = squares(residual)
    for sweep in range(ITERS):
        mapped = operate(direction, damping)
        step_size = norm_now / lax.psum(jnp.sum(direction * mapped), ("grp", "dom"))
        pressure = pressure + step_size * direction
        residual = residual - step_size * mapped
        norm_next = squares(residual)
        direction = residual + norm_next / norm_now * direction
        norm_now = norm_next
    pressure_wide = padded_cells(pressure)
    new_velocity = predicted - jnp.stack(
        [
            0.5
            * (window_at(pressure_wide, unit_step) - window_at(pressure_wide, backward(unit_step)))
            for unit_step in UNIT_STEPS
        ]
    )
    pressure_at = pressure.reshape(-1)[iface_cell]
    velocity_at = new_velocity.reshape(3, -1)[:, iface_cell]
    traction = -pressure_at[None] * normals + WALL_FRICTION * velocity_at
    owner_dev = iface_owner[:, 0]
    point_count = owner_dev.shape[0]
    devices = lax.axis_size("grp") * lax.axis_size("dom")
    owner_cap = max(2, 2 * point_count // devices)
    order_index = lax.iota(jnp.int32, point_count)
    earlier = (owner_dev[None, :] == owner_dev[:, None]) & (
        order_index[None, :] < order_index[:, None]
    )
    slot_rank = jnp.sum(earlier.astype(jnp.int32), axis=1)
    slot_index = owner_dev * owner_cap + slot_rank
    slot_count = devices * owner_cap
    payload = jnp.concatenate([traction, rbf_weight, iface_node.astype(jnp.float32)[None]], axis=0)
    outgoing = jnp.zeros((payload.shape[0], slot_count), jnp.float32).at[:, slot_index].set(payload)
    received = lax.all_to_all(outgoing, ("grp", "dom"), split_axis=1, concat_axis=1, tiled=True)
    slot_traction = received[:3]
    slot_weight = received[3 : 3 + RBFW]
    slot_node = received[3 + RBFW].astype(jnp.int32)
    applied = jnp.zeros((3, shell_nodes), jnp.float32)
    for offset in range(RBFW):
        applied = applied.at[:, slot_node + offset].add(slot_weight[offset][None] * slot_traction)
    node_velocity = inv_mass[None] * (applied - stiff_force)
    new_displacement = displacement + SHELL_STEP * node_velocity
    slot_velocity = jnp.zeros((3, slot_count), jnp.float32)
    for offset in range(RBFW):
        slot_velocity = (
            slot_velocity + slot_weight[offset][None] * node_velocity[:, slot_node + offset]
        )
    returned_vals = lax.all_to_all(
        slot_velocity, ("grp", "dom"), split_axis=1, concat_axis=1, tiled=True
    )
    iface_velocity = returned_vals[:, slot_index]
    return (new_velocity, pressure, new_displacement, iface_velocity)


def relay_kernel(*refs):
    count = (len(refs) - 2) // 3
    ins, outs, held = refs[:count], refs[count:2 * count], refs[2 * count:3 * count]
    come, go = refs[-2:]
    pieces = []
    for a, b, c in zip(ins, outs, held):
        if len(a.shape) > 2:
            pieces += [(a.at[k], b.at[k], c.at[k]) for k in range(a.shape[0])]
        else:
            pieces.append((a, b, c))
    arrive = [pltpu.make_async_copy(a, c, come.at[n]) for n, (a, b, c) in enumerate(pieces)]
    leave = [pltpu.make_async_copy(c, b, go.at[n]) for n, (a, b, c) in enumerate(pieces)]
    for cp in arrive:
        cp.start()
    for x, y in zip(arrive, leave):
        x.wait()
        y.start()
    for y in leave:
        y.wait()


def relay(new_velocity, pressure, new_displacement, iface_velocity):
    arrays = (new_velocity, pressure.reshape(4, CX // 4, CY, 2 * HZ), new_displacement, iface_velocity)
    anywhere = pl.BlockSpec(memory_space=pl.ANY)
    count = 3 + 4 + 2
    outs = pl.pallas_call(
        relay_kernel,
        out_shape=tuple(jax.ShapeDtypeStruct(a.shape, a.dtype) for a in arrays),
        in_specs=[anywhere] * len(arrays),
        out_specs=(anywhere,) * len(arrays),
        scratch_shapes=[pltpu.VMEM(a.shape, a.dtype) for a in arrays]
        + [pltpu.SemaphoreType.DMA((count,)), pltpu.SemaphoreType.DMA((count,))],
        compiler_params=pltpu.CompilerParams(vmem_limit_bytes=60 << 20),
        name="relay",
    )(*arrays)
    return outs[0], outs[1].reshape(pressure.shape), outs[2], outs[3]


def local(*args):
    *outs, sound = fused(*args)
    return lax.cond(sound.reshape(()) > 0, lambda: relay(*outs), lambda: plain(*args))


def solution(mesh):
    return jax.shard_map(
        local,
        mesh=mesh,
        in_specs=(
            P(None, "grp", "dom", None),
            P("grp", "dom", None),
            P(None, ("grp", "dom")),
            P(None, None, ("grp", "dom")),
            P(None, ("grp", "dom")),
            P(("grp", "dom")),
            P(("grp", "dom")),
            P(("grp", "dom"), None),
            P(("grp", "dom")),
            P(None, ("grp", "dom")),
            P(None, ("grp", "dom")),
        ),
        out_specs=(
            P(None, "grp", "dom", None),
            P("grp", "dom", None),
            P(None, ("grp", "dom")),
            P(None, ("grp", "dom")),
        ),
        check_vma=False,
    )
```

```python
import jax
import jax.numpy as jnp
from jax import lax
from jax.experimental import pallas as pl
from jax.experimental.pallas import tpu as pltpu
from jax.sharding import PartitionSpec as P

MESH = pl.DeviceIdType.MESH
NGRP, NDOM = 4, 32
NDEV = NGRP * NDOM
CX, CY, HZ = 16, 32, 128
PX, PY, OX, OY = CX + 4, CY + 16, 2, 8
SLOT = {0: 0, 2: 1, 1: 2}
SHIFT, HALF = 6.26, 6.24
TIME_STEP = 0.1
WALL_FRICTION = 0.5
SHELL_STEP = 0.5
RIM, RBFW, NBLK, NPTS = 64, 4, 32, 128
W_BASIS, W_WEIGHT, W_NODE, W_NEXT = 32, 47, 51, 32
EARLY, LATE = [(0, 0), (0, 1), (1, 1), (1, 2), (2, 2)], [(2, 3), (3, 3), (3, 4)]


def rows_of(ref):
    return ref.reshape(PX * 2 * PY, HZ)


class Plane:
    def __init__(self, x, y, n):
        self.x, self.y, self.n = x, y, n

    def get(self, f, dx=0, dy=0):
        return [f[self.x + dx, h, self.y + dy:self.y + dy + self.n, :] for h in (0, 1)]

    def put(self, f, halves):
        for h in (0, 1):
            f[self.x, h, self.y:self.y + self.n, :] = halves[h]


class Inner:
    def __init__(self, x, k):
        self.x, self.k, self.n = x, k, CY // 2
        self.y = OY + k * self.n

    def get(self, f, dx=0, dy=0):
        if dy == (1 if self.k else -1):
            own = [f[self.x + dx, h, self.y:self.y + self.n, :] for h in (0, 1)]
            return [pltpu.roll(v, 1 if dy < 0 else self.n - 1, 0) for v in own]
        return [f[self.x + dx, h, self.y + dy:self.y + dy + self.n, :] for h in (0, 1)]

    def put(self, f, halves):
        for h in (0, 1):
            f[self.x, h, self.y:self.y + self.n, :] = halves[h]


class Strip:
    def __init__(self, y):
        self.y = y

    def at(self, dx, dy, h):
        return pl.ds(((OX + dx) * 2 + h) * PY + self.y + dy, CX, stride=2 * PY)

    def get(self, f, dx=0, dy=0):
        flat = rows_of(f)
        return [flat[self.at(dx, dy, h), :] for h in (0, 1)]

    def put(self, f, halves):
        flat = rows_of(f)
        for h in (0, 1):
            flat[self.at(0, 0, h), :] = halves[h]


def lanes(a):
    return lax.broadcasted_iota(jnp.int32, a.shape, 1)


def up(a):
    r0, r1 = (pltpu.roll(v, HZ - 1, 1) for v in a)
    edge = lanes(a[0]) == HZ - 1
    return [jnp.where(edge, r1, r0), jnp.where(edge, 0.0, r1)]


def down(a):
    r0, r1 = (pltpu.roll(v, 1, 1) for v in a)
    edge = lanes(a[0]) == 0
    return [jnp.where(edge, 0.0, r0), jnp.where(edge, r0, r1)]


def each(fn, *lists):
    return [fn(*vals) for vals in zip(*lists)]


def pairs_of(region, f):
    centre = region.get(f)
    return centre, (
        (region.get(f, 1, 0), region.get(f, -1, 0)),
        (region.get(f, 0, 1), region.get(f, 0, -1)),
        (up(centre), down(centre)),
    )


def predict(region, vel, c, out):
    others = [region.get(vel.at[SLOT[d]]) for d in range(3)]
    centre, sides = pairs_of(region, vel.at[SLOT[c]])
    res = []
    for h in (0, 1):
        lap = -6.0 * centre[h]
        adv = None
        for d in range(3):
            a, b = sides[d][0][h], sides[d][1][h]
            lap = lap + a + b
            term = others[d][h] * (0.5 * (a - b))
            adv = term if adv is None else adv + term
        res.append(centre[h] + TIME_STEP * (lap - adv))
    region.put(out.at[SLOT[c]], res)


def apply(region, damp, f):
    centre, sides = pairs_of(region, f)
    dv = region.get(damp)
    res = []
    for h in (0, 1):
        s = None
        for a, b in sides:
            s = a[h] + b[h] if s is None else s + a[h] + b[h]
        res.append(((dv[h] + (6.0 - SHIFT)) * centre[h] - s) * (1.0 / HALF))
    return res


def cheb(region, damp, f, before, out):
    res = apply(region, damp, f)
    if before is not None:
        res = each(lambda a, b: 2.0 * a - b, res, region.get(before))
    if out is not None:
        region.put(out, res)
    return res


def all_planes(fn, lo=OX, hi=OX + CX, parts=2, unroll=2):
    def body(x, carry):
        for k in range(parts):
            fn(Plane(x, OY + k * (CY // parts), CY // parts))
        return carry

    lax.fori_loop(lo, hi, body, 0, unroll=unroll)


def inner_planes(fn):
    def body(x, carry):
        for k in range(2):
            fn(Inner(x, k))
        return carry

    lax.fori_loop(OX + 1, OX + CX - 1, body, 0, unroll=2)


def planes_at(fn, xs):
    for x in xs:
        for k in range(2):
            fn(Plane(x, OY + k * (CY // 2), CY // 2))


def position():
    return lax.axis_index("grp"), lax.axis_index("dom")


def clear_outside(f):
    g, d = position()

    @pl.when(g == 0)
    def _():
        f[0:OX] = jnp.zeros((OX, 2, PY, HZ), jnp.float32)

    @pl.when(g == NGRP - 1)
    def _():
        f[OX + CX:PX] = jnp.zeros((PX - OX - CX, 2, PY, HZ), jnp.float32)

    @pl.when(d == 0)
    def _():
        f[:, :, 0:OY, :] = jnp.zeros((PX, 2, OY, HZ), jnp.float32)

    @pl.when(d == NDOM - 1)
    def _():
        f[:, :, OY + CY:PY, :] = jnp.zeros((PX, 2, PY - OY - CY, HZ), jnp.float32)


def clear_faces(f):
    g, d = position()
    xs, ys = slice(OX, OX + CX), slice(OY, OY + CY)

    @pl.when(g == 0)
    def _():
        f[0:OX, :, ys, :] = jnp.zeros((OX, 2, CY, HZ), jnp.float32)

    @pl.when(g == NGRP - 1)
    def _():
        f[OX + CX:PX, :, ys, :] = jnp.zeros((PX - OX - CX, 2, CY, HZ), jnp.float32)

    @pl.when(d == 0)
    def _():
        f[xs, :, 0:OY, :] = jnp.zeros((CX, 2, OY, HZ), jnp.float32)

    @pl.when(d == NDOM - 1)
    def _():
        f[xs, :, OY + CY:PY, :] = jnp.zeros((CX, 2, PY - OY - CY, HZ), jnp.float32)


def neighbour(dg, dd):
    g, d = position()
    return lax.rem(g + dg + NGRP, NGRP), lax.rem(d + dd + NDOM, NDOM)


def sides_of(ref, lead, width):
    lo, hi = OX, OX + CX
    a, b = OY, OY + CY
    ys = slice(a, b)
    xs = slice(lo, hi)
    w = width
    return [
        ((1, 0), lead + (slice(hi - w, hi), slice(None), ys), lead + (slice(lo - w, lo), slice(None), ys)),
        ((-1, 0), lead + (slice(lo, lo + w), slice(None), ys), lead + (slice(hi, hi + w), slice(None), ys)),
        ((0, 1), lead + (xs, slice(None), slice(b - w, b)), lead + (xs, slice(None), slice(a - w, a))),
        ((0, -1), lead + (xs, slice(None), slice(a, a + w)), lead + (xs, slice(None), slice(b, b + w))),
    ]


def corners_of(ref, lead):
    out = []
    for dg in (1, -1):
        for dd in (1, -1):
            sx = OX + CX - 1 if dg == 1 else OX
            tx = OX - 1 if dg == 1 else OX + CX
            sy = OY + CY - 1 if dd == 1 else OY
            ty = OY - 1 if dd == 1 else OY + CY
            out.append((
                (dg, dd),
                lead + (slice(sx, sx + 1), slice(None), slice(sy, sy + 1)),
                lead + (slice(tx, tx + 1), slice(None), slice(ty, ty + 1)),
            ))
    return out


def start_all(ref, items, send, recv, base):
    copies = []
    for k, (way, src, dst) in enumerate(items):
        cp = pltpu.make_async_remote_copy(
            src_ref=ref.at[src], dst_ref=ref.at[dst],
            send_sem=send.at[base + k], recv_sem=recv.at[base + k],
            device_id=neighbour(*way), device_id_type=MESH,
        )
        cp.start()
        copies.append(cp)
    return copies


def everyone(fn):
    g, d = position()
    for dg in (2, 1, 3, 0):
        tg = lax.rem(g + dg, NGRP)

        def body(i, carry):
            fn(tg, lax.rem(d + i, NDOM))
            return carry

        if dg:
            lax.fori_loop(8, 8 + NDOM, body, 0, unroll=16)
        else:
            lax.fori_loop(8, NDOM, body, 0, unroll=12)
            lax.fori_loop(1, 8, body, 0, unroll=7)


def greet_near():
    barrier = pltpu.get_barrier_semaphore()
    for dg in (-1, 0, 1):
        for dd in (-1, 0, 1):
            if dg or dd:
                pl.semaphore_signal(barrier, inc=1, device_id=neighbour(dg, dd), device_id_type=MESH)
    return barrier


def pass_on(token, reach):
    for dd in (reach, -reach):
        pl.semaphore_signal(token, inc=1, device_id=neighbour(0, dd), device_id_type=MESH)


def exchange_start(out_ref, in_ref, own, send, recv):
    g, d = position()
    me = g * NDOM + d
    mine = pltpu.make_async_copy(out_ref.at[pl.ds(me, 1)], in_ref.at[pl.ds(me, 1)], own)
    mine.start()
    everyone(lambda tg, td: pltpu.make_async_remote_copy(
        src_ref=out_ref.at[pl.ds(tg * NDOM + td, 1)], dst_ref=in_ref.at[pl.ds(me, 1)],
        send_sem=send, recv_sem=recv, device_id=(tg, td), device_id_type=MESH,
    ).start())
    return mine


def exchange_wait(mine, out_ref, in_ref, send, recv):
    rest = pl.ds(0, NDEV - 1)
    mine.wait()
    pltpu.make_async_copy(out_ref.at[rest], in_ref.at[rest], recv).wait()
    pltpu.make_async_copy(out_ref.at[rest], in_ref.at[rest], send).wait()


def iterate(gram):
    def times(v):
        out = [None] * 5

        def put(i, val):
            out[i] = val if out[i] is None else out[i] + val

        for j, val in enumerate(v):
            if val is None:
                continue
            put(j, SHIFT * val)
            if j == 0:
                put(1, HALF * val)
            else:
                put(j + 1, (0.5 * HALF) * val)
                put(j - 1, (0.5 * HALF) * val)
        return out

    worst = None

    def form(a, b):
        nonlocal worst
        total = size = None
        for i in range(5):
            for j in range(5):
                if a[i] is None or b[j] is None:
                    continue
                term = a[i] * b[j] * gram(min(i, j), max(i, j))
                total = term if total is None else total + term
                mag = jnp.abs(term)
                size = mag if size is None else size + mag
        ratio = total / size
        worst = ratio if worst is None else jnp.minimum(worst, ratio)
        return total

    def axpy(a, s, b):
        return [x if y is None else (s * y if x is None else x + s * y) for x, y in zip(a, b)]

    one = jnp.ones_like(gram(0, 0))
    r = [one, None, None, None, None]
    d = list(r)
    p = [None] * 5
    rr = gram(0, 0)
    for k in range(4):
        m = times(d)
        step = rr / form(d, m)
        p = axpy(p, step, d)
        if k == 3:
            break
        r = axpy(r, -step, m)
        new = form(r, r)
        d = axpy(r, new / rr, d)
        rr = new
    return p[:4], worst


def lane_of(shape):
    return lax.broadcasted_iota(jnp.int32, shape, 1)


def row_of(shape):
    return lax.broadcasted_iota(jnp.int32, shape, 0)


def thirds(x):
    a = x.astype(jnp.bfloat16)
    rest = x - a.astype(jnp.float32)
    b = rest.astype(jnp.bfloat16)
    return a, b, (rest - b.astype(jnp.float32)).astype(jnp.bfloat16)


def pick(onehot, x):
    width = x.shape[1]
    wide = jnp.concatenate(thirds(x), axis=1)
    out = jnp.dot(onehot, wide, preferred_element_type=jnp.float32)
    return out[:, :width] + out[:, width:2 * width] + out[:, 2 * width:]


def spread(src, dst, count, stride):
    for b in range(NBLK):
        dst[pl.ds(b, count, stride=stride), :] = src[:, b * HZ:(b + 1) * HZ]


def shell_gather(q, disp, conn, dofs):
    sub = row_of((8, HZ))
    for a in range(4):
        rel = conn[a, 8 * q:8 * q + 8, :] - HZ * (8 * q + sub)
        near = rel < HZ
        low = jnp.where(near, rel, rel - HZ)
        for c in range(3):
            here = jnp.take_along_axis(disp[c, 8 * q:8 * q + 8, :], low, axis=1, mode="promise_in_bounds")
            there = jnp.take_along_axis(disp[c, 8 * q + 1:8 * q + 9, :], low, axis=1, mode="promise_in_bounds")
            dofs[pl.ds(8 * q * 16 + 3 * a + c, 8, stride=16), :] = jnp.where(near, here, there)


def shell_product(q, stiff, dofs, force):
    sub = row_of((8, HZ))

    def body(i, carry):
        parts = []
        for b in range(8 * q, 8 * q + 8):
            z = slice(b * HZ, (b + 1) * HZ)
            top = stiff[i, 0:8, z] * dofs[b * 16:b * 16 + 8, :]
            low = stiff[i, 8:12, z] * dofs[b * 16 + 8:b * 16 + 12, :]
            parts.append(top + jnp.concatenate([low, jnp.zeros((4, HZ), jnp.float32)], axis=0))
        first = sub < 4
        parts = [
            jnp.where(first, parts[k], parts[k + 4]) + pltpu.roll(jnp.where(first, parts[k + 4], parts[k]), 4, 0)
            for k in range(4)
        ]
        for bit in (2, 1):
            keep = (sub & bit) == 0
            parts = [
                jnp.where(keep, parts[k] + pltpu.roll(parts[k], 8 - bit, 0),
                          parts[k + bit] + pltpu.roll(parts[k + bit], bit, 0))
                for k in range(bit)
            ]
        force[i, 8 * q:8 * q + 8, :] = parts[0]
        return carry

    lax.fori_loop(0, 12, body, 0)


def shell_scatter(q, conn, force, own, over):
    lane = lane_of((8, HZ))
    element = HZ * (8 * q + row_of((8, HZ))) + lane
    rel = [conn[a, 8 * q:8 * q + 8, :] - element for a in range(4)]
    vals = [[force[3 * a + c, 8 * q:8 * q + 8, :] for c in range(3)] for a in range(4)]

    def body(d, acc):
        hit = [r == d for r in rel]
        inside = lane >= d
        out = []
        for c in range(3):
            s = jnp.zeros((8, HZ), jnp.float32)
            for a in range(4):
                s = jnp.where(hit[a], vals[a][c], s)
            s = pltpu.roll(s, d, 1)
            out.append(acc[2 * c] + jnp.where(inside, s, 0.0))
            out.append(acc[2 * c + 1] + jnp.where(inside, 0.0, s))
        return tuple(out)

    acc = lax.fori_loop(0, RIM + 1, body, tuple(jnp.zeros((8, HZ), jnp.float32) for _ in range(6)), unroll=5)
    for c in range(3):
        own[c, 8 * q:8 * q + 8, :] = acc[2 * c]
        over[c, 8 * q + 1:8 * q + 9, :] = acc[2 * c + 1]


def sample(cells, f, mid0, mid1, dx, dy):
    def body(i, carry):
        for u in range(4):
            k = i * 4 + u
            cell = cells[k]
            x, y, h = (cell >> 13) + OX, ((cell >> 8) & (CY - 1)) + OY, (cell >> 7) & 1
            at = pl.ds(k, 1)
            mid0[at, :] = f[x, 0, pl.ds(y, 1), :]
            mid1[at, :] = f[x, 1, pl.ds(y, 1), :]
            dx[at, :] = f[x + 1, h, pl.ds(y, 1), :] - f[x - 1, h, pl.ds(y, 1), :]
            dy[at, :] = f[x, h, pl.ds(y + 1, 1), :] - f[x, h, pl.ds(y - 1, 1), :]
        return carry

    lax.fori_loop(0, NPTS // 4, body, 0)


def sample_centre(cells, fields, outs):
    def body(i, carry):
        for u in range(4):
            k = i * 4 + u
            cell = cells[k]
            x, y, h = (cell >> 13) + OX, ((cell >> 8) & (CY - 1)) + OY, (cell >> 7) & 1
            for f, o in zip(fields, outs):
                o[pl.ds(k, 1), :] = f[x, h, pl.ds(y, 1), :]
        return carry

    lax.fori_loop(0, NPTS // 4, body, 0)


def column(row):
    return jnp.transpose(jnp.broadcast_to(row, (HZ, HZ)))


def total_of(x):
    return jnp.sum(x, axis=1, keepdims=True)


def step_kernel(vel_hbm, damp_hbm, stiff_hbm, disp_hbm, conn_hbm, *rest):
    small_hbm, rest = rest[:7], rest[7:]
    small, rest = rest[-7:], rest[:-7]
    step_body(vel_hbm, damp_hbm, stiff_hbm, disp_hbm, conn_hbm, small_hbm, small, *rest)


def step_body(vel_hbm, damp_hbm, stiff_hbm, disp_hbm, conn_hbm, small_hbm, small,
                nv_hbm, p_hbm, disp_res, iface_res, flag_ref, disp_in, conn_in, disp_out, iface_out, msem,
                vel, damp, pred, t0, t1, t2, t3, press, nvel, stiff,
                disp, conn, dofs, force, own, over, mid0, mid1, dx, dy, words, table, nodal,
                rows_out, rows_in, back_out, back_in, lsem, ksem, ssem, rsem, asem, tokens):
    barrier = greet_near()
    g, d = position()
    me = g * NDOM + d
    loads = []
    for h in (0, 1):
        z = slice(h * HZ, (h + 1) * HZ)
        for c in range(3):
            loads.append(pltpu.make_async_copy(
                vel_hbm.at[c, :, :, z], vel.at[SLOT[c], OX:OX + CX, h, OY:OY + CY, :], lsem.at[len(loads)]))
        loads.append(pltpu.make_async_copy(
            damp_hbm.at[:, :, z], damp.at[OX:OX + CX, h, OY:OY + CY, :], lsem.at[len(loads)]))
    for q in range(4):
        z = slice(q * 8 * HZ, (q + 1) * 8 * HZ)
        loads.append(pltpu.make_async_copy(stiff_hbm.at[:, :, z], stiff.at[:, :, z], ksem.at[q]))
    minor = [pltpu.make_async_copy(a, b, msem.at[n])
             for n, (a, b) in enumerate(zip((disp_hbm, conn_hbm) + small_hbm, (disp_in, conn_in) + small))]
    for cp in loads[:8] + minor + loads[8:]:
        cp.start()
    blocks = loads[8:]
    mass, cells, cell_row, owner, node, weight, normal = small

    square = (HZ, HZ)
    for cp in loads[:8]:
        cp.wait()
    pl.semaphore_wait(barrier, 8)

    one = slice(None)
    f_x, f_y, f_z = SLOT[0], SLOT[1], SLOT[2]
    faces = corners_of(vel, (one,))
    wide_x, wide_y = sides_of(vel, (f_x,), 2)[:2], sides_of(vel, (f_y,), 2)[2:]
    thin_x, thin_y = sides_of(vel, (slice(1, 3),), 1)[:2], sides_of(vel, (slice(0, 2),), 1)[2:]
    copies = start_all(vel, faces + wide_x + wide_y + thin_x + thin_y, ssem, rsem, 0)
    damps = start_all(damp, sides_of(damp, (), 1), ssem, rsem, 12)
    minor[0].wait()
    spread(disp_in, disp.reshape(3 * 40, HZ), 3, 40)
    before, after = lax.rem(me + NDEV - 1, NDEV), lax.rem(me + 1, NDEV)
    rim = pltpu.make_async_remote_copy(
        src_ref=disp.at[:, 0:1, :], dst_ref=disp.at[:, NBLK:NBLK + 1, :], send_sem=ssem.at[32], recv_sem=rsem.at[32],
        device_id=(lax.div(before, NDOM), lax.rem(before, NDOM)), device_id_type=MESH)
    rim.start()
    minor[1].wait()
    spread(conn_in, conn.reshape(4 * NBLK, HZ), 4, NBLK)
    for q in range(3):
        shell_gather(q, disp, conn, dofs)
        blocks[q].wait()
        shell_product(q, stiff, dofs, force)

    def pred_main(region):
        for c in range(3):
            predict(region, vel, c, pred)

    inner_planes(pred_main)
    for cp in copies[4:]:
        cp.wait()
    for c in range(3):
        clear_faces(vel.at[c])
    planes_at(pred_main, (OX, OX + CX - 1))
    for y in (OY, OY + CY - 1):
        pred_main(Strip(y))
    for cp in copies[:4]:
        cp.wait()
    pass_on(tokens.at[0], 2)
    for c in (0, 1):
        clear_outside(vel.at[SLOT[c]])
    planes_at(lambda region: predict(region, vel, 0, pred), (OX - 1, OX + CX))
    for y in (OY - 1, OY + CY):
        predict(Strip(y), vel, 1, pred)
    clear_outside(pred.at[f_x])
    clear_outside(pred.at[f_y])

    def diverge(region):
        fx, fy, fz = pred.at[f_x], pred.at[f_y], region.get(pred.at[f_z])
        s = each(lambda a, b: 0.5 * (a - b), region.get(fx, 1, 0), region.get(fx, -1, 0))
        s = each(lambda s, a, b: s + 0.5 * (a - b), s, region.get(fy, 0, 1), region.get(fy, 0, -1))
        s = each(lambda s, a, b: -(s + 0.5 * (a - b)), s, up(fz), down(fz))
        region.put(t0, s)

    all_planes(diverge)

    def swap(f, base):
        return start_all(f, corners_of(f, ()) + sides_of(f, (), 2), ssem, rsem, base)

    def grow_inner(f, before, out):
        inner_planes(lambda region: cheb(region, damp, f, before, out))

    def grow_edge(moving, f, before, out):
        for cp in moving[4:]:
            cp.wait()
        clear_faces(f)
        grow = lambda region: cheb(region, damp, f, before, out)
        planes_at(grow, (OX, OX + CX - 1))
        for y in (OY, OY + CY - 1):
            grow(Strip(y))
        for cp in moving[:4]:
            cp.wait()
        clear_outside(f)
        planes_at(grow, (OX - 1, OX + CX))
        for y in (OY - 1, OY + CY):
            grow(Strip(y))
        clear_outside(out)

    moving = swap(t0, 16)
    pl.semaphore_wait(tokens.at[0], 2)
    pass_on(tokens.at[1], 4)
    for cp in damps:
        cp.wait()
    rim.wait()

    @pl.when(me == NDEV - 1)
    def _():
        disp[:, NBLK:NBLK + 1, :] = jnp.zeros((3, 1, HZ), jnp.float32)

    shell_gather(3, disp, conn, dofs)
    blocks[3].wait()
    shell_product(3, stiff, dofs, force)
    shell_scatter(3, conn, force, own, over)
    edge = pltpu.make_async_remote_copy(
        src_ref=over.at[:, NBLK:NBLK + 1, :], dst_ref=over.at[:, 0:1, :], send_sem=ssem.at[33], recv_sem=rsem.at[33],
        device_id=(lax.div(after, NDOM), lax.rem(after, NDOM)), device_id_type=MESH)
    edge.start()
    shell_scatter(0, conn, force, own, over)
    grow_inner(t0, None, t1)
    pl.semaphore_wait(tokens.at[1], 2)
    pass_on(tokens.at[2], 8)
    grow_edge(moving, t0, None, t1)
    all_planes(lambda region: cheb(region, damp, t1, t0, t2))

    moving = swap(t2, 24)
    for cp in minor[2:]:
        cp.wait()
    owns = owner[...] == row_of(square)
    first = jnp.min(jnp.where(owns, lane_of(square), HZ), axis=1, keepdims=True)
    for s in (0, 1):
        table[:, s * HZ:(s + 1) * HZ] = jnp.where(
            owns & ((lane_of(square) == first) == (s == 0)), 1.0, 0.0).astype(jnp.bfloat16)
    words[...] = jnp.zeros(square, jnp.float32)
    words[W_WEIGHT:W_WEIGHT + 4, :] = weight[...]
    words[W_NODE:W_NODE + 1, :] = node[...].astype(jnp.float32)
    words[...] = jnp.transpose(words[...])
    z_all = column(cell_row[...]) & (2 * HZ - 1)
    lane = lane_of(square)
    hit0, hit1 = lane == z_all, lane + HZ == z_all
    hit = hit0 | hit1
    normals = [column(normal[c:c + 1, :]) for c in range(3)]

    lane1 = lane_of((1, HZ))

    def gather_dots(pairs, fields):
        def body(x, acc):
            acc = list(acc)
            for k in range(2):
                ts = fields(Plane(x, OY + 16 * k, 16))
                for n, (i, j) in enumerate(pairs):
                    for h in (0, 1):
                        prod = ts[i][h] * ts[j][h]
                        acc[n] = acc[n] + (prod[0:8] + prod[8:16])
            return tuple(acc)

        acc = lax.fori_loop(OX, OX + CX, body, tuple(jnp.zeros((8, HZ), jnp.float32) for _ in pairs), unroll=2)
        return [total_of(jnp.sum(a, axis=0, keepdims=True)) for a in acc]

    def place(word, values):
        words[...] += jnp.where(lane == word, total_of(values), 0.0)

    def basis_words(j, f):
        sample(cells, f, mid0, mid1, dx, dy)
        a, b = mid0[...], mid1[...]
        value = jnp.where(hit0, a, 0.0) + jnp.where(hit1, b, 0.0)
        slope = (jnp.where(lane == z_all + 1, a, 0.0) + jnp.where(lane + HZ == z_all + 1, b, 0.0)
                 - jnp.where(lane == z_all - 1, a, 0.0) - jnp.where(lane + HZ == z_all - 1, b, 0.0))
        slopes = (jnp.where(hit, dx[...], 0.0), jnp.where(hit, dy[...], 0.0), slope)
        for c in range(3):
            place(W_BASIS + 3 * (j + 1) + c, -value * normals[c] - (0.5 * WALL_FRICTION) * slopes[c])

    sample_centre(cells, [pred.at[SLOT[c]] for c in range(3)], [mid0, mid1, dx])
    for c, ref in enumerate((mid0, mid1, dx)):
        place(W_BASIS + c, jnp.where(hit, WALL_FRICTION * ref[...], 0.0))
    basis_words(0, t0)
    basis_words(1, t1)
    grow_inner(t2, t1, t3)
    early = gather_dots(EARLY, lambda region: [region.get(t) for t in (t0, t1, t2)])
    row = jnp.zeros((1, HZ), jnp.float32)
    for n, part in enumerate(early):
        row = row + jnp.where(lane1 == n, part, 0.0)
    grow_edge(moving, t2, t1, t3)
    basis_words(2, t2)
    late = gather_dots(LATE, lambda region: [None, None, region.get(t2), region.get(t3), cheb(region, damp, t3, t2, None)])
    basis_words(3, t3)
    for n, part in enumerate(late):
        row = row + jnp.where(lane1 == len(EARLY) + n, part, 0.0)
    payload = words[...]
    both = jnp.concatenate([payload, pltpu.roll(payload, W_NEXT, 1)], axis=0)
    rows_out[...] = pick(table[...], both) + row
    pl.semaphore_wait(tokens.at[2], 2)
    mine = exchange_start(rows_out, rows_in, lsem.at[8], asem.at[0], asem.at[1])
    shell_scatter(1, conn, force, own, over)
    shell_scatter(2, conn, force, own, over)
    edge.wait()

    @pl.when(me == 0)
    def _():
        over[:, 0:1, :] = jnp.zeros((3, 1, HZ), jnp.float32)

    exchange_wait(mine, rows_out, rows_in, asem.at[0], asem.at[1])
    got = rows_in[...]
    total = jnp.sum(got, axis=0, keepdims=True)
    sums = [jnp.broadcast_to(total_of(jnp.where(lane1 == n, total, 0.0)), (1, HZ)) for n in range(8)]
    moment = list(sums[:2])
    for k in range(2, 8):
        moment.append(2.0 * sums[k] - moment[k % 2])
    gram = {(i, j): 0.5 * (moment[i + j] + moment[j - i]) for i in range(5) for j in range(i, 5) if i + j < 8}
    coef, worst = iterate(lambda i, j: gram[(i, j)])
    flag_ref[0, 0] = jnp.where(worst > GUARD, 1, 0).astype(jnp.int32)[0, 0]

    words[...] = jnp.transpose(got)
    lefts, lefts2, rights, rights2 = [], [], [], []
    for s in (0, 1):
        at = W_BASIS + s * W_NEXT
        traction = words[at:at + 3, :]
        for j in range(4):
            traction = traction + coef[j] * words[at + 3 * (j + 1):at + 3 * (j + 1) + 3, :]
        where = words[W_NODE + s * W_NEXT:W_NODE + s * W_NEXT + 1, :].astype(jnp.int32)
        high, low = where // HZ, where % HZ
        block = row_of((NBLK, HZ))
        lefts.append(jnp.concatenate([jnp.where(block == high, traction[c:c + 1], 0.0) for c in range(3)], axis=0))
        lefts2.append(jnp.concatenate([jnp.where(block == high + 1, traction[c:c + 1], 0.0) for c in range(3)], axis=0))
        right = right2 = jnp.zeros(square, jnp.float32)
        for j in range(RBFW):
            w = words[W_WEIGHT + s * W_NEXT + j:W_WEIGHT + s * W_NEXT + j + 1, :]
            right = jnp.where(row_of(square) == low + j, w, right)
            right2 = jnp.where(row_of(square) + HZ == low + j, w, right2)
        rights.append(right)
        rights2.append(right2)
    applied = lax.dot_general(
        jnp.concatenate(lefts + lefts2, axis=1), jnp.concatenate(rights + rights2, axis=1),
        (((1,), (1,)), ((), ())), precision=lax.Precision.HIGHEST, preferred_element_type=jnp.float32)
    for c in range(3):
        net = own[c] + over[c, 0:NBLK, :]
        moved = mass[...] * (applied[c * NBLK:(c + 1) * NBLK] - net)
        nodal[c, 0:NBLK, :] = moved
        nodal[c, NBLK:NBLK + 8, :] = jnp.zeros((8, HZ), jnp.float32)
        force[c] = disp[c, 0:NBLK, :] + SHELL_STEP * moved
    near = jnp.concatenate([nodal[c, 0:NBLK, :] for c in range(3)] + [nodal[c, 1:NBLK + 1, :] for c in range(3)], axis=1)
    stack = jnp.concatenate(thirds(near), axis=0)
    result = jnp.zeros(square, jnp.float32)
    for s in (0, 1):
        where = got[:, W_NODE + s * W_NEXT:W_NODE + s * W_NEXT + 1].astype(jnp.int32)
        high, low = where // HZ, where % HZ
        block = lax.rem(lane_of((HZ, 3 * NBLK)), NBLK)
        chosen = jnp.where(block == high, 1.0, 0.0).astype(jnp.bfloat16)
        vals = jnp.dot(chosen, stack, preferred_element_type=jnp.float32)
        here = there = jnp.zeros(square, jnp.float32)
        for j in range(RBFW):
            w = got[:, W_WEIGHT + s * W_NEXT + j:W_WEIGHT + s * W_NEXT + j + 1]
            here = jnp.where(lane == low + j, w, here)
            there = jnp.where(lane + HZ == low + j, w, there)
        for c in range(3):
            v = total_of(vals[:, c * HZ:(c + 1) * HZ] * here + vals[:, (3 + c) * HZ:(4 + c) * HZ] * there)
            result = jnp.where(lane == 3 * s + c, v, result)
    back_out[...] = result
    mine = exchange_start(back_out, back_in, lsem.at[8], asem.at[2], asem.at[3])

    def combine(region):
        res = None
        for c, t in zip(coef, (t0, t1, t2, t3)):
            vals = [c * v for v in region.get(t)]
            res = vals if res is None else each(lambda a, b: a + b, res, vals)
        region.put(press, res)

    all_planes(combine, OX - 1, OX + CX + 1)
    for y in (OY - 1, OY + CY):
        combine(Strip(y))

    def correct(region):
        _, sides = pairs_of(region, press)
        for c in range(3):
            prior = region.get(pred.at[SLOT[c]])
            new = each(lambda v, a, b: v - 0.5 * (a - b), prior, sides[c][0], sides[c][1])
            for h in (0, 1):
                nvel[c, region.x - OX, h, region.y - OY:region.y - OY + region.n, :] = new[h]

    all_planes(correct)
    stores = []
    for h in (0, 1):
        z = slice(h * HZ, (h + 1) * HZ)
        stores.append(pltpu.make_async_copy(nvel.at[:, :, h], nv_hbm.at[:, :, :, z], lsem.at[2 * h]))
        stores.append(pltpu.make_async_copy(
            press.at[OX:OX + CX, h, OY:OY + CY, :], p_hbm.at[:, :, z], lsem.at[2 * h + 1]))
    for cp in stores:
        cp.start()
    for b in range(NBLK):
        disp_out[:, b * HZ:(b + 1) * HZ] = force.reshape(12 * NBLK, HZ)[pl.ds(b, 3, stride=NBLK), :]
    stores.append(pltpu.make_async_copy(disp_out, disp_res, lsem.at[4]))
    stores[-1].start()
    exchange_wait(mine, back_out, back_in, asem.at[2], asem.at[3])
    answers = jnp.transpose(back_in[...])[0:8]
    answers = jnp.concatenate(thirds(answers), axis=0)
    found = [jnp.dot(answers, table[:, s * HZ:(s + 1) * HZ], preferred_element_type=jnp.float32) for s in (0, 1)]
    found = [f[0:8] + f[8:16] + f[16:24] for f in found]
    iface_out[...] = found[0][0:3] + found[1][3:6]
    stores.append(pltpu.make_async_copy(iface_out, iface_res, lsem.at[5]))
    stores[-1].start()
    for cp in stores:
        cp.wait()


def fused(velocity, damping, displacement, stiffness, connectivity, inv_mass, iface_cell, iface_owner, iface_node,
          rbf_weight, normals):
    field = (PX, 2, PY, HZ)
    f32, i32 = jnp.float32, jnp.int32
    anywhere = pl.BlockSpec(memory_space=pl.ANY)
    smem = pl.BlockSpec(memory_space=pltpu.SMEM)
    square = pltpu.VMEM((HZ, HZ), f32)
    outs = pl.pallas_call(
        step_kernel,
        out_shape=(
            jax.ShapeDtypeStruct(velocity.shape, f32),
            jax.ShapeDtypeStruct(damping.shape, f32),
            jax.ShapeDtypeStruct(displacement.shape, f32),
            jax.ShapeDtypeStruct(normals.shape, f32),
            jax.ShapeDtypeStruct((1, 1), i32),
        ),
        in_specs=[pl.BlockSpec(memory_space=pltpu.HBM)] * 12,
        out_specs=(anywhere,) * 4 + (smem,),
        scratch_shapes=[
            pltpu.VMEM(displacement.shape, f32),
            pltpu.VMEM(connectivity.shape, i32),
            pltpu.VMEM(displacement.shape, f32),
            pltpu.VMEM(normals.shape, f32),
            pltpu.SemaphoreType.DMA((9,)),
            pltpu.VMEM((3,) + field, f32),
            pltpu.VMEM(field, f32),
            pltpu.VMEM((3,) + field, f32),
            pltpu.VMEM(field, f32),
            pltpu.VMEM(field, f32),
            pltpu.VMEM(field, f32),
            pltpu.VMEM(field, f32),
            pltpu.VMEM(field, f32),
            pltpu.VMEM((3, CX, 2, CY, HZ), f32),
            pltpu.VMEM((12, 12, NBLK * HZ), f32),
            pltpu.VMEM((3, 40, HZ), f32),
            pltpu.VMEM((4, NBLK, HZ), i32),
            pltpu.VMEM((NBLK * 16, HZ), f32),
            pltpu.VMEM((12, NBLK, HZ), f32),
            pltpu.VMEM((3, NBLK, HZ), f32),
            pltpu.VMEM((3, 40, HZ), f32),
            square, square, square, square, square,
            pltpu.VMEM((HZ, 2 * HZ), jnp.bfloat16),
            pltpu.VMEM((3, 40, HZ), f32),
            square, square, square, square,
            pltpu.SemaphoreType.DMA((9,)),
            pltpu.SemaphoreType.DMA((4,)),
            pltpu.SemaphoreType.DMA((34,)),
            pltpu.SemaphoreType.DMA((34,)),
            pltpu.SemaphoreType.DMA((4,)),
            pltpu.SemaphoreType.REGULAR((3,)),
            pltpu.VMEM((NBLK, HZ), f32),
            pltpu.SMEM((NPTS,), i32),
            pltpu.VMEM((1, NPTS), i32),
            pltpu.VMEM((1, NPTS), i32),
            pltpu.VMEM((1, NPTS), i32),
            pltpu.VMEM((RBFW, NPTS), f32),
            pltpu.VMEM((3, NPTS), f32),
        ],
        compiler_params=pltpu.CompilerParams(
            collective_id=0, has_side_effects=True, vmem_limit_bytes=VLIMIT << 20),
        name="step",
    )(
        velocity, damping, stiffness, displacement, connectivity, inv_mass.reshape(NBLK, HZ), iface_cell,
        iface_cell.reshape(1, NPTS), iface_owner.reshape(1, NPTS), iface_node.reshape(1, NPTS), rbf_weight, normals,
    )
    return outs


ITERS = 4
VISCOSITY = 1.0
GUARD = 4e-4
VLIMIT = 60
UNIT_STEPS = ((1, 0, 0), (0, 1, 0), (0, 0, 1))


def with_halo(block, sides, width):
    for axis, dim in sides:
        count = lax.axis_size(axis)
        forward = [(i, i + 1) for i in range(count - 1)]
        backward = [(target, source) for source, target in forward]
        low = lax.ppermute(
            lax.slice_in_dim(block, block.shape[dim] - width, None, axis=dim), axis, forward
        )
        high = lax.ppermute(lax.slice_in_dim(block, 0, width, axis=dim), axis, backward)
        block = jnp.concatenate([low, block, high], axis=dim)
    return block


def from_behind(value, axis, steps):
    count = lax.axis_size(axis)
    leading, last = (max(0, -steps), min(count, count - steps))
    return lax.ppermute(value, axis, [(source, source + steps) for source in range(leading, last)])


def window_at(padded, offsets):
    size_x = padded.shape[-3] - 2
    size_y = padded.shape[-2] - 2
    size_z = padded.shape[-1] - 2
    return padded[
        ...,
        1 + offsets[0] : 1 + offsets[0] + size_x,
        1 + offsets[1] : 1 + offsets[1] + size_y,
        1 + offsets[2] : 1 + offsets[2] + size_z,
    ]


def backward(unit_step):
    return tuple((-value for value in unit_step))


def pad_depth(source):
    spec = [(0, 0)] * (source.ndim - 1) + [(1, 1)]
    return jnp.pad(source, spec)


def predictor(padded):
    centre = window_at(padded, (0, 0, 0))
    laplace = -6.0 * centre
    advect = jnp.zeros_like(centre)
    for axis_num, unit_step in enumerate(UNIT_STEPS):
        forward = window_at(padded, unit_step)
        behind_cells = window_at(padded, backward(unit_step))
        laplace = laplace + forward + behind_cells
        advect = advect + centre[axis_num : axis_num + 1] * (0.5 * (forward - behind_cells))
    return centre + TIME_STEP * (VISCOSITY * laplace - advect)


def divergence(padded):
    summed = jnp.zeros(window_at(padded[0], (0, 0, 0)).shape, jnp.float32)
    for axis_num, unit_step in enumerate(UNIT_STEPS):
        component = padded[axis_num]
        summed = summed + 0.5 * (
            window_at(component, unit_step) - window_at(component, backward(unit_step))
        )
    return -summed


def padded_cells(source):
    extended = with_halo(source, (("grp", 0), ("dom", 1)), 1)
    return pad_depth(extended)


def operate(source, damping):
    padded = padded_cells(source)
    centre = window_at(padded, (0, 0, 0))
    beside = jnp.zeros_like(centre)
    for unit_step in UNIT_STEPS:
        beside = beside + window_at(padded, unit_step) + window_at(padded, backward(unit_step))
    return (6.0 + damping) * centre - beside


def squares(residual):
    return lax.psum(jnp.sum(residual * residual), ("grp", "dom"))


def plain(
    velocity,
    damping,
    displacement,
    stiffness,
    connectivity,
    inv_mass,
    iface_cell,
    iface_owner,
    iface_node,
    rbf_weight,
    normals,
):
    shell_nodes = displacement.shape[1]
    rim_values = from_behind(displacement[:, :RIM], ("grp", "dom"), -1)
    extended_disp = jnp.concatenate([displacement, rim_values], axis=1)
    element_count = connectivity.shape[1]
    corner_values = extended_disp[:, connectivity]
    element_dofs = jnp.transpose(corner_values, (1, 0, 2)).reshape(12, element_count)
    element_force = jnp.sum(stiffness * element_dofs[None], axis=1).reshape(4, 3, element_count)
    node_force = jnp.zeros((3, shell_nodes + RIM), jnp.float32)
    for corner in range(4):
        node_force = node_force.at[:, connectivity[corner]].add(element_force[corner])
    rim_force = from_behind(node_force[:, shell_nodes:], ("grp", "dom"), 1)
    stiff_force = node_force[:, :shell_nodes] + jnp.pad(rim_force, ((0, 0), (0, shell_nodes - RIM)))
    extended = with_halo(velocity, (("grp", 1), ("dom", 2)), 1)
    predicted = predictor(pad_depth(extended))
    star_wide = with_halo(predicted, (("grp", 1), ("dom", 2)), 1)
    star_padded = pad_depth(star_wide)
    right_side = divergence(star_padded)
    pressure = jnp.zeros_like(right_side)
    residual = right_side
    direction = right_side
    norm_now = squares(residual)
    for sweep in range(ITERS):
        mapped = operate(direction, damping)
        step_size = norm_now / lax.psum(jnp.sum(direction * mapped), ("grp", "dom"))
        pressure = pressure + step_size * direction
        residual = residual - step_size * mapped
        norm_next = squares(residual)
        direction = residual + norm_next / norm_now * direction
        norm_now = norm_next
    pressure_wide = padded_cells(pressure)
    new_velocity = predicted - jnp.stack(
        [
            0.5
            * (window_at(pressure_wide, unit_step) - window_at(pressure_wide, backward(unit_step)))
            for unit_step in UNIT_STEPS
        ]
    )
    pressure_at = pressure.reshape(-1)[iface_cell]
    velocity_at = new_velocity.reshape(3, -1)[:, iface_cell]
    traction = -pressure_at[None] * normals + WALL_FRICTION * velocity_at
    owner_dev = iface_owner[:, 0]
    point_count = owner_dev.shape[0]
    devices = lax.axis_size("grp") * lax.axis_size("dom")
    owner_cap = max(2, 2 * point_count // devices)
    order_index = lax.iota(jnp.int32, point_count)
    earlier = (owner_dev[None, :] == owner_dev[:, None]) & (
        order_index[None, :] < order_index[:, None]
    )
    slot_rank = jnp.sum(earlier.astype(jnp.int32), axis=1)
    slot_index = owner_dev * owner_cap + slot_rank
    slot_count = devices * owner_cap
    payload = jnp.concatenate([traction, rbf_weight, iface_node.astype(jnp.float32)[None]], axis=0)
    outgoing = jnp.zeros((payload.shape[0], slot_count), jnp.float32).at[:, slot_index].set(payload)
    received = lax.all_to_all(outgoing, ("grp", "dom"), split_axis=1, concat_axis=1, tiled=True)
    slot_traction = received[:3]
    slot_weight = received[3 : 3 + RBFW]
    slot_node = received[3 + RBFW].astype(jnp.int32)
    applied = jnp.zeros((3, shell_nodes), jnp.float32)
    for offset in range(RBFW):
        applied = applied.at[:, slot_node + offset].add(slot_weight[offset][None] * slot_traction)
    node_velocity = inv_mass[None] * (applied - stiff_force)
    new_displacement = displacement + SHELL_STEP * node_velocity
    slot_velocity = jnp.zeros((3, slot_count), jnp.float32)
    for offset in range(RBFW):
        slot_velocity = (
            slot_velocity + slot_weight[offset][None] * node_velocity[:, slot_node + offset]
        )
    returned_vals = lax.all_to_all(
        slot_velocity, ("grp", "dom"), split_axis=1, concat_axis=1, tiled=True
    )
    iface_velocity = returned_vals[:, slot_index]
    return (new_velocity, pressure, new_displacement, iface_velocity)


def relay_kernel(*refs):
    count = (len(refs) - 2) // 3
    ins, outs, held = refs[:count], refs[count:2 * count], refs[2 * count:3 * count]
    come, go = refs[-2:]
    pieces = []
    for a, b, c in zip(ins, outs, held):
        if len(a.shape) > 2:
            pieces += [(a.at[k], b.at[k], c.at[k]) for k in range(a.shape[0])]
        else:
            pieces.append((a, b, c))
    arrive = [pltpu.make_async_copy(a, c, come.at[n]) for n, (a, b, c) in enumerate(pieces)]
    leave = [pltpu.make_async_copy(c, b, go.at[n]) for n, (a, b, c) in enumerate(pieces)]
    for cp in arrive:
        cp.start()
    for x, y in zip(arrive, leave):
        x.wait()
        y.start()
    for y in leave:
        y.wait()


def relay(new_velocity, pressure, new_displacement, iface_velocity):
    arrays = (new_velocity, pressure.reshape(4, CX // 4, CY, 2 * HZ), new_displacement, iface_velocity)
    anywhere = pl.BlockSpec(memory_space=pl.ANY)
    count = 3 + 4 + 2
    outs = pl.pallas_call(
        relay_kernel,
        out_shape=tuple(jax.ShapeDtypeStruct(a.shape, a.dtype) for a in arrays),
        in_specs=[anywhere] * len(arrays),
        out_specs=(anywhere,) * len(arrays),
        scratch_shapes=[pltpu.VMEM(a.shape, a.dtype) for a in arrays]
        + [pltpu.SemaphoreType.DMA((count,)), pltpu.SemaphoreType.DMA((count,))],
        compiler_params=pltpu.CompilerParams(vmem_limit_bytes=60 << 20),
        name="relay",
    )(*arrays)
    return outs[0], outs[1].reshape(pressure.shape), outs[2], outs[3]


def local(*args):
    *outs, sound = fused(*args)
    return lax.cond(sound.reshape(()) > 0, lambda: relay(*outs), lambda: plain(*args))


def solution(mesh):
    return jax.shard_map(
        local,
        mesh=mesh,
        in_specs=(
            P(None, "grp", "dom", None),
            P("grp", "dom", None),
            P(None, ("grp", "dom")),
            P(None, None, ("grp", "dom")),
            P(None, ("grp", "dom")),
            P(("grp", "dom")),
            P(("grp", "dom")),
            P(("grp", "dom"), None),
            P(("grp", "dom")),
            P(None, ("grp", "dom")),
            P(None, ("grp", "dom")),
        ),
        out_specs=(
            P(None, "grp", "dom", None),
            P("grp", "dom", None),
            P(None, ("grp", "dom")),
            P(None, ("grp", "dom")),
        ),
        check_vma=False,
    )
```

```python
import jax
import jax.numpy as jnp
from jax import lax
from jax.experimental import pallas as pl
from jax.experimental.pallas import tpu as pltpu
from jax.sharding import PartitionSpec as P

MESH = pl.DeviceIdType.MESH
NGRP, NDOM = 4, 32
NDEV = NGRP * NDOM
CX, CY, HZ = 16, 32, 128
PX, PY, OX, OY = CX + 4, CY + 16, 2, 8
SLOT = {0: 0, 2: 1, 1: 2}
SHIFT, HALF = 6.26, 6.24
TIME_STEP = 0.1
WALL_FRICTION = 0.5
SHELL_STEP = 0.5
RIM, RBFW, NBLK, NPTS = 64, 4, 32, 128
W_BASIS, W_WEIGHT, W_NODE, W_NEXT = 32, 47, 51, 32
EARLY, LATE = [(0, 0), (0, 1), (1, 1), (1, 2), (2, 2)], [(2, 3), (3, 3), (3, 4)]


def rows_of(ref):
    return ref.reshape(PX * 2 * PY, HZ)


class Plane:
    def __init__(self, x, y, n):
        self.x, self.y, self.n = x, y, n

    def get(self, f, dx=0, dy=0):
        return [f[self.x + dx, h, self.y + dy:self.y + dy + self.n, :] for h in (0, 1)]

    def put(self, f, halves):
        for h in (0, 1):
            f[self.x, h, self.y:self.y + self.n, :] = halves[h]


class Inner:
    def __init__(self, x, k):
        self.x, self.k, self.n = x, k, CY // 2
        self.y = OY + k * self.n

    def get(self, f, dx=0, dy=0):
        if dy == (1 if self.k else -1):
            own = [f[self.x + dx, h, self.y:self.y + self.n, :] for h in (0, 1)]
            return [pltpu.roll(v, 1 if dy < 0 else self.n - 1, 0) for v in own]
        return [f[self.x + dx, h, self.y + dy:self.y + dy + self.n, :] for h in (0, 1)]

    def put(self, f, halves):
        for h in (0, 1):
            f[self.x, h, self.y:self.y + self.n, :] = halves[h]


class Strip:
    def __init__(self, y):
        self.y = y

    def at(self, dx, dy, h):
        return pl.ds(((OX + dx) * 2 + h) * PY + self.y + dy, CX, stride=2 * PY)

    def get(self, f, dx=0, dy=0):
        flat = rows_of(f)
        return [flat[self.at(dx, dy, h), :] for h in (0, 1)]

    def put(self, f, halves):
        flat = rows_of(f)
        for h in (0, 1):
            flat[self.at(0, 0, h), :] = halves[h]


def lanes(a):
    return lax.broadcasted_iota(jnp.int32, a.shape, 1)


def up(a):
    r0, r1 = (pltpu.roll(v, HZ - 1, 1) for v in a)
    edge = lanes(a[0]) == HZ - 1
    return [jnp.where(edge, r1, r0), jnp.where(edge, 0.0, r1)]


def down(a):
    r0, r1 = (pltpu.roll(v, 1, 1) for v in a)
    edge = lanes(a[0]) == 0
    return [jnp.where(edge, 0.0, r0), jnp.where(edge, r0, r1)]


def each(fn, *lists):
    return [fn(*vals) for vals in zip(*lists)]


def pairs_of(region, f):
    centre = region.get(f)
    return centre, (
        (region.get(f, 1, 0), region.get(f, -1, 0)),
        (region.get(f, 0, 1), region.get(f, 0, -1)),
        (up(centre), down(centre)),
    )


def predict(region, vel, c, out):
    others = [region.get(vel.at[SLOT[d]]) for d in range(3)]
    centre, sides = pairs_of(region, vel.at[SLOT[c]])
    res = []
    for h in (0, 1):
        lap = -6.0 * centre[h]
        adv = None
        for d in range(3):
            a, b = sides[d][0][h], sides[d][1][h]
            lap = lap + a + b
            term = others[d][h] * (0.5 * (a - b))
            adv = term if adv is None else adv + term
        res.append(centre[h] + TIME_STEP * (lap - adv))
    region.put(out.at[SLOT[c]], res)


def apply(region, damp, f):
    centre, sides = pairs_of(region, f)
    dv = region.get(damp)
    res = []
    for h in (0, 1):
        s = None
        for a, b in sides:
            s = a[h] + b[h] if s is None else s + a[h] + b[h]
        res.append(((dv[h] + (6.0 - SHIFT)) * centre[h] - s) * (1.0 / HALF))
    return res


def cheb(region, damp, f, before, out):
    res = apply(region, damp, f)
    if before is not None:
        res = each(lambda a, b: 2.0 * a - b, res, region.get(before))
    if out is not None:
        region.put(out, res)
    return res


def all_planes(fn, lo=OX, hi=OX + CX, parts=2, unroll=2):
    def body(x, carry):
        for k in range(parts):
            fn(Plane(x, OY + k * (CY // parts), CY // parts))
        return carry

    lax.fori_loop(lo, hi, body, 0, unroll=unroll)


def inner_planes(fn):
    def body(x, carry):
        for k in range(2):
            fn(Inner(x, k))
        return carry

    lax.fori_loop(OX + 1, OX + CX - 1, body, 0, unroll=2)


def planes_at(fn, xs):
    for x in xs:
        for k in range(2):
            fn(Plane(x, OY + k * (CY // 2), CY // 2))


def position():
    return lax.axis_index("grp"), lax.axis_index("dom")


def clear_outside(f):
    g, d = position()

    @pl.when(g == 0)
    def _():
        f[0:OX] = jnp.zeros((OX, 2, PY, HZ), jnp.float32)

    @pl.when(g == NGRP - 1)
    def _():
        f[OX + CX:PX] = jnp.zeros((PX - OX - CX, 2, PY, HZ), jnp.float32)

    @pl.when(d == 0)
    def _():
        f[:, :, 0:OY, :] = jnp.zeros((PX, 2, OY, HZ), jnp.float32)

    @pl.when(d == NDOM - 1)
    def _():
        f[:, :, OY + CY:PY, :] = jnp.zeros((PX, 2, PY - OY - CY, HZ), jnp.float32)


def clear_faces(f):
    g, d = position()
    xs, ys = slice(OX, OX + CX), slice(OY, OY + CY)

    @pl.when(g == 0)
    def _():
        f[0:OX, :, ys, :] = jnp.zeros((OX, 2, CY, HZ), jnp.float32)

    @pl.when(g == NGRP - 1)
    def _():
        f[OX + CX:PX, :, ys, :] = jnp.zeros((PX - OX - CX, 2, CY, HZ), jnp.float32)

    @pl.when(d == 0)
    def _():
        f[xs, :, 0:OY, :] = jnp.zeros((CX, 2, OY, HZ), jnp.float32)

    @pl.when(d == NDOM - 1)
    def _():
        f[xs, :, OY + CY:PY, :] = jnp.zeros((CX, 2, PY - OY - CY, HZ), jnp.float32)


def neighbour(dg, dd):
    g, d = position()
    return lax.rem(g + dg + NGRP, NGRP), lax.rem(d + dd + NDOM, NDOM)


def sides_of(ref, lead, width):
    lo, hi = OX, OX + CX
    a, b = OY, OY + CY
    ys = slice(a, b)
    xs = slice(lo, hi)
    w = width
    return [
        ((1, 0), lead + (slice(hi - w, hi), slice(None), ys), lead + (slice(lo - w, lo), slice(None), ys)),
        ((-1, 0), lead + (slice(lo, lo + w), slice(None), ys), lead + (slice(hi, hi + w), slice(None), ys)),
        ((0, 1), lead + (xs, slice(None), slice(b - w, b)), lead + (xs, slice(None), slice(a - w, a))),
        ((0, -1), lead + (xs, slice(None), slice(a, a + w)), lead + (xs, slice(None), slice(b, b + w))),
    ]


def corners_of(ref, lead):
    out = []
    for dg in (1, -1):
        for dd in (1, -1):
            sx = OX + CX - 1 if dg == 1 else OX
            tx = OX - 1 if dg == 1 else OX + CX
            sy = OY + CY - 1 if dd == 1 else OY
            ty = OY - 1 if dd == 1 else OY + CY
            out.append((
                (dg, dd),
                lead + (slice(sx, sx + 1), slice(None), slice(sy, sy + 1)),
                lead + (slice(tx, tx + 1), slice(None), slice(ty, ty + 1)),
            ))
    return out


def start_all(ref, items, send, recv, base):
    copies = []
    for k, (way, src, dst) in enumerate(items):
        cp = pltpu.make_async_remote_copy(
            src_ref=ref.at[src], dst_ref=ref.at[dst],
            send_sem=send.at[base + k], recv_sem=recv.at[base + k],
            device_id=neighbour(*way), device_id_type=MESH,
        )
        cp.start()
        copies.append(cp)
    return copies


def everyone(fn):
    g, d = position()
    for dg in (2, 1, 3, 0):
        tg = lax.rem(g + dg, NGRP)

        def body(i, carry):
            fn(tg, lax.rem(d + i, NDOM))
            return carry

        if dg:
            lax.fori_loop(8, 8 + NDOM, body, 0, unroll=16)
        else:
            lax.fori_loop(8, NDOM, body, 0, unroll=12)
            lax.fori_loop(1, 8, body, 0, unroll=7)


def greet_near():
    barrier = pltpu.get_barrier_semaphore()
    for dg in (-1, 0, 1):
        for dd in (-1, 0, 1):
            if dg or dd:
                pl.semaphore_signal(barrier, inc=1, device_id=neighbour(dg, dd), device_id_type=MESH)
    return barrier


def pass_on(token, reach):
    for dd in (reach, -reach):
        pl.semaphore_signal(token, inc=1, device_id=neighbour(0, dd), device_id_type=MESH)


def exchange_start(out_ref, in_ref, own, send, recv):
    g, d = position()
    me = g * NDOM + d
    mine = pltpu.make_async_copy(out_ref.at[pl.ds(me, 1)], in_ref.at[pl.ds(me, 1)], own)
    mine.start()
    everyone(lambda tg, td: pltpu.make_async_remote_copy(
        src_ref=out_ref.at[pl.ds(tg * NDOM + td, 1)], dst_ref=in_ref.at[pl.ds(me, 1)],
        send_sem=send, recv_sem=recv, device_id=(tg, td), device_id_type=MESH,
    ).start())
    return mine


def exchange_wait(mine, out_ref, in_ref, send, recv):
    rest = pl.ds(0, NDEV - 1)
    mine.wait()
    pltpu.make_async_copy(out_ref.at[rest], in_ref.at[rest], recv).wait()
    pltpu.make_async_copy(out_ref.at[rest], in_ref.at[rest], send).wait()


def iterate(gram):
    def times(v):
        out = [None] * 5

        def put(i, val):
            out[i] = val if out[i] is None else out[i] + val

        for j, val in enumerate(v):
            if val is None:
                continue
            put(j, SHIFT * val)
            if j == 0:
                put(1, HALF * val)
            else:
                put(j + 1, (0.5 * HALF) * val)
                put(j - 1, (0.5 * HALF) * val)
        return out

    worst = None

    def form(a, b):
        nonlocal worst
        total = size = None
        for i in range(5):
            for j in range(5):
                if a[i] is None or b[j] is None:
                    continue
                term = a[i] * b[j] * gram(min(i, j), max(i, j))
                total = term if total is None else total + term
                mag = jnp.abs(term)
                size = mag if size is None else size + mag
        ratio = total / size
        worst = ratio if worst is None else jnp.minimum(worst, ratio)
        return total

    def axpy(a, s, b):
        return [x if y is None else (s * y if x is None else x + s * y) for x, y in zip(a, b)]

    one = jnp.ones_like(gram(0, 0))
    r = [one, None, None, None, None]
    d = list(r)
    p = [None] * 5
    rr = gram(0, 0)
    for k in range(4):
        m = times(d)
        step = rr / form(d, m)
        p = axpy(p, step, d)
        if k == 3:
            break
        r = axpy(r, -step, m)
        new = form(r, r)
        d = axpy(r, new / rr, d)
        rr = new
    return p[:4], worst


def lane_of(shape):
    return lax.broadcasted_iota(jnp.int32, shape, 1)


def row_of(shape):
    return lax.broadcasted_iota(jnp.int32, shape, 0)


def thirds(x):
    a = x.astype(jnp.bfloat16)
    rest = x - a.astype(jnp.float32)
    b = rest.astype(jnp.bfloat16)
    return a, b, (rest - b.astype(jnp.float32)).astype(jnp.bfloat16)


def pick(onehot, x):
    width = x.shape[1]
    wide = jnp.concatenate(thirds(x), axis=1)
    out = jnp.dot(onehot, wide, preferred_element_type=jnp.float32)
    return out[:, :width] + out[:, width:2 * width] + out[:, 2 * width:]


def spread(src, dst, count, stride):
    for b in range(NBLK):
        dst[pl.ds(b, count, stride=stride), :] = src[:, b * HZ:(b + 1) * HZ]


def shell_gather(q, disp, conn, dofs):
    sub = row_of((8, HZ))
    for a in range(4):
        rel = conn[a, 8 * q:8 * q + 8, :] - HZ * (8 * q + sub)
        near = rel < HZ
        low = jnp.where(near, rel, rel - HZ)
        for c in range(3):
            here = jnp.take_along_axis(disp[c, 8 * q:8 * q + 8, :], low, axis=1, mode="promise_in_bounds")
            there = jnp.take_along_axis(disp[c, 8 * q + 1:8 * q + 9, :], low, axis=1, mode="promise_in_bounds")
            dofs[pl.ds(8 * q * 16 + 3 * a + c, 8, stride=16), :] = jnp.where(near, here, there)


def shell_product(q, stiff, dofs, force):
    sub = row_of((8, HZ))

    def body(i, carry):
        parts = []
        for b in range(8 * q, 8 * q + 8):
            z = slice(b * HZ, (b + 1) * HZ)
            top = stiff[i, 0:8, z] * dofs[b * 16:b * 16 + 8, :]
            low = stiff[i, 8:12, z] * dofs[b * 16 + 8:b * 16 + 12, :]
            parts.append(top + jnp.concatenate([low, jnp.zeros((4, HZ), jnp.float32)], axis=0))
        first = sub < 4
        parts = [
            jnp.where(first, parts[k], parts[k + 4]) + pltpu.roll(jnp.where(first, parts[k + 4], parts[k]), 4, 0)
            for k in range(4)
        ]
        for bit in (2, 1):
            keep = (sub & bit) == 0
            parts = [
                jnp.where(keep, parts[k] + pltpu.roll(parts[k], 8 - bit, 0),
                          parts[k + bit] + pltpu.roll(parts[k + bit], bit, 0))
                for k in range(bit)
            ]
        force[i, 8 * q:8 * q + 8, :] = parts[0]
        return carry

    lax.fori_loop(0, 12, body, 0)


def shell_scatter(q, conn, force, own, over):
    lane = lane_of((8, HZ))
    element = HZ * (8 * q + row_of((8, HZ))) + lane
    rel = [conn[a, 8 * q:8 * q + 8, :] - element for a in range(4)]
    vals = [[force[3 * a + c, 8 * q:8 * q + 8, :] for c in range(3)] for a in range(4)]

    def body(d, acc):
        hit = [r == d for r in rel]
        inside = lane >= d
        out = []
        for c in range(3):
            s = jnp.zeros((8, HZ), jnp.float32)
            for a in range(4):
                s = jnp.where(hit[a], vals[a][c], s)
            s = pltpu.roll(s, d, 1)
            out.append(acc[2 * c] + jnp.where(inside, s, 0.0))
            out.append(acc[2 * c + 1] + jnp.where(inside, 0.0, s))
        return tuple(out)

    acc = lax.fori_loop(0, RIM + 1, body, tuple(jnp.zeros((8, HZ), jnp.float32) for _ in range(6)), unroll=5)
    for c in range(3):
        own[c, 8 * q:8 * q + 8, :] = acc[2 * c]
        over[c, 8 * q + 1:8 * q + 9, :] = acc[2 * c + 1]


def sample(cells, f, mid0, mid1, dx, dy):
    def body(i, carry):
        for u in range(8):
            k = i * 8 + u
            cell = cells[k]
            x, y, h = (cell >> 13) + OX, ((cell >> 8) & (CY - 1)) + OY, (cell >> 7) & 1
            at = pl.ds(k, 1)
            mid0[at, :] = f[x, 0, pl.ds(y, 1), :]
            mid1[at, :] = f[x, 1, pl.ds(y, 1), :]
            dx[at, :] = f[x + 1, h, pl.ds(y, 1), :] - f[x - 1, h, pl.ds(y, 1), :]
            dy[at, :] = f[x, h, pl.ds(y + 1, 1), :] - f[x, h, pl.ds(y - 1, 1), :]
        return carry

    lax.fori_loop(0, NPTS // 8, body, 0)


def sample_centre(cells, fields, outs):
    def body(i, carry):
        for u in range(8):
            k = i * 8 + u
            cell = cells[k]
            x, y, h = (cell >> 13) + OX, ((cell >> 8) & (CY - 1)) + OY, (cell >> 7) & 1
            for f, o in zip(fields, outs):
                o[pl.ds(k, 1), :] = f[x, h, pl.ds(y, 1), :]
        return carry

    lax.fori_loop(0, NPTS // 8, body, 0)


def column(row):
    return jnp.transpose(jnp.broadcast_to(row, (HZ, HZ)))


def total_of(x):
    return jnp.sum(x, axis=1, keepdims=True)


def step_kernel(vel_hbm, damp_hbm, stiff_hbm, disp_hbm, conn_hbm, *rest):
    small_hbm, rest = rest[:7], rest[7:]
    small, rest = rest[-7:], rest[:-7]
    step_body(vel_hbm, damp_hbm, stiff_hbm, disp_hbm, conn_hbm, small_hbm, small, *rest)


def step_body(vel_hbm, damp_hbm, stiff_hbm, disp_hbm, conn_hbm, small_hbm, small,
                nv_hbm, p_hbm, disp_res, iface_res, flag_ref, disp_in, conn_in, disp_out, iface_out, msem,
                vel, damp, pred, t0, t1, t2, t3, press, nvel, stiff,
                disp, conn, dofs, force, own, over, mid0, mid1, dx, dy, words, table, nodal,
                rows_out, rows_in, back_out, back_in, lsem, ksem, ssem, rsem, asem, tokens):
    barrier = greet_near()
    g, d = position()
    me = g * NDOM + d
    loads = []
    for h in (0, 1):
        z = slice(h * HZ, (h + 1) * HZ)
        for c in range(3):
            loads.append(pltpu.make_async_copy(
                vel_hbm.at[c, :, :, z], vel.at[SLOT[c], OX:OX + CX, h, OY:OY + CY, :], lsem.at[len(loads)]))
        loads.append(pltpu.make_async_copy(
            damp_hbm.at[:, :, z], damp.at[OX:OX + CX, h, OY:OY + CY, :], lsem.at[len(loads)]))
    for q in range(4):
        z = slice(q * 8 * HZ, (q + 1) * 8 * HZ)
        loads.append(pltpu.make_async_copy(stiff_hbm.at[:, :, z], stiff.at[:, :, z], ksem.at[q]))
    minor = [pltpu.make_async_copy(a, b, msem.at[n])
             for n, (a, b) in enumerate(zip((disp_hbm, conn_hbm) + small_hbm, (disp_in, conn_in) + small))]
    for cp in loads[:8] + minor + loads[8:]:
        cp.start()
    blocks = loads[8:]
    mass, cells, cell_row, owner, node, weight, normal = small

    square = (HZ, HZ)
    for cp in loads[:8]:
        cp.wait()
    pl.semaphore_wait(barrier, 8)

    one = slice(None)
    f_x, f_y, f_z = SLOT[0], SLOT[1], SLOT[2]
    faces = corners_of(vel, (one,))
    wide_x, wide_y = sides_of(vel, (f_x,), 2)[:2], sides_of(vel, (f_y,), 2)[2:]
    thin_x, thin_y = sides_of(vel, (slice(1, 3),), 1)[:2], sides_of(vel, (slice(0, 2),), 1)[2:]
    copies = start_all(vel, faces + wide_x + wide_y + thin_x + thin_y, ssem, rsem, 0)
    damps = start_all(damp, sides_of(damp, (), 1), ssem, rsem, 12)
    minor[0].wait()
    spread(disp_in, disp.reshape(3 * 40, HZ), 3, 40)
    before, after = lax.rem(me + NDEV - 1, NDEV), lax.rem(me + 1, NDEV)
    rim = pltpu.make_async_remote_copy(
        src_ref=disp.at[:, 0:1, :], dst_ref=disp.at[:, NBLK:NBLK + 1, :], send_sem=ssem.at[32], recv_sem=rsem.at[32],
        device_id=(lax.div(before, NDOM), lax.rem(before, NDOM)), device_id_type=MESH)
    rim.start()
    minor[1].wait()
    spread(conn_in, conn.reshape(4 * NBLK, HZ), 4, NBLK)
    for q in range(3):
        shell_gather(q, disp, conn, dofs)
        blocks[q].wait()
        shell_product(q, stiff, dofs, force)

    def pred_main(region):
        for c in range(3):
            predict(region, vel, c, pred)

    inner_planes(pred_main)
    for cp in copies[4:]:
        cp.wait()
    for c in range(3):
        clear_faces(vel.at[c])
    planes_at(pred_main, (OX, OX + CX - 1))
    for y in (OY, OY + CY - 1):
        pred_main(Strip(y))
    for cp in copies[:4]:
        cp.wait()
    pass_on(tokens.at[0], 2)
    for c in (0, 1):
        clear_outside(vel.at[SLOT[c]])
    planes_at(lambda region: predict(region, vel, 0, pred), (OX - 1, OX + CX))
    for y in (OY - 1, OY + CY):
        predict(Strip(y), vel, 1, pred)
    clear_outside(pred.at[f_x])
    clear_outside(pred.at[f_y])

    def diverge(region):
        fx, fy, fz = pred.at[f_x], pred.at[f_y], region.get(pred.at[f_z])
        s = each(lambda a, b: 0.5 * (a - b), region.get(fx, 1, 0), region.get(fx, -1, 0))
        s = each(lambda s, a, b: s + 0.5 * (a - b), s, region.get(fy, 0, 1), region.get(fy, 0, -1))
        s = each(lambda s, a, b: -(s + 0.5 * (a - b)), s, up(fz), down(fz))
        region.put(t0, s)

    all_planes(diverge)

    def swap(f, base):
        return start_all(f, corners_of(f, ()) + sides_of(f, (), 2), ssem, rsem, base)

    def grow_inner(f, before, out):
        inner_planes(lambda region: cheb(region, damp, f, before, out))

    def grow_edge(moving, f, before, out):
        for cp in moving[4:]:
            cp.wait()
        clear_faces(f)
        grow = lambda region: cheb(region, damp, f, before, out)
        planes_at(grow, (OX, OX + CX - 1))
        for y in (OY, OY + CY - 1):
            grow(Strip(y))
        for cp in moving[:4]:
            cp.wait()
        clear_outside(f)
        planes_at(grow, (OX - 1, OX + CX))
        for y in (OY - 1, OY + CY):
            grow(Strip(y))
        clear_outside(out)

    moving = swap(t0, 16)
    pl.semaphore_wait(tokens.at[0], 2)
    pass_on(tokens.at[1], 4)
    for cp in damps:
        cp.wait()
    rim.wait()

    @pl.when(me == NDEV - 1)
    def _():
        disp[:, NBLK:NBLK + 1, :] = jnp.zeros((3, 1, HZ), jnp.float32)

    shell_gather(3, disp, conn, dofs)
    blocks[3].wait()
    shell_product(3, stiff, dofs, force)
    shell_scatter(3, conn, force, own, over)
    edge = pltpu.make_async_remote_copy(
        src_ref=over.at[:, NBLK:NBLK + 1, :], dst_ref=over.at[:, 0:1, :], send_sem=ssem.at[33], recv_sem=rsem.at[33],
        device_id=(lax.div(after, NDOM), lax.rem(after, NDOM)), device_id_type=MESH)
    edge.start()
    shell_scatter(0, conn, force, own, over)
    grow_inner(t0, None, t1)
    pl.semaphore_wait(tokens.at[1], 2)
    pass_on(tokens.at[2], 8)
    grow_edge(moving, t0, None, t1)
    all_planes(lambda region: cheb(region, damp, t1, t0, t2))

    moving = swap(t2, 24)
    for cp in minor[2:]:
        cp.wait()
    owns = owner[...] == row_of(square)
    first = jnp.min(jnp.where(owns, lane_of(square), HZ), axis=1, keepdims=True)
    for s in (0, 1):
        table[:, s * HZ:(s + 1) * HZ] = jnp.where(
            owns & ((lane_of(square) == first) == (s == 0)), 1.0, 0.0).astype(jnp.bfloat16)
    words[...] = jnp.zeros(square, jnp.float32)
    words[W_WEIGHT:W_WEIGHT + 4, :] = weight[...]
    words[W_NODE:W_NODE + 1, :] = node[...].astype(jnp.float32)
    words[...] = jnp.transpose(words[...])
    z_all = column(cell_row[...]) & (2 * HZ - 1)
    lane = lane_of(square)
    hit0, hit1 = lane == z_all, lane + HZ == z_all
    hit = hit0 | hit1
    normals = [column(normal[c:c + 1, :]) for c in range(3)]

    lane1 = lane_of((1, HZ))

    def gather_dots(pairs, fields):
        def body(x, acc):
            acc = list(acc)
            for k in range(2):
                ts = fields(Plane(x, OY + 16 * k, 16))
                for n, (i, j) in enumerate(pairs):
                    for h in (0, 1):
                        prod = ts[i][h] * ts[j][h]
                        acc[n] = acc[n] + (prod[0:8] + prod[8:16])
            return tuple(acc)

        acc = lax.fori_loop(OX, OX + CX, body, tuple(jnp.zeros((8, HZ), jnp.float32) for _ in pairs), unroll=2)
        return [total_of(jnp.sum(a, axis=0, keepdims=True)) for a in acc]

    def place(word, values):
        words[...] += jnp.where(lane == word, total_of(values), 0.0)

    def basis_words(j, f):
        sample(cells, f, mid0, mid1, dx, dy)
        a, b = mid0[...], mid1[...]
        value = jnp.where(hit0, a, 0.0) + jnp.where(hit1, b, 0.0)
        slope = (jnp.where(lane == z_all + 1, a, 0.0) + jnp.where(lane + HZ == z_all + 1, b, 0.0)
                 - jnp.where(lane == z_all - 1, a, 0.0) - jnp.where(lane + HZ == z_all - 1, b, 0.0))
        slopes = (jnp.where(hit, dx[...], 0.0), jnp.where(hit, dy[...], 0.0), slope)
        for c in range(3):
            place(W_BASIS + 3 * (j + 1) + c, -value * normals[c] - (0.5 * WALL_FRICTION) * slopes[c])

    sample_centre(cells, [pred.at[SLOT[c]] for c in range(3)], [mid0, mid1, dx])
    for c, ref in enumerate((mid0, mid1, dx)):
        place(W_BASIS + c, jnp.where(hit, WALL_FRICTION * ref[...], 0.0))
    basis_words(0, t0)
    basis_words(1, t1)
    grow_inner(t2, t1, t3)
    early = gather_dots(EARLY, lambda region: [region.get(t) for t in (t0, t1, t2)])
    row = jnp.zeros((1, HZ), jnp.float32)
    for n, part in enumerate(early):
        row = row + jnp.where(lane1 == n, part, 0.0)
    grow_edge(moving, t2, t1, t3)
    basis_words(2, t2)
    late = gather_dots(LATE, lambda region: [None, None, region.get(t2), region.get(t3), cheb(region, damp, t3, t2, None)])
    basis_words(3, t3)
    for n, part in enumerate(late):
        row = row + jnp.where(lane1 == len(EARLY) + n, part, 0.0)
    payload = words[...]
    both = jnp.concatenate([payload, pltpu.roll(payload, W_NEXT, 1)], axis=0)
    rows_out[...] = pick(table[...], both) + row
    pl.semaphore_wait(tokens.at[2], 2)
    mine = exchange_start(rows_out, rows_in, lsem.at[8], asem.at[0], asem.at[1])
    shell_scatter(1, conn, force, own, over)
    shell_scatter(2, conn, force, own, over)
    edge.wait()

    @pl.when(me == 0)
    def _():
        over[:, 0:1, :] = jnp.zeros((3, 1, HZ), jnp.float32)

    exchange_wait(mine, rows_out, rows_in, asem.at[0], asem.at[1])
    got = rows_in[...]
    total = jnp.sum(got, axis=0, keepdims=True)
    sums = [jnp.broadcast_to(total_of(jnp.where(lane1 == n, total, 0.0)), (1, HZ)) for n in range(8)]
    moment = list(sums[:2])
    for k in range(2, 8):
        moment.append(2.0 * sums[k] - moment[k % 2])
    gram = {(i, j): 0.5 * (moment[i + j] + moment[j - i]) for i in range(5) for j in range(i, 5) if i + j < 8}
    coef, worst = iterate(lambda i, j: gram[(i, j)])
    flag_ref[0, 0] = jnp.where(worst > GUARD, 1, 0).astype(jnp.int32)[0, 0]

    words[...] = jnp.transpose(got)
    lefts, lefts2, rights, rights2 = [], [], [], []
    for s in (0, 1):
        at = W_BASIS + s * W_NEXT
        traction = words[at:at + 3, :]
        for j in range(4):
            traction = traction + coef[j] * words[at + 3 * (j + 1):at + 3 * (j + 1) + 3, :]
        where = words[W_NODE + s * W_NEXT:W_NODE + s * W_NEXT + 1, :].astype(jnp.int32)
        high, low = where // HZ, where % HZ
        block = row_of((NBLK, HZ))
        lefts.append(jnp.concatenate([jnp.where(block == high, traction[c:c + 1], 0.0) for c in range(3)], axis=0))
        lefts2.append(jnp.concatenate([jnp.where(block == high + 1, traction[c:c + 1], 0.0) for c in range(3)], axis=0))
        right = right2 = jnp.zeros(square, jnp.float32)
        for j in range(RBFW):
            w = words[W_WEIGHT + s * W_NEXT + j:W_WEIGHT + s * W_NEXT + j + 1, :]
            right = jnp.where(row_of(square) == low + j, w, right)
            right2 = jnp.where(row_of(square) + HZ == low + j, w, right2)
        rights.append(right)
        rights2.append(right2)
    applied = lax.dot_general(
        jnp.concatenate(lefts + lefts2, axis=1), jnp.concatenate(rights + rights2, axis=1),
        (((1,), (1,)), ((), ())), precision=lax.Precision.HIGHEST, preferred_element_type=jnp.float32)
    for c in range(3):
        net = own[c] + over[c, 0:NBLK, :]
        moved = mass[...] * (applied[c * NBLK:(c + 1) * NBLK] - net)
        nodal[c, 0:NBLK, :] = moved
        nodal[c, NBLK:NBLK + 8, :] = jnp.zeros((8, HZ), jnp.float32)
        force[c] = disp[c, 0:NBLK, :] + SHELL_STEP * moved
    near = jnp.concatenate([nodal[c, 0:NBLK, :] for c in range(3)] + [nodal[c, 1:NBLK + 1, :] for c in range(3)], axis=1)
    stack = jnp.concatenate(thirds(near), axis=0)
    result = jnp.zeros(square, jnp.float32)
    for s in (0, 1):
        where = got[:, W_NODE + s * W_NEXT:W_NODE + s * W_NEXT + 1].astype(jnp.int32)
        high, low = where // HZ, where % HZ
        block = lax.rem(lane_of((HZ, 3 * NBLK)), NBLK)
        chosen = jnp.where(block == high, 1.0, 0.0).astype(jnp.bfloat16)
        vals = jnp.dot(chosen, stack, preferred_element_type=jnp.float32)
        here = there = jnp.zeros(square, jnp.float32)
        for j in range(RBFW):
            w = got[:, W_WEIGHT + s * W_NEXT + j:W_WEIGHT + s * W_NEXT + j + 1]
            here = jnp.where(lane == low + j, w, here)
            there = jnp.where(lane + HZ == low + j, w, there)
        for c in range(3):
            v = total_of(vals[:, c * HZ:(c + 1) * HZ] * here + vals[:, (3 + c) * HZ:(4 + c) * HZ] * there)
            result = jnp.where(lane == 3 * s + c, v, result)
    back_out[...] = result
    mine = exchange_start(back_out, back_in, lsem.at[8], asem.at[2], asem.at[3])

    def combine(region):
        res = None
        for c, t in zip(coef, (t0, t1, t2, t3)):
            vals = [c * v for v in region.get(t)]
            res = vals if res is None else each(lambda a, b: a + b, res, vals)
        region.put(press, res)

    all_planes(combine, OX - 1, OX + CX + 1)
    for y in (OY - 1, OY + CY):
        combine(Strip(y))

    def correct(region):
        _, sides = pairs_of(region, press)
        for c in range(3):
            prior = region.get(pred.at[SLOT[c]])
            new = each(lambda v, a, b: v - 0.5 * (a - b), prior, sides[c][0], sides[c][1])
            for h in (0, 1):
                nvel[c, region.x - OX, h, region.y - OY:region.y - OY + region.n, :] = new[h]

    all_planes(correct)
    stores = []
    for h in (0, 1):
        z = slice(h * HZ, (h + 1) * HZ)
        stores.append(pltpu.make_async_copy(nvel.at[:, :, h], nv_hbm.at[:, :, :, z], lsem.at[2 * h]))
        stores.append(pltpu.make_async_copy(
            press.at[OX:OX + CX, h, OY:OY + CY, :], p_hbm.at[:, :, z], lsem.at[2 * h + 1]))
    for cp in stores:
        cp.start()
    for b in range(NBLK):
        disp_out[:, b * HZ:(b + 1) * HZ] = force.reshape(12 * NBLK, HZ)[pl.ds(b, 3, stride=NBLK), :]
    stores.append(pltpu.make_async_copy(disp_out, disp_res, lsem.at[4]))
    stores[-1].start()
    exchange_wait(mine, back_out, back_in, asem.at[2], asem.at[3])
    answers = jnp.transpose(back_in[...])[0:8]
    answers = jnp.concatenate(thirds(answers), axis=0)
    found = [jnp.dot(answers, table[:, s * HZ:(s + 1) * HZ], preferred_element_type=jnp.float32) for s in (0, 1)]
    found = [f[0:8] + f[8:16] + f[16:24] for f in found]
    iface_out[...] = found[0][0:3] + found[1][3:6]
    stores.append(pltpu.make_async_copy(iface_out, iface_res, lsem.at[5]))
    stores[-1].start()
    for cp in stores:
        cp.wait()


def fused(velocity, damping, displacement, stiffness, connectivity, inv_mass, iface_cell, iface_owner, iface_node,
          rbf_weight, normals):
    field = (PX, 2, PY, HZ)
    f32, i32 = jnp.float32, jnp.int32
    anywhere = pl.BlockSpec(memory_space=pl.ANY)
    smem = pl.BlockSpec(memory_space=pltpu.SMEM)
    square = pltpu.VMEM((HZ, HZ), f32)
    outs = pl.pallas_call(
        step_kernel,
        out_shape=(
            jax.ShapeDtypeStruct(velocity.shape, f32),
            jax.ShapeDtypeStruct(damping.shape, f32),
            jax.ShapeDtypeStruct(displacement.shape, f32),
            jax.ShapeDtypeStruct(normals.shape, f32),
            jax.ShapeDtypeStruct((1, 1), i32),
        ),
        in_specs=[pl.BlockSpec(memory_space=pltpu.HBM)] * 12,
        out_specs=(anywhere,) * 4 + (smem,),
        scratch_shapes=[
            pltpu.VMEM(displacement.shape, f32),
            pltpu.VMEM(connectivity.shape, i32),
            pltpu.VMEM(displacement.shape, f32),
            pltpu.VMEM(normals.shape, f32),
            pltpu.SemaphoreType.DMA((9,)),
            pltpu.VMEM((3,) + field, f32),
            pltpu.VMEM(field, f32),
            pltpu.VMEM((3,) + field, f32),
            pltpu.VMEM(field, f32),
            pltpu.VMEM(field, f32),
            pltpu.VMEM(field, f32),
            pltpu.VMEM(field, f32),
            pltpu.VMEM(field, f32),
            pltpu.VMEM((3, CX, 2, CY, HZ), f32),
            pltpu.VMEM((12, 12, NBLK * HZ), f32),
            pltpu.VMEM((3, 40, HZ), f32),
            pltpu.VMEM((4, NBLK, HZ), i32),
            pltpu.VMEM((NBLK * 16, HZ), f32),
            pltpu.VMEM((12, NBLK, HZ), f32),
            pltpu.VMEM((3, NBLK, HZ), f32),
            pltpu.VMEM((3, 40, HZ), f32),
            square, square, square, square, square,
            pltpu.VMEM((HZ, 2 * HZ), jnp.bfloat16),
            pltpu.VMEM((3, 40, HZ), f32),
            square, square, square, square,
            pltpu.SemaphoreType.DMA((9,)),
            pltpu.SemaphoreType.DMA((4,)),
            pltpu.SemaphoreType.DMA((34,)),
            pltpu.SemaphoreType.DMA((34,)),
            pltpu.SemaphoreType.DMA((4,)),
            pltpu.SemaphoreType.REGULAR((3,)),
            pltpu.VMEM((NBLK, HZ), f32),
            pltpu.SMEM((NPTS,), i32),
            pltpu.VMEM((1, NPTS), i32),
            pltpu.VMEM((1, NPTS), i32),
            pltpu.VMEM((1, NPTS), i32),
            pltpu.VMEM((RBFW, NPTS), f32),
            pltpu.VMEM((3, NPTS), f32),
        ],
        compiler_params=pltpu.CompilerParams(
            collective_id=0, has_side_effects=True, vmem_limit_bytes=VLIMIT << 20),
        name="step",
    )(
        velocity, damping, stiffness, displacement, connectivity, inv_mass.reshape(NBLK, HZ), iface_cell,
        iface_cell.reshape(1, NPTS), iface_owner.reshape(1, NPTS), iface_node.reshape(1, NPTS), rbf_weight, normals,
    )
    return outs


ITERS = 4
VISCOSITY = 1.0
GUARD = 4e-4
VLIMIT = 60
UNIT_STEPS = ((1, 0, 0), (0, 1, 0), (0, 0, 1))


def with_halo(block, sides, width):
    for axis, dim in sides:
        count = lax.axis_size(axis)
        forward = [(i, i + 1) for i in range(count - 1)]
        backward = [(target, source) for source, target in forward]
        low = lax.ppermute(
            lax.slice_in_dim(block, block.shape[dim] - width, None, axis=dim), axis, forward
        )
        high = lax.ppermute(lax.slice_in_dim(block, 0, width, axis=dim), axis, backward)
        block = jnp.concatenate([low, block, high], axis=dim)
    return block


def from_behind(value, axis, steps):
    count = lax.axis_size(axis)
    leading, last = (max(0, -steps), min(count, count - steps))
    return lax.ppermute(value, axis, [(source, source + steps) for source in range(leading, last)])


def window_at(padded, offsets):
    size_x = padded.shape[-3] - 2
    size_y = padded.shape[-2] - 2
    size_z = padded.shape[-1] - 2
    return padded[
        ...,
        1 + offsets[0] : 1 + offsets[0] + size_x,
        1 + offsets[1] : 1 + offsets[1] + size_y,
        1 + offsets[2] : 1 + offsets[2] + size_z,
    ]


def backward(unit_step):
    return tuple((-value for value in unit_step))


def pad_depth(source):
    spec = [(0, 0)] * (source.ndim - 1) + [(1, 1)]
    return jnp.pad(source, spec)


def predictor(padded):
    centre = window_at(padded, (0, 0, 0))
    laplace = -6.0 * centre
    advect = jnp.zeros_like(centre)
    for axis_num, unit_step in enumerate(UNIT_STEPS):
        forward = window_at(padded, unit_step)
        behind_cells = window_at(padded, backward(unit_step))
        laplace = laplace + forward + behind_cells
        advect = advect + centre[axis_num : axis_num + 1] * (0.5 * (forward - behind_cells))
    return centre + TIME_STEP * (VISCOSITY * laplace - advect)


def divergence(padded):
    summed = jnp.zeros(window_at(padded[0], (0, 0, 0)).shape, jnp.float32)
    for axis_num, unit_step in enumerate(UNIT_STEPS):
        component = padded[axis_num]
        summed = summed + 0.5 * (
            window_at(component, unit_step) - window_at(component, backward(unit_step))
        )
    return -summed


def padded_cells(source):
    extended = with_halo(source, (("grp", 0), ("dom", 1)), 1)
    return pad_depth(extended)


def operate(source, damping):
    padded = padded_cells(source)
    centre = window_at(padded, (0, 0, 0))
    beside = jnp.zeros_like(centre)
    for unit_step in UNIT_STEPS:
        beside = beside + window_at(padded, unit_step) + window_at(padded, backward(unit_step))
    return (6.0 + damping) * centre - beside


def squares(residual):
    return lax.psum(jnp.sum(residual * residual), ("grp", "dom"))


def plain(
    velocity,
    damping,
    displacement,
    stiffness,
    connectivity,
    inv_mass,
    iface_cell,
    iface_owner,
    iface_node,
    rbf_weight,
    normals,
):
    shell_nodes = displacement.shape[1]
    rim_values = from_behind(displacement[:, :RIM], ("grp", "dom"), -1)
    extended_disp = jnp.concatenate([displacement, rim_values], axis=1)
    element_count = connectivity.shape[1]
    corner_values = extended_disp[:, connectivity]
    element_dofs = jnp.transpose(corner_values, (1, 0, 2)).reshape(12, element_count)
    element_force = jnp.sum(stiffness * element_dofs[None], axis=1).reshape(4, 3, element_count)
    node_force = jnp.zeros((3, shell_nodes + RIM), jnp.float32)
    for corner in range(4):
        node_force = node_force.at[:, connectivity[corner]].add(element_force[corner])
    rim_force = from_behind(node_force[:, shell_nodes:], ("grp", "dom"), 1)
    stiff_force = node_force[:, :shell_nodes] + jnp.pad(rim_force, ((0, 0), (0, shell_nodes - RIM)))
    extended = with_halo(velocity, (("grp", 1), ("dom", 2)), 1)
    predicted = predictor(pad_depth(extended))
    star_wide = with_halo(predicted, (("grp", 1), ("dom", 2)), 1)
    star_padded = pad_depth(star_wide)
    right_side = divergence(star_padded)
    pressure = jnp.zeros_like(right_side)
    residual = right_side
    direction = right_side
    norm_now = squares(residual)
    for sweep in range(ITERS):
        mapped = operate(direction, damping)
        step_size = norm_now / lax.psum(jnp.sum(direction * mapped), ("grp", "dom"))
        pressure = pressure + step_size * direction
        residual = residual - step_size * mapped
        norm_next = squares(residual)
        direction = residual + norm_next / norm_now * direction
        norm_now = norm_next
    pressure_wide = padded_cells(pressure)
    new_velocity = predicted - jnp.stack(
        [
            0.5
            * (window_at(pressure_wide, unit_step) - window_at(pressure_wide, backward(unit_step)))
            for unit_step in UNIT_STEPS
        ]
    )
    pressure_at = pressure.reshape(-1)[iface_cell]
    velocity_at = new_velocity.reshape(3, -1)[:, iface_cell]
    traction = -pressure_at[None] * normals + WALL_FRICTION * velocity_at
    owner_dev = iface_owner[:, 0]
    point_count = owner_dev.shape[0]
    devices = lax.axis_size("grp") * lax.axis_size("dom")
    owner_cap = max(2, 2 * point_count // devices)
    order_index = lax.iota(jnp.int32, point_count)
    earlier = (owner_dev[None, :] == owner_dev[:, None]) & (
        order_index[None, :] < order_index[:, None]
    )
    slot_rank = jnp.sum(earlier.astype(jnp.int32), axis=1)
    slot_index = owner_dev * owner_cap + slot_rank
    slot_count = devices * owner_cap
    payload = jnp.concatenate([traction, rbf_weight, iface_node.astype(jnp.float32)[None]], axis=0)
    outgoing = jnp.zeros((payload.shape[0], slot_count), jnp.float32).at[:, slot_index].set(payload)
    received = lax.all_to_all(outgoing, ("grp", "dom"), split_axis=1, concat_axis=1, tiled=True)
    slot_traction = received[:3]
    slot_weight = received[3 : 3 + RBFW]
    slot_node = received[3 + RBFW].astype(jnp.int32)
    applied = jnp.zeros((3, shell_nodes), jnp.float32)
    for offset in range(RBFW):
        applied = applied.at[:, slot_node + offset].add(slot_weight[offset][None] * slot_traction)
    node_velocity = inv_mass[None] * (applied - stiff_force)
    new_displacement = displacement + SHELL_STEP * node_velocity
    slot_velocity = jnp.zeros((3, slot_count), jnp.float32)
    for offset in range(RBFW):
        slot_velocity = (
            slot_velocity + slot_weight[offset][None] * node_velocity[:, slot_node + offset]
        )
    returned_vals = lax.all_to_all(
        slot_velocity, ("grp", "dom"), split_axis=1, concat_axis=1, tiled=True
    )
    iface_velocity = returned_vals[:, slot_index]
    return (new_velocity, pressure, new_displacement, iface_velocity)


def relay_kernel(*refs):
    count = (len(refs) - 2) // 3
    ins, outs, held = refs[:count], refs[count:2 * count], refs[2 * count:3 * count]
    come, go = refs[-2:]
    pieces = []
    for a, b, c in zip(ins, outs, held):
        if len(a.shape) > 2:
            pieces += [(a.at[k], b.at[k], c.at[k]) for k in range(a.shape[0])]
        else:
            pieces.append((a, b, c))
    arrive = [pltpu.make_async_copy(a, c, come.at[n]) for n, (a, b, c) in enumerate(pieces)]
    leave = [pltpu.make_async_copy(c, b, go.at[n]) for n, (a, b, c) in enumerate(pieces)]
    for cp in arrive:
        cp.start()
    for x, y in zip(arrive, leave):
        x.wait()
        y.start()
    for y in leave:
        y.wait()


def relay(new_velocity, pressure, new_displacement, iface_velocity):
    arrays = (new_velocity, pressure.reshape(4, CX // 4, CY, 2 * HZ), new_displacement, iface_velocity)
    anywhere = pl.BlockSpec(memory_space=pl.ANY)
    count = 3 + 4 + 2
    outs = pl.pallas_call(
        relay_kernel,
        out_shape=tuple(jax.ShapeDtypeStruct(a.shape, a.dtype) for a in arrays),
        in_specs=[anywhere] * len(arrays),
        out_specs=(pl.BlockSpec(memory_space=pltpu.HBM),) * len(arrays),
        scratch_shapes=[pltpu.VMEM(a.shape, a.dtype) for a in arrays]
        + [pltpu.SemaphoreType.DMA((count,)), pltpu.SemaphoreType.DMA((count,))],
        compiler_params=pltpu.CompilerParams(vmem_limit_bytes=60 << 20),
        name="relay",
    )(*arrays)
    return outs[0], outs[1].reshape(pressure.shape), outs[2], outs[3]


def local(*args):
    *outs, sound = fused(*args)
    return lax.cond(sound.reshape(()) > 0, lambda: relay(*outs), lambda: plain(*args))


def solution(mesh):
    return jax.shard_map(
        local,
        mesh=mesh,
        in_specs=(
            P(None, "grp", "dom", None),
            P("grp", "dom", None),
            P(None, ("grp", "dom")),
            P(None, None, ("grp", "dom")),
            P(None, ("grp", "dom")),
            P(("grp", "dom")),
            P(("grp", "dom")),
            P(("grp", "dom"), None),
            P(("grp", "dom")),
            P(None, ("grp", "dom")),
            P(None, ("grp", "dom")),
        ),
        out_specs=(
            P(None, "grp", "dom", None),
            P("grp", "dom", None),
            P(None, ("grp", "dom")),
            P(None, ("grp", "dom")),
        ),
        check_vma=False,
    )
```
